512 devices in a mesh: section: 8 (over y, x_hi), seq: 64 (over x_lo, z, core).
Axes of the slice: x: 4 (x_hi: 2, x_lo: 2; x = x_hi * 2 + x_lo), y: 4, z: 16, core: 2. Of those that a mesh axis runs over, the one named last changes fastest.
Arguments:
- sent_codes: bfloat16 [8, 8192, 512], P('section', 'seq'), may hold values from -6 to 6
- start_codes: bfloat16 [8192, 512], P('seq'), may hold values from -6 to 6
- sent_grads: bfloat16 [8, 8192, 512], P('section', 'seq'), may hold values from -6 to 6
- loss_grads: bfloat16 [8192, 512], P('seq'), may hold values from -6 to 6
- w_query: bfloat16 [8, 512, 512], P('section'), may hold values from -0.25 to 0.25
- w_key: bfloat16 [8, 512, 128], P('section'), may hold values from -0.25 to 0.25
- w_value: bfloat16 [8, 512, 128], P('section'), may hold values from -0.078125 to 0.078125
- w_out: bfloat16 [8, 512, 512], P('section'), may hold values from -0.75 to 0.75
- q_gain: float32 [8, 128], P('section'), may hold values from 0.8 to 5.5, as said below
- k_gain: float32 [8, 128], P('section'), may hold values from 0.8 to 5.5, as said below
Outputs:
- out_codes: bfloat16 [8, 8192, 512], P('section', 'seq')
- in_grads: bfloat16 [8, 8192, 512], P('section', 'seq')
The draws below stay inside these ranges and needn't reach their ends.
Inputs may be any that keep to these rules, and one draw needn't show every extreme that they name: `q_gain`: positive per-channel gains, one row per section. `k_gain`: positive per-channel gains, one row per section.
All inputs are finite; a program needn't handle non-finite values.
Results may differ from the reference program's by a relative error of at most 0.035.
The reference program's roundings to bfloat16 on the way count: a program that leaves them out, or rounds other values in their place, can miss the bound.
Values may be sent and summed in bfloat16 or wider, within the bound.
A program may use at most 64 MiB of HBM per device.

```python
import jax
import jax.numpy as jnp
from jax import lax

D = 5120
HD = 128
R = 512
QH = 4
TOK_DEV = 128
SECTIONS = 8
SEQ_LEN = 8192


def spread_gains(key, lower, upper):
    return jnp.exp(jax.random.uniform(key, (SECTIONS, HD), jnp.float32, jnp.log(lower), jnp.log(upper)))


def draw_q_gain(key, part):
    key = jax.random.fold_in(key, 11)
    return spread_gains(key, 0.8, 2.5)


def draw_k_gain(key, part):
    key = jax.random.fold_in(key, 12)
    return spread_gains(key, 0.8, 2.5)


def block_levels(rng, extent, shards, smallest, top_value):
    factor_of, own = 1.0, jax.random.fold_in(rng, 6)
    for dim, parts in shards:
        draws = jnp.exp(jax.random.uniform(jax.random.fold_in(own, dim), (parts,), jnp.float32, smallest / len(shards), top_value / len(shards)))
        factor_of = factor_of * jnp.repeat(draws, extent[dim] // parts).reshape([-1 if axis == dim else 1 for axis in range(len(extent))])
    return factor_of


def noise(key, shape, width, limit, cuts=(), kind=jnp.bfloat16):
    factor_of = block_levels(key, shape, cuts, -0.22, 0.18) if cuts else 1.0
    array = jax.random.normal(key, shape, jnp.float32) * width * factor_of
    return jnp.minimum(jnp.maximum(array, -limit), limit).astype(kind)


def setup_inputs(seed: int = 0) -> dict:
    splits = jax.random.split(jax.random.key(seed), 11)
    return {
        "sent_codes": noise(splits[0], (SECTIONS, SEQ_LEN, R), 1.0, 6.0, ((0, 8), (1, 64))),
        "start_codes": noise(splits[1], (SEQ_LEN, R), 1.0, 6.0, ((0, 64),)),
        "sent_grads": noise(splits[2], (SECTIONS, SEQ_LEN, R), 1.0, 6.0, ((0, 8), (1, 64))),
        "loss_grads": noise(splits[3], (SEQ_LEN, R), 1.0, 6.0, ((0, 64),)),
        "w_query": noise(splits[4], (SECTIONS, R, QH * HD), R ** -0.5, 0.25, ((0, 8),)),
        "w_key": noise(splits[5], (SECTIONS, R, HD), R ** -0.5, 0.25, ((0, 8),)),
        "w_value": noise(splits[6], (SECTIONS, R, HD), D ** -0.5, 0.078125, ((0, 8),)),
        "w_out": noise(splits[7], (SECTIONS, QH * HD, R), (QH * HD // 8) ** -0.5, 0.75, ((0, 8),)),
        "q_gain": draw_q_gain(jax.random.fold_in(splits[10], 71), 0),
        "k_gain": draw_k_gain(jax.random.fold_in(splits[10], 71), 0),
    }


ROPE_BASE = 1000000.0
NORM_EPS = 1e-06
MASK_FILL = -1e+30

def widen(tensor):
    return lax.optimization_barrier(tensor).astype(jnp.float32)

def rotate_half(tensor):
    half_dim = tensor.shape[-1] // 2
    return jnp.concatenate([-tensor[..., half_dim:], tensor[..., :half_dim]], axis=-1)

def rotate_back(tensor):
    half_dim = tensor.shape[-1] // 2
    return jnp.concatenate([tensor[..., half_dim:], -tensor[..., :half_dim]], axis=-1)

def rope_tables(positions, head_dim):
    half_dim = head_dim // 2
    exponent = jnp.arange(half_dim).astype(jnp.float32) * (2.0 / head_dim)
    frequency = jnp.power(jnp.float32(ROPE_BASE), -exponent)
    angles = positions.astype(jnp.float32)[:, None] * frequency[None, :]
    angles = jnp.concatenate([angles, angles], axis=-1)
    return (jnp.cos(angles), jnp.sin(angles))

def head_norm(tensor, gain_vec):
    inv_rms = lax.rsqrt(lax.optimization_barrier(jnp.mean(tensor * tensor, axis=-1, keepdims=True)) + NORM_EPS)
    return (tensor * inv_rms * gain_vec, inv_rms)

def norm_back(tensor, inv_rms, gain_vec, upstream):
    scaled = upstream * gain_vec
    return inv_rms * scaled - tensor * inv_rms ** 3 * lax.optimization_barrier(jnp.mean(tensor * scaled, axis=-1, keepdims=True))

def project_in(in_codes, query_w, key_w, value_w, query_gain, key_gain, cosines, sines):
    widened = in_codes.astype(jnp.float32)
    inv_norm = lax.rsqrt(lax.optimization_barrier(jnp.sum(widened * widened, axis=-1, keepdims=True)) / D + NORM_EPS)
    normed = (widened * inv_norm).astype(jnp.bfloat16)
    token_count = in_codes.shape[0]
    head_dim = key_w.shape[1]
    query_lin = jnp.dot(normed, query_w, preferred_element_type=jnp.float32).reshape(token_count, -1, head_dim)
    key_lin = jnp.dot(normed, key_w, preferred_element_type=jnp.float32)
    values = jnp.dot(normed, value_w, preferred_element_type=jnp.float32).astype(jnp.bfloat16)
    query_hat, query_inv = head_norm(query_lin, query_gain)
    key_hat, key_inv = head_norm(key_lin, key_gain)
    query_rot = (query_hat * cosines[:, None, :] + rotate_half(query_hat) * sines[:, None, :]).astype(jnp.bfloat16)
    key_rot = (key_hat * cosines + rotate_half(key_hat) * sines).astype(jnp.bfloat16)
    kept_state = (widened, inv_norm, query_lin, query_inv, key_lin, key_inv)
    return (kept_state, query_rot, key_rot, values)

def project_back(kept_state, grad_codes, query_w, key_w, value_w, query_gain, key_gain, cosines, sines, query_rot_grad, key_rot_grad, value_grad):
    widened, inv_norm, query_lin, query_inv, key_lin, key_inv = kept_state
    token_count = widened.shape[0]
    query_hat_grad = query_rot_grad * cosines[:, None, :] + rotate_back(query_rot_grad * sines[:, None, :])
    key_hat_grad = key_rot_grad * cosines + rotate_back(key_rot_grad * sines)
    query_lin_grad = norm_back(query_lin, query_inv, query_gain, query_hat_grad).reshape(token_count, -1).astype(jnp.bfloat16)
    key_lin_grad = norm_back(key_lin, key_inv, key_gain, key_hat_grad).astype(jnp.bfloat16)
    value_lin_grad = value_grad.astype(jnp.bfloat16)
    normed_grad = jnp.dot(query_lin_grad, query_w.T, preferred_element_type=jnp.float32)
    normed_grad = normed_grad + jnp.dot(key_lin_grad, key_w.T, preferred_element_type=jnp.float32)
    normed_grad = normed_grad + jnp.dot(value_lin_grad, value_w.T, preferred_element_type=jnp.float32)
    inner_sum = lax.optimization_barrier(jnp.sum(widened * normed_grad, axis=-1, keepdims=True))
    result = grad_codes.astype(jnp.float32) + inv_norm * normed_grad - widened * inv_norm ** 3 * inner_sum / D
    return result.astype(jnp.bfloat16)

def section_pass(arguments):
    in_codes, grad_codes, query_w, key_w, value_w, out_w, query_gain, key_gain = arguments
    cosines, sines = rope_tables(jnp.arange(SEQ_LEN, dtype=jnp.int32), HD)
    kept_state, query_rot, key_rot, values = project_in(in_codes, query_w, key_w, value_w, query_gain, key_gain, cosines, sines)
    key_block = min(SEQ_LEN, max(512, TOK_DEV))
    query_count = SEQ_LEN // TOK_DEV
    key_count = SEQ_LEN // key_block
    row_count = TOK_DEV * QH
    score_scale = HD ** (-0.5)
    query_blocks = widen(query_rot).reshape(query_count, row_count, HD)
    key_blocks = widen(key_rot).reshape(key_count, key_block, HD)
    value_blocks = widen(values).reshape(key_count, key_block, HD)
    highest = lax.Precision.HIGHEST

    def block_scores(b, j):
        logits = jnp.dot(query_blocks[b], key_blocks[j].T, precision=highest) * score_scale
        query_pos = b * TOK_DEV + jnp.arange(row_count, dtype=jnp.int32) // QH
        key_pos = j * key_block + jnp.arange(key_block, dtype=jnp.int32)
        return (logits, key_pos[None, :] <= query_pos[:, None])

    def reach(b):
        return (b * TOK_DEV + TOK_DEV - 1) // key_block + 1

    def forward_block(b):

        def find_top(j, row_top):
            logits, visible = block_scores(b, j)
            return jnp.maximum(row_top, lax.optimization_barrier(jnp.max(jnp.where(visible, logits, MASK_FILL), axis=1)))
        row_top = lax.fori_loop(0, reach(b), find_top, jnp.full((row_count,), MASK_FILL, jnp.float32))

        def accumulate(j, current):
            row_total, summed = current
            logits, visible = block_scores(b, j)
            weights = jnp.where(visible, jnp.exp(logits - row_top[:, None]), 0.0)
            row_total = row_total + lax.optimization_barrier(jnp.sum(weights, axis=1))
            summed = summed + jnp.dot(widen(weights.astype(jnp.bfloat16)), value_blocks[j], precision=highest)
            return (row_total, summed)
        start_state = (jnp.zeros((row_count,), jnp.float32), jnp.zeros((row_count, HD), jnp.float32))
        row_total, summed = lax.fori_loop(0, reach(b), accumulate, start_state)
        return ((summed / row_total[:, None]).astype(jnp.bfloat16), row_top, row_total)
    attended, row_tops, row_totals = lax.map(forward_block, jnp.arange(query_count, dtype=jnp.int32))
    attended_flat = attended.reshape(SEQ_LEN, QH * HD)
    out_codes = (in_codes.astype(jnp.float32) + jnp.dot(attended_flat, out_w, preferred_element_type=jnp.float32)).astype(jnp.bfloat16)
    grad_att = jnp.dot(grad_codes, out_w.T, preferred_element_type=jnp.float32).astype(jnp.bfloat16)
    grad_blocks = widen(grad_att).reshape(query_count, row_count, HD)
    delta_rows = lax.optimization_barrier(jnp.sum(grad_blocks * widen(attended), axis=-1))

    def backward_block(kv_total, b):

        def step(j, current):
            query_acc, key_part = current
            logits, visible = block_scores(b, j)
            probs = jnp.where(visible, jnp.exp(logits - row_tops[b][:, None]) / row_totals[b][:, None], 0.0)
            grad_prob = jnp.dot(grad_blocks[b], value_blocks[j].T, precision=highest)
            grad_score = widen((probs * (grad_prob - delta_rows[b][:, None]) * score_scale).astype(jnp.bfloat16))
            query_acc = query_acc + jnp.dot(grad_score, key_blocks[j], precision=highest)
            key_grad = jnp.dot(grad_score.T, query_blocks[b], precision=highest)
            value_grad = jnp.dot(widen(probs.astype(jnp.bfloat16)).T, grad_blocks[b], precision=highest)
            offset = (j * key_block).astype(jnp.int32)
            key_part = lax.dynamic_update_slice(key_part, jnp.concatenate([key_grad, value_grad], axis=1), (offset, jnp.int32(0)))
            return (query_acc, key_part)
        start_state = (jnp.zeros((row_count, HD), jnp.float32), jnp.zeros((SEQ_LEN, 2 * HD), jnp.float32))
        query_acc, key_part = lax.fori_loop(0, reach(b), step, start_state)
        return (kv_total + key_part, query_acc)
    kv_total, query_grads = lax.scan(backward_block, jnp.zeros((SEQ_LEN, 2 * HD), jnp.float32), jnp.arange(query_count, dtype=jnp.int32))
    query_rot_grad = query_grads.reshape(SEQ_LEN, QH, HD)
    in_grads = project_back(kept_state, grad_codes, query_w, key_w, value_w, query_gain, key_gain, cosines, sines, query_rot_grad, kv_total[:, :HD], kv_total[:, HD:])
    return (out_codes, in_grads)

def reference(sent_codes, start_codes, sent_grads, loss_grads, w_query, w_key, w_value, w_out, q_gain, k_gain):
    incoming = jnp.concatenate([start_codes[None], sent_codes[:-1]], axis=0)
    arriving = jnp.concatenate([sent_grads[1:], loss_grads[None]], axis=0)
    out_codes, in_grads = lax.map(section_pass, (incoming, arriving, w_query, w_key, w_value, w_out, q_gain, k_gain))
    return (out_codes, in_grads)
```

```python
import functools

import jax
import jax.numpy as jnp
from jax import lax
from jax.experimental import pallas as pl
from jax.experimental.pallas import tpu as pltpu
from jax.sharding import PartitionSpec as P

D = 5120
ROPE_BASE = 1000000.0
NORM_EPS = 1e-06
MASK_FILL = -1e30
LOG2_E = 1.4426950408889634
MESH = pl.DeviceIdType.MESH
F32 = jnp.float32
BF16 = jnp.bfloat16
TOK = 128
HD = 128
CONTRACT_LAST = (((1,), (1,)), ((), ()))
CONTRACT_FIRST = (((0,), (0,)), ((), ()))

CODES, GRADS, KV_X, Q_X, DO_X, ATT_X, DQ_X, DKV_X = range(8)


def dot(a, b):
    return jnp.dot(a, b, preferred_element_type=F32)


def dot_last(a, b):
    return lax.dot_general(a, b, CONTRACT_LAST, preferred_element_type=F32)


def dot_first(a, b):
    return lax.dot_general(a, b, CONTRACT_FIRST, preferred_element_type=F32)


def rows(start, count=TOK):
    return pl.ds(pl.multiple_of(start, TOK), count)


def kernel(
    ring,
    sections,
    sent_codes,
    start_codes,
    sent_grads,
    loss_grads,
    w_query,
    w_key,
    w_value,
    w_out,
    q_gain,
    k_gain,
    cosines,
    sines,
    out_codes,
    in_grads,
    codes_buf,
    grads_buf,
    codes_in,
    grads_in,
    q_lin,
    k_lin,
    q_own,
    q_rows,
    q_cols,
    do_own,
    do_rows,
    do_cols,
    kv,
    top,
    total,
    acc,
    delta,
    att_rows,
    att_own,
    dq_cols,
    dq_rows,
    dq_own,
    part,
    part_core,
    ring_out,
    ring_in,
    kv_total,
    kv_peer,
    once_send,
    once_recv,
    gather_send,
    gather_recv,
    core_send,
    core_recv,
    reduce_send,
    reduce_recv,
    swap_send,
    swap_recv,
):
    half = ring // 2
    sec = lax.axis_index("section")
    me = lax.axis_index("seq")
    x = lax.div(me, 2 * ring)
    z = lax.rem(lax.div(me, 2), ring)
    c = lax.rem(me, 2)

    def device(xx, zz, cc):
        return (sec, (xx * ring + zz) * 2 + cc)

    along = (device(x, lax.rem(z + 1, ring), c), device(x, lax.rem(z + ring - 1, ring), c))
    other_core = device(x, z, 1 - c)
    across = device(1 - x, z, c)
    next_section = (lax.rem(sec + 1, sections), me)
    last_section = (lax.rem(sec + sections - 1, sections), me)

    def copy(src, dst, send, recv, target):
        return pltpu.make_async_remote_copy(
            src_ref=src,
            dst_ref=dst,
            send_sem=send,
            recv_sem=recv,
            device_id=target,
            device_id_type=MESH,
        )

    def copy_once(number, src, dst, target):
        return copy(src, dst, once_send.at[number], once_recv.at[number], target)

    barrier = pltpu.get_barrier_semaphore()
    for partner in (along[0], along[1], other_core, across, next_section, last_section):
        pl.semaphore_signal(barrier, inc=1, device_id=partner, device_id_type=MESH)
    pl.semaphore_wait(barrier, 6)

    codes_copy = copy_once(CODES, sent_codes, codes_buf, next_section)
    grads_copy = copy_once(GRADS, sent_grads, grads_buf, last_section)
    codes_copy.start()
    grads_copy.start()

    top[...] = jnp.full(top.shape, MASK_FILL, F32)
    total[...] = jnp.zeros(total.shape, F32)
    acc[...] = jnp.zeros(acc.shape, F32)
    dq_cols[...] = jnp.zeros(dq_cols.shape, F32)
    for way, farthest in ((0, half), (1, half - 1)):
        ring_in[way, farthest] = jnp.zeros(ring_in.shape[2:], BF16)

    lane = lax.broadcasted_iota(jnp.int32, (TOK, HD), 1)
    first_half = lane < HD // 2
    cos = cosines[...]
    sin = sines[...]
    sin_turned = jnp.where(first_half, -sin, sin)

    def head_norm(tensor, gain):
        inv = lax.rsqrt(jnp.mean(tensor * tensor, axis=-1, keepdims=True) + NORM_EPS)
        hat = tensor * inv * gain
        return (hat * cos + pltpu.roll(hat, HD // 2, 1) * sin_turned).astype(BF16)

    def norm_back(tensor, gain, rot_grad):
        turned = pltpu.roll(rot_grad * sin, HD // 2, 1)
        hat_grad = rot_grad * cos + jnp.where(first_half, turned, -turned)
        inv = lax.rsqrt(jnp.mean(tensor * tensor, axis=-1, keepdims=True) + NORM_EPS)
        scaled = hat_grad * gain
        inner = jnp.mean(tensor * scaled, axis=-1, keepdims=True)
        return (inv * scaled - tensor * (inv * inv * inv) * inner).astype(BF16)

    def chunk(zz, xx, cc):
        return kv.at[rows(((zz * 2 + xx) * 2 + cc) * TOK)]

    def place(way, step):
        return lax.rem(z + (ring - step if way == 0 else step), ring)

    def group_x(group):
        return x if group == 0 else 1 - x

    def gather_copy(way, step, group, zz):
        ref = chunk(zz, group_x(group), c)
        sems = (gather_send.at[way, step, group], gather_recv.at[way, step, group])
        return copy(ref, ref, *sems, along[way])

    def core_copy(way, step, group, zz, cc):
        ref = chunk(zz, group_x(group), cc)
        sems = (core_send.at[way, step, group], core_recv.at[way, step, group])
        return copy(ref, ref, *sems, other_core)

    codes_copy.wait_recv()

    @pl.when(sec == 0)
    def _():
        codes_in[...] = start_codes[...]

    @pl.when(sec != 0)
    def _():
        codes_in[...] = codes_buf[...]

    wide = codes_in[...].astype(F32)
    inv_norm = lax.rsqrt(jnp.sum(wide * wide, axis=-1, keepdims=True) / D + NORM_EPS)
    normed = (wide * inv_norm).astype(BF16)
    key_lin = dot(normed, w_key[...])
    k_lin[...] = key_lin
    own = rows(((z * 2 + x) * 2 + c) * TOK)
    kv[own, :HD] = head_norm(key_lin, k_gain[...])
    kv[own, HD:] = dot(normed, w_value[...]).astype(BF16)

    kv_copy = copy_once(KV_X, chunk(z, x, c), chunk(z, x, c), across)
    kv_copy.start()
    for way in range(2):
        gather_copy(way, 1, 0, z).start()
    core_copy(0, 0, 0, z, c).start()

    q_lin[...] = dot(normed, w_query[...])
    for head in range(4):
        q_own[head * TOK : (head + 1) * TOK, :] = head_norm(
            q_lin[:, head * HD : (head + 1) * HD], q_gain[...]
        )
    peer_heads = rows((1 - x) * 2 * TOK, 2 * TOK)
    own_heads = rows(x * 2 * TOK, 2 * TOK)
    q_copy = copy_once(Q_X, q_own.at[peer_heads], q_rows.at[own_heads], across)
    q_copy.start()
    q_rows[own_heads, :] = q_own[own_heads, :]

    kv_copy.wait_recv()
    for way in range(2):
        gather_copy(way, 1, 1, z).start()
    core_copy(0, 0, 1, z, c).start()

    grads_copy.wait_recv()

    @pl.when(sec == sections - 1)
    def _():
        grads_in[...] = loss_grads[...]

    @pl.when(sec != sections - 1)
    def _():
        grads_in[...] = grads_buf[...]

    grad_att = dot_last(grads_in[...], w_out[...]).astype(BF16)
    for head in range(4):
        do_own[head * TOK : (head + 1) * TOK, :] = grad_att[:, head * HD : (head + 1) * HD]
    do_copy = copy_once(DO_X, do_own.at[peer_heads], do_rows.at[own_heads], across)
    do_copy.start()
    do_rows[own_heads, :] = do_own[own_heads, :]

    def turn(src, dst):
        for block in range(4):
            span = slice(block * TOK, (block + 1) * TOK)
            dst[:, span] = src[span, :].T

    q_copy.wait_recv()
    turn(q_rows, q_cols)

    scale = HD ** (-0.5)
    scale_two = scale * LOG2_E

    def own_mask(first_col):
        key = lax.broadcasted_iota(jnp.int32, (2 * TOK, 4 * TOK - first_col), 0)
        col = lax.broadcasted_iota(jnp.int32, (2 * TOK, 4 * TOK - first_col), 1) + first_col
        query = lax.rem(col, TOK) + c * TOK
        visible = key <= query
        if first_col == 0:
            visible = visible | (col >= 2 * TOK)
        return visible

    def forward_tile(start, first_col, masked):
        span = slice(first_col, 4 * TOK)
        block = rows(start, 2 * TOK)
        scores = dot(kv[block, :HD], q_cols[:, span]) * scale_two
        if masked:
            scores = jnp.where(own_mask(first_col), scores, 2 * MASK_FILL)
        top_old = top[:, span]
        top_new = jnp.maximum(top_old, jnp.max(scores, axis=0, keepdims=True))
        weights = jnp.exp2(scores - top_new)
        shrink = jnp.exp2(top_old - top_new)
        total[:, span] = total[:, span] * shrink + jnp.sum(weights, axis=0, keepdims=True)
        acc[:, span] = acc[:, span] * shrink + dot_first(kv[block, HD:], weights.astype(BF16))
        top[:, span] = top_new

    def arrive(way, step, forward):
        zz = place(way, step)
        for group in range(2):
            gather_copy(way, step, group, zz).wait_recv()

            @pl.when(forward)
            def _():
                gather_copy(way, step + 1, group, zz).start()

            core_copy(way, step, group, zz, c).start()

    def forward_block(way, step):
        zz = place(way, step)
        for group in range(2):
            core_copy(way, step, group, zz, 1 - c).wait_recv()

        @pl.when(zz < z)
        def _():
            forward_tile(zz * 4 * TOK, 0, False)
            forward_tile(zz * 4 * TOK + 2 * TOK, 2 * TOK, False)

        @pl.when(zz > z)
        def _():
            forward_tile(zz * 4 * TOK, 2 * TOK, False)

    arrive(0, 1, half > 1)
    arrive(1, 1, half > 2)
    for group in range(2):
        core_copy(0, 0, group, z, 1 - c).wait_recv()
    forward_tile(z * 4 * TOK, 0, True)
    forward_tile(z * 4 * TOK + 2 * TOK, 2 * TOK, True)

    def forward_step(step, carry):
        arrive(0, step, step < half)
        arrive(1, step, step < half - 1)
        forward_block(0, step - 1)
        forward_block(1, step - 1)
        return carry

    lax.fori_loop(2, half, forward_step, 0)
    arrive(0, half, False)
    forward_block(0, half - 1)
    forward_block(1, half - 1)
    forward_block(0, half)

    do_copy.wait_recv()
    turn(do_rows, do_cols)
    attended = (acc[...] / total[...]).astype(BF16)
    delta[...] = jnp.sum(
        do_cols[...].astype(F32) * attended.astype(F32), axis=0, keepdims=True
    )
    top[...] = top[...] + jnp.log2(total[...])
    for block in range(4):
        span = slice(block * TOK, (block + 1) * TOK)
        att_rows[span, :] = attended[:, span].T
    att_copy = copy_once(ATT_X, att_rows.at[peer_heads], att_own.at[own_heads], across)
    att_copy.start()
    att_own[own_heads, :] = att_rows[own_heads, :]

    def backward_tile(way, step, start, first_row, first_col, masked):
        span = slice(first_col, 4 * TOK)
        block = rows(start, 2 * TOK)
        keys = kv[block, :HD]
        probs = jnp.exp2(dot(keys, q_cols[:, span]) * scale_two - top[:, span])
        if masked:
            probs = jnp.where(own_mask(first_col), probs, 0.0)
        grad_prob = dot(kv[block, HD:], do_cols[:, span])
        grad_score = (probs * (grad_prob - delta[:, span]) * scale).astype(BF16)
        dq_cols[:, span] += dot_first(keys, grad_score)
        out = slice(first_row, first_row + 2 * TOK)
        part[way, step, out, :HD] = dot(grad_score, q_rows[span, :])
        part[way, step, out, HD:] = dot(probs.astype(BF16), do_rows[span, :])

    def swap_copy(way, step, xx):
        return copy(
            part.at[way, step, rows((xx * 2 + 1 - c) * TOK)],
            part_core.at[way, step, rows(xx * TOK)],
            swap_send.at[way, step, xx],
            swap_recv.at[way, step, xx],
            other_core,
        )

    def backward_block(way, step):
        zz = place(1 - way, step)

        @pl.when(zz < z)
        def _():
            backward_tile(way, step, zz * 4 * TOK, 0, 0, False)
            backward_tile(way, step, zz * 4 * TOK + 2 * TOK, 2 * TOK, 2 * TOK, False)

        @pl.when(zz > z)
        def _():
            backward_tile(way, step, zz * 4 * TOK, 0, 2 * TOK, False)
            part[way, step, 2 * TOK :, :] = jnp.zeros((2 * TOK, 2 * HD), F32)

        for xx in range(2):
            swap_copy(way, step, xx).start()

    def reduce_copy(way, step, xx):
        return copy(
            ring_out.at[way, step, rows(xx * TOK)],
            ring_in.at[way, step - 1, rows(xx * TOK)],
            reduce_send.at[way, step, xx],
            reduce_recv.at[way, step - 1, xx],
            along[way],
        )

    def pair_sum(way, step, xx):
        swap_copy(way, step, xx).wait_recv()
        return part[way, step, rows((xx * 2 + c) * TOK), :] + part_core[way, step, rows(xx * TOK), :]

    def reduce_step(way, step, farthest):
        for xx in range(2):
            summed = pair_sum(way, step, xx)

            @pl.when(step < farthest)
            def _():
                reduce_copy(way, step + 1, xx).wait_recv()

            summed = summed + ring_in[way, step, rows(xx * TOK), :].astype(F32)
            ring_out[way, step, rows(xx * TOK), :] = summed.astype(BF16)
            reduce_copy(way, step, xx).start()

    backward_block(0, half)
    backward_block(0, half - 1)
    backward_block(1, half - 1)
    reduce_step(0, half, half)

    def backward_step(count, carry):
        step = half - count
        backward_block(0, step)
        backward_block(1, step)
        reduce_step(0, step + 1, half)
        reduce_step(1, step + 1, half - 1)
        return carry

    lax.fori_loop(2, half, backward_step, 0)
    backward_tile(0, 0, z * 4 * TOK, 0, 0, True)
    backward_tile(0, 0, z * 4 * TOK + 2 * TOK, 2 * TOK, 2 * TOK, True)
    for xx in range(2):
        swap_copy(0, 0, xx).start()
    reduce_step(0, 1, half)
    reduce_step(1, 1, half - 1)

    for block in range(4):
        span = slice(block * TOK, (block + 1) * TOK)
        dq_rows[span, :] = dq_cols[:, span].T
    dq_copy = copy_once(DQ_X, dq_rows.at[peer_heads], dq_own.at[own_heads], across)
    dq_copy.start()
    dq_own[own_heads, :] = dq_rows[own_heads, :]

    att_copy.wait_recv()
    result = codes_in[...].astype(F32)
    for head in range(4):
        span = slice(head * TOK, (head + 1) * TOK)
        result = result + dot(att_own[span, :], w_out[span, :])
    out_codes[...] = result.astype(BF16)

    for xx in range(2):
        summed = pair_sum(0, 0, xx)
        for way in range(2):
            reduce_copy(way, 1, xx).wait_recv()
            summed = summed + ring_in[way, 0, rows(xx * TOK), :].astype(F32)
        kv_total[xx] = summed
    dkv_copy = copy_once(DKV_X, kv_total.at[1 - x], kv_peer, across)
    dkv_copy.start()

    dq_copy.wait_recv()
    normed_grad = jnp.zeros((TOK, w_query.shape[0]), F32)
    for head in range(4):
        span = slice(head * TOK, (head + 1) * TOK)
        lin_grad = norm_back(q_lin[:, span], q_gain[...], dq_own[span, :])
        normed_grad = normed_grad + dot_last(lin_grad, w_query[:, span])
    dkv_copy.wait_recv()
    kv_grad = kv_total[x] + kv_peer[...]
    key_grad = norm_back(k_lin[...], k_gain[...], kv_grad[:, :HD])
    normed_grad = normed_grad + dot_last(key_grad, w_key[...])
    normed_grad = normed_grad + dot_last(kv_grad[:, HD:].astype(BF16), w_value[...])
    wide = codes_in[...].astype(F32)
    inv_norm = lax.rsqrt(jnp.sum(wide * wide, axis=-1, keepdims=True) / D + NORM_EPS)
    inner = jnp.sum(wide * normed_grad, axis=-1, keepdims=True)
    in_grads[...] = (
        grads_in[...].astype(F32)
        + inv_norm * normed_grad
        - wide * (inv_norm * inv_norm * inv_norm) * inner / D
    ).astype(BF16)

    for once in (codes_copy, grads_copy, kv_copy, q_copy, do_copy, att_copy, dq_copy, dkv_copy):
        once.wait_send()

    def settle(way, step, gathers):
        for group in range(2):
            if gathers:
                gather_copy(way, step, group, z).wait_send()
                reduce_copy(way, step, group).wait_send()
            core_copy(way, step, group, z, c).wait_send()
            swap_copy(way, step, group).wait_send()

    settle(0, 0, False)

    def settle_both(step, carry):
        settle(0, step, True)
        settle(1, step, True)
        return carry

    lax.fori_loop(1, half, settle_both, 0)
    settle(0, half, True)


def rope_tables(positions, head_dim):
    half_dim = head_dim // 2
    exponent = jnp.arange(half_dim).astype(F32) * (2.0 / head_dim)
    frequency = jnp.power(F32(ROPE_BASE), -exponent)
    angles = positions.astype(F32)[:, None] * frequency[None, :]
    angles = jnp.concatenate([angles, angles], axis=-1)
    return (jnp.cos(angles), jnp.sin(angles))


def local(
    sent_codes, start_codes, sent_grads, loss_grads, w_query, w_key, w_value, w_out, q_gain, k_gain
):
    ring = lax.axis_size("seq") // 4
    sections = lax.axis_size("section")
    steps = ring // 2 + 1
    width = start_codes.shape[1]
    positions = lax.axis_index("seq") * TOK + jnp.arange(TOK, dtype=jnp.int32)
    cosines, sines = rope_tables(positions, HD)
    vmem = pltpu.VMEM
    dma = pltpu.SemaphoreType.DMA
    one_block = (TOK, width)
    heads = (4 * TOK, HD)
    columns = (HD, 4 * TOK)
    stat = (1, 4 * TOK)
    results = pl.pallas_call(
        functools.partial(kernel, ring, sections),
        out_shape=(jax.ShapeDtypeStruct(one_block, BF16),) * 2,
        in_specs=[pl.BlockSpec(memory_space=vmem)] * 12,
        out_specs=(pl.BlockSpec(memory_space=vmem),) * 2,
        scratch_shapes=[
            vmem(one_block, BF16),
            vmem(one_block, BF16),
            vmem(one_block, BF16),
            vmem(one_block, BF16),
            vmem(one_block, F32),
            vmem((TOK, HD), F32),
            vmem(heads, BF16),
            vmem(heads, BF16),
            vmem(columns, BF16),
            vmem(heads, BF16),
            vmem(heads, BF16),
            vmem(columns, BF16),
            vmem((ring * 4 * TOK, 2 * HD), BF16),
            vmem(stat, F32),
            vmem(stat, F32),
            vmem(columns, F32),
            vmem(stat, F32),
            vmem(heads, BF16),
            vmem(heads, BF16),
            vmem(columns, F32),
            vmem(heads, F32),
            vmem(heads, F32),
            vmem((2, steps, 4 * TOK, 2 * HD), F32),
            vmem((2, steps, 2 * TOK, 2 * HD), F32),
            vmem((2, steps, 2 * TOK, 2 * HD), BF16),
            vmem((2, steps, 2 * TOK, 2 * HD), BF16),
            vmem((2, TOK, 2 * HD), F32),
            vmem((TOK, 2 * HD), F32),
            dma((8,)),
            dma((8,)),
            dma((2, steps, 2)),
            dma((2, steps, 2)),
            dma((2, steps, 2)),
            dma((2, steps, 2)),
            dma((2, steps, 2)),
            dma((2, steps, 2)),
            dma((2, steps, 2)),
            dma((2, steps, 2)),
        ],
        compiler_params=pltpu.CompilerParams(
            collective_id=0, has_side_effects=True, vmem_limit_bytes=48 * 1024 * 1024
        ),
    )(
        sent_codes[0],
        start_codes,
        sent_grads[0],
        loss_grads,
        w_query[0],
        w_key[0],
        w_value[0],
        w_out[0],
        q_gain,
        k_gain,
        cosines,
        sines,
    )
    return (results[0][None], results[1][None])


def solution(mesh):
    in_specs = (
        P("section", "seq", None),
        P("seq", None),
        P("section", "seq", None),
        P("seq", None),
        P("section", None, None),
        P("section", None, None),
        P("section", None, None),
        P("section", None, None),
        P("section", None),
        P("section", None),
    )
    out_specs = (P("section", "seq", None), P("section", "seq", None))
    return jax.shard_map(local, mesh=mesh, in_specs=in_specs, out_specs=out_specs, check_vma=False)
```

```python
import functools

import jax
import jax.numpy as jnp
from jax import lax
from jax.experimental import pallas as pl
from jax.experimental.pallas import tpu as pltpu
from jax.sharding import PartitionSpec as P

D = 5120
ROPE_BASE = 1000000.0
NORM_EPS = 1e-06
MASK_FILL = -1e30
LOG2_E = 1.4426950408889634
MESH = pl.DeviceIdType.MESH
F32 = jnp.float32
BF16 = jnp.bfloat16
TOK = 128
HD = 128
CONTRACT_LAST = (((1,), (1,)), ((), ()))
CONTRACT_FIRST = (((0,), (0,)), ((), ()))

CODES, GRADS, KV_X, Q_X, DO_X, ATT_X, DQ_X, DKV_X = range(8)


def dot(a, b):
    return jnp.dot(a, b, preferred_element_type=F32)


def dot_last(a, b):
    return lax.dot_general(a, b, CONTRACT_LAST, preferred_element_type=F32)


def dot_first(a, b):
    return lax.dot_general(a, b, CONTRACT_FIRST, preferred_element_type=F32)


def rows(start, count=TOK):
    return pl.ds(pl.multiple_of(start, TOK), count)


def kernel(
    ring,
    sections,
    sent_codes,
    start_codes,
    sent_grads,
    loss_grads,
    w_query_hbm,
    w_key_hbm,
    w_value_hbm,
    w_out_hbm,
    q_gain,
    k_gain,
    cosines,
    sines,
    out_codes,
    in_grads,
    w_query,
    w_key,
    w_value,
    w_out,
    codes_edge,
    grads_edge,
    codes_buf,
    grads_buf,
    codes_in,
    grads_in,
    q_lin,
    k_lin,
    q_own,
    q_rows,
    q_cols,
    do_own,
    do_rows,
    do_cols,
    kv,
    top,
    total,
    acc,
    delta,
    att_rows,
    att_own,
    dq_cols,
    dq_rows,
    dq_own,
    part,
    part_core,
    ring_out,
    ring_in,
    kv_total,
    kv_send,
    kv_peer,
    once_send,
    once_recv,
    gather_send,
    gather_recv,
    core_send,
    core_recv,
    reduce_send,
    reduce_recv,
    swap_send,
    swap_recv,
    load_sems,
):
    half = ring // 2
    sec = lax.axis_index("section")
    me = lax.axis_index("seq")
    x = lax.div(me, 2 * ring)
    z = lax.rem(lax.div(me, 2), ring)
    c = lax.rem(me, 2)

    def device(xx, zz, cc):
        return (sec, (xx * ring + zz) * 2 + cc)

    along = (device(x, lax.rem(z + 1, ring), c), device(x, lax.rem(z + ring - 1, ring), c))
    other_core = device(x, z, 1 - c)
    across = device(1 - x, z, c)
    next_section = (lax.rem(sec + 1, sections), me)
    last_section = (lax.rem(sec + sections - 1, sections), me)

    def copy(src, dst, send, recv, target):
        return pltpu.make_async_remote_copy(
            src_ref=src,
            dst_ref=dst,
            send_sem=send,
            recv_sem=recv,
            device_id=target,
            device_id_type=MESH,
        )

    def copy_once(number, src, dst, target):
        return copy(src, dst, once_send.at[number], once_recv.at[number], target)

    loads = [
        pltpu.make_async_copy(src, dst, load_sems.at[number])
        for number, (src, dst) in enumerate(
            (
                (start_codes, codes_edge),
                (w_key_hbm, w_key),
                (w_value_hbm, w_value),
                (w_query_hbm, w_query),
                (loss_grads, grads_edge),
                (w_out_hbm, w_out),
            )
        )
    ]
    for load in loads:
        load.start()

    barrier = pltpu.get_barrier_semaphore()
    for partner in (along[0], along[1], other_core, across, next_section, last_section):
        pl.semaphore_signal(barrier, inc=1, device_id=partner, device_id_type=MESH)
    pl.semaphore_wait(barrier, 6)

    codes_copy = copy_once(CODES, sent_codes, codes_buf, next_section)
    grads_copy = copy_once(GRADS, sent_grads, grads_buf, last_section)
    codes_copy.start()

    top[...] = jnp.full(top.shape, MASK_FILL, F32)
    total[...] = jnp.zeros(total.shape, F32)
    acc[...] = jnp.zeros(acc.shape, F32)
    dq_cols[...] = jnp.zeros(dq_cols.shape, F32)
    for way, farthest in ((0, half), (1, half - 1)):
        ring_in[way, farthest] = jnp.zeros(ring_in.shape[2:], BF16)

    lane = lax.broadcasted_iota(jnp.int32, (TOK, HD), 1)
    first_half = lane < HD // 2
    cos = cosines[...]
    sin = sines[...]
    sin_turned = jnp.where(first_half, -sin, sin)

    def head_norm(tensor, gain):
        inv = lax.rsqrt(jnp.mean(tensor * tensor, axis=-1, keepdims=True) + NORM_EPS)
        hat = tensor * inv * gain
        return (hat * cos + pltpu.roll(hat, HD // 2, 1) * sin_turned).astype(BF16)

    def norm_back(tensor, gain, rot_grad):
        turned = pltpu.roll(rot_grad * sin, HD // 2, 1)
        hat_grad = rot_grad * cos + jnp.where(first_half, turned, -turned)
        inv = lax.rsqrt(jnp.mean(tensor * tensor, axis=-1, keepdims=True) + NORM_EPS)
        scaled = hat_grad * gain
        inner = jnp.mean(tensor * scaled, axis=-1, keepdims=True)
        return (inv * scaled - tensor * (inv * inv * inv) * inner).astype(BF16)

    def chunk(zz, xx, cc):
        return kv.at[rows(((zz * 2 + xx) * 2 + cc) * TOK)]

    def place(way, step):
        return lax.rem(z + (ring - step if way == 0 else step), ring)

    def group_x(group):
        return x if group == 0 else 1 - x

    def gather_copy(way, step, group, zz):
        ref = chunk(zz, group_x(group), c)
        sems = (gather_send.at[way, step, group], gather_recv.at[way, step, group])
        return copy(ref, ref, *sems, along[way])

    def core_copy(way, step, group, zz, cc):
        ref = chunk(zz, group_x(group), cc)
        sems = (core_send.at[way, step, group], core_recv.at[way, step, group])
        return copy(ref, ref, *sems, other_core)

    for load in loads[:3]:
        load.wait()
    codes_copy.wait_recv()

    @pl.when(sec == 0)
    def _():
        codes_in[...] = codes_edge[...]

    @pl.when(sec != 0)
    def _():
        codes_in[...] = codes_buf[...]

    wide = codes_in[...].astype(F32)
    inv_norm = lax.rsqrt(jnp.sum(wide * wide, axis=-1, keepdims=True) / D + NORM_EPS)
    normed = (wide * inv_norm).astype(BF16)
    key_lin = dot(normed, w_key[...])
    k_lin[...] = key_lin
    own = rows(((z * 2 + x) * 2 + c) * TOK)
    kv[own, :HD] = head_norm(key_lin, k_gain[...])
    kv[own, HD:] = dot(normed, w_value[...]).astype(BF16)

    kv_copy = copy_once(KV_X, chunk(z, x, c), chunk(z, x, c), across)
    kv_copy.start()
    for way in range(2):
        gather_copy(way, 1, 0, z).start()
    core_copy(0, 0, 0, z, c).start()

    loads[3].wait()
    q_lin[...] = dot(normed, w_query[...])
    for head in range(4):
        q_own[head * TOK : (head + 1) * TOK, :] = head_norm(
            q_lin[:, head * HD : (head + 1) * HD], q_gain[...]
        )
    peer_heads = rows((1 - x) * 2 * TOK, 2 * TOK)
    own_heads = rows(x * 2 * TOK, 2 * TOK)
    q_copy = copy_once(Q_X, q_own.at[peer_heads], q_rows.at[own_heads], across)
    q_copy.start()
    q_rows[own_heads, :] = q_own[own_heads, :]

    kv_copy.wait_recv()
    for way in range(2):
        gather_copy(way, 1, 1, z).start()
    core_copy(0, 0, 1, z, c).start()
    grads_copy.start()

    def turn(src, dst):
        for block in range(4):
            span = slice(block * TOK, (block + 1) * TOK)
            dst[:, span] = src[span, :].T

    q_copy.wait_recv()
    turn(q_rows, q_cols)

    scale = HD ** (-0.5)
    scale_two = scale * LOG2_E

    def own_mask(first_col):
        key = lax.broadcasted_iota(jnp.int32, (2 * TOK, 4 * TOK - first_col), 0)
        col = lax.broadcasted_iota(jnp.int32, (2 * TOK, 4 * TOK - first_col), 1) + first_col
        query = lax.rem(col, TOK) + c * TOK
        visible = key <= query
        if first_col == 0:
            visible = visible | (col >= 2 * TOK)
        return visible

    def forward_tile(start, first_col, masked):
        span = slice(first_col, 4 * TOK)
        block = rows(start, 2 * TOK)
        scores = dot(kv[block, :HD], q_cols[:, span]) * scale_two
        if masked:
            scores = jnp.where(own_mask(first_col), scores, 2 * MASK_FILL)
        top_old = top[:, span]
        top_new = jnp.maximum(top_old, jnp.max(scores, axis=0, keepdims=True))
        weights = jnp.exp2(scores - top_new)
        shrink = jnp.exp2(top_old - top_new)
        total[:, span] = total[:, span] * shrink + jnp.sum(weights, axis=0, keepdims=True)
        acc[:, span] = acc[:, span] * shrink + dot_first(kv[block, HD:], weights.astype(BF16))
        top[:, span] = top_new

    def arrive(way, step, forward):
        zz = place(way, step)
        for group in range(2):
            gather_copy(way, step, group, zz).wait_recv()

            @pl.when(forward)
            def _():
                gather_copy(way, step + 1, group, zz).start()

            core_copy(way, step, group, zz, c).start()

    def forward_block(way, step):
        zz = place(way, step)
        for group in range(2):
            core_copy(way, step, group, zz, 1 - c).wait_recv()

        @pl.when(zz < z)
        def _():
            forward_tile(zz * 4 * TOK, 0, False)
            forward_tile(zz * 4 * TOK + 2 * TOK, 2 * TOK, False)

        @pl.when(zz > z)
        def _():
            forward_tile(zz * 4 * TOK, 2 * TOK, False)

    for group in range(2):
        core_copy(0, 0, group, z, 1 - c).wait_recv()
    forward_tile(z * 4 * TOK, 0, True)
    arrive(0, 1, half > 1)
    arrive(1, 1, half > 2)
    forward_tile(z * 4 * TOK + 2 * TOK, 2 * TOK, True)

    for load in loads[4:]:
        load.wait()
    grads_copy.wait_recv()

    @pl.when(sec == sections - 1)
    def _():
        grads_in[...] = grads_edge[...]

    @pl.when(sec != sections - 1)
    def _():
        grads_in[...] = grads_buf[...]

    grad_att = dot_last(grads_in[...], w_out[...]).astype(BF16)
    for head in range(4):
        do_own[head * TOK : (head + 1) * TOK, :] = grad_att[:, head * HD : (head + 1) * HD]
    do_copy = copy_once(DO_X, do_own.at[peer_heads], do_rows.at[own_heads], across)
    do_copy.start()
    do_rows[own_heads, :] = do_own[own_heads, :]

    def forward_step(step, carry):
        arrive(0, step, step < half)
        forward_block(0, step - 1)
        arrive(1, step, step < half - 1)
        forward_block(1, step - 1)
        return carry

    lax.fori_loop(2, half, forward_step, 0)
    arrive(0, half, False)
    forward_block(0, half - 1)
    forward_block(1, half - 1)
    forward_block(0, half)

    do_copy.wait_recv()
    turn(do_rows, do_cols)
    attended = (acc[...] / total[...]).astype(BF16)
    delta[...] = jnp.sum(
        do_cols[...].astype(F32) * attended.astype(F32), axis=0, keepdims=True
    )
    top[...] = top[...] + jnp.log2(total[...])
    for block in range(4):
        span = slice(block * TOK, (block + 1) * TOK)
        att_rows[span, :] = attended[:, span].T
    att_copy = copy_once(ATT_X, att_rows.at[peer_heads], att_own.at[own_heads], across)
    att_copy.start()
    att_own[own_heads, :] = att_rows[own_heads, :]

    def backward_tile(way, step, start, first_row, first_col, masked):
        span = slice(first_col, 4 * TOK)
        block = rows(start, 2 * TOK)
        keys = kv[block, :HD]
        probs = jnp.exp2(dot(keys, q_cols[:, span]) * scale_two - top[:, span])
        if masked:
            probs = jnp.where(own_mask(first_col), probs, 0.0)
        grad_prob = dot(kv[block, HD:], do_cols[:, span])
        grad_score = (probs * (grad_prob - delta[:, span]) * scale).astype(BF16)
        dq_cols[:, span] += dot_first(keys, grad_score)
        out = slice(first_row, first_row + 2 * TOK)
        part[way, step, out, :HD] = dot(grad_score, q_rows[span, :])
        part[way, step, out, HD:] = dot(probs.astype(BF16), do_rows[span, :])

    def swap_copy(way, step, xx):
        return copy(
            part.at[way, step, rows((xx * 2 + 1 - c) * TOK)],
            part_core.at[way, step, rows(xx * TOK)],
            swap_send.at[way, step, xx],
            swap_recv.at[way, step, xx],
            other_core,
        )

    def backward_block(way, step):
        zz = place(1 - way, step)

        @pl.when(zz < z)
        def _():
            backward_tile(way, step, zz * 4 * TOK, 0, 0, False)
            backward_tile(way, step, zz * 4 * TOK + 2 * TOK, 2 * TOK, 2 * TOK, False)

        @pl.when(zz > z)
        def _():
            backward_tile(way, step, zz * 4 * TOK, 0, 2 * TOK, False)
            part[way, step, 2 * TOK :, :] = jnp.zeros((2 * TOK, 2 * HD), F32)

        for xx in range(2):
            swap_copy(way, step, xx).start()

    def reduce_copy(way, step, xx):
        return copy(
            ring_out.at[way, step, rows(xx * TOK)],
            ring_in.at[way, step - 1, rows(xx * TOK)],
            reduce_send.at[way, step, xx],
            reduce_recv.at[way, step - 1, xx],
            along[way],
        )

    def pair_sum(way, step, xx):
        swap_copy(way, step, xx).wait_recv()
        return part[way, step, rows((xx * 2 + c) * TOK), :] + part_core[way, step, rows(xx * TOK), :]

    def reduce_step(way, step, farthest):
        for xx in range(2):
            summed = pair_sum(way, step, xx)

            @pl.when(step < farthest)
            def _():
                reduce_copy(way, step + 1, xx).wait_recv()

            summed = summed + ring_in[way, step, rows(xx * TOK), :].astype(F32)
            ring_out[way, step, rows(xx * TOK), :] = summed.astype(BF16)
            reduce_copy(way, step, xx).start()

    backward_block(0, half)
    backward_block(1, half - 1)
    reduce_step(0, half, half)
    backward_block(0, half - 1)

    def backward_step(count, carry):
        step = half - count
        reduce_step(1, step + 1, half - 1)
        backward_block(1, step)
        reduce_step(0, step + 1, half)
        backward_block(0, step)
        return carry

    lax.fori_loop(2, half, backward_step, 0)
    backward_tile(0, 0, z * 4 * TOK, 0, 0, True)
    backward_tile(0, 0, z * 4 * TOK + 2 * TOK, 2 * TOK, 2 * TOK, True)
    for xx in range(2):
        swap_copy(0, 0, xx).start()
    reduce_step(0, 1, half)
    reduce_step(1, 1, half - 1)

    for block in range(4):
        span = slice(block * TOK, (block + 1) * TOK)
        dq_rows[span, :] = dq_cols[:, span].T
    dq_copy = copy_once(DQ_X, dq_rows.at[peer_heads], dq_own.at[own_heads], across)
    dq_copy.start()
    dq_own[own_heads, :] = dq_rows[own_heads, :]

    att_copy.wait_recv()
    result = codes_in[...].astype(F32)
    for head in range(4):
        span = slice(head * TOK, (head + 1) * TOK)
        result = result + dot(att_own[span, :], w_out[span, :])
    out_codes[...] = result.astype(BF16)

    for xx in range(2):
        summed = pair_sum(0, 0, xx)
        for way in range(2):
            reduce_copy(way, 1, xx).wait_recv()
            summed = summed + ring_in[way, 0, rows(xx * TOK), :].astype(F32)
        kv_total[xx] = summed
        kv_send[xx] = summed.astype(BF16)
    dkv_copy = copy_once(DKV_X, kv_send.at[1 - x], kv_peer, across)
    dkv_copy.start()

    dq_copy.wait_recv()
    normed_grad = jnp.zeros((TOK, w_query.shape[0]), F32)
    for head in range(4):
        span = slice(head * TOK, (head + 1) * TOK)
        lin_grad = norm_back(q_lin[:, span], q_gain[...], dq_own[span, :])
        normed_grad = normed_grad + dot_last(lin_grad, w_query[:, span])
    dkv_copy.wait_recv()
    kv_grad = kv_total[x] + kv_peer[...].astype(F32)
    key_grad = norm_back(k_lin[...], k_gain[...], kv_grad[:, :HD])
    normed_grad = normed_grad + dot_last(key_grad, w_key[...])
    normed_grad = normed_grad + dot_last(kv_grad[:, HD:].astype(BF16), w_value[...])
    wide = codes_in[...].astype(F32)
    inv_norm = lax.rsqrt(jnp.sum(wide * wide, axis=-1, keepdims=True) / D + NORM_EPS)
    inner = jnp.sum(wide * normed_grad, axis=-1, keepdims=True)
    in_grads[...] = (
        grads_in[...].astype(F32)
        + inv_norm * normed_grad
        - wide * (inv_norm * inv_norm * inv_norm) * inner / D
    ).astype(BF16)

    for once in (codes_copy, grads_copy, kv_copy, q_copy, do_copy, att_copy, dq_copy, dkv_copy):
        once.wait_send()

    def settle(way, step, gathers):
        for group in range(2):
            if gathers:
                gather_copy(way, step, group, z).wait_send()
                reduce_copy(way, step, group).wait_send()
            core_copy(way, step, group, z, c).wait_send()
            swap_copy(way, step, group).wait_send()

    settle(0, 0, False)

    def settle_both(step, carry):
        settle(0, step, True)
        settle(1, step, True)
        return carry

    lax.fori_loop(1, half, settle_both, 0)
    settle(0, half, True)


def rope_tables(positions, head_dim):
    half_dim = head_dim // 2
    exponent = jnp.arange(half_dim).astype(F32) * (2.0 / head_dim)
    frequency = jnp.power(F32(ROPE_BASE), -exponent)
    angles = positions.astype(F32)[:, None] * frequency[None, :]
    angles = jnp.concatenate([angles, angles], axis=-1)
    return (jnp.cos(angles), jnp.sin(angles))


def local(
    sent_codes, start_codes, sent_grads, loss_grads, w_query, w_key, w_value, w_out, q_gain, k_gain
):
    ring = lax.axis_size("seq") // 4
    sections = lax.axis_size("section")
    steps = ring // 2 + 1
    width = start_codes.shape[1]
    positions = lax.axis_index("seq") * TOK + jnp.arange(TOK, dtype=jnp.int32)
    cosines, sines = rope_tables(positions, HD)
    vmem = pltpu.VMEM
    dma = pltpu.SemaphoreType.DMA
    one_block = (TOK, width)
    heads = (4 * TOK, HD)
    columns = (HD, 4 * TOK)
    stat = (1, 4 * TOK)
    results = pl.pallas_call(
        functools.partial(kernel, ring, sections),
        out_shape=(jax.ShapeDtypeStruct(one_block, BF16),) * 2,
        in_specs=[pl.BlockSpec(memory_space=pltpu.HBM)] * 8 + [pl.BlockSpec(memory_space=vmem)] * 4,
        out_specs=(pl.BlockSpec(memory_space=vmem),) * 2,
        scratch_shapes=[
            vmem(w_query.shape[1:], BF16),
            vmem(w_key.shape[1:], BF16),
            vmem(w_value.shape[1:], BF16),
            vmem(w_out.shape[1:], BF16),
            vmem(one_block, BF16),
            vmem(one_block, BF16),
            vmem(one_block, BF16),
            vmem(one_block, BF16),
            vmem(one_block, BF16),
            vmem(one_block, BF16),
            vmem(one_block, F32),
            vmem((TOK, HD), F32),
            vmem(heads, BF16),
            vmem(heads, BF16),
            vmem(columns, BF16),
            vmem(heads, BF16),
            vmem(heads, BF16),
            vmem(columns, BF16),
            vmem((ring * 4 * TOK, 2 * HD), BF16),
            vmem(stat, F32),
            vmem(stat, F32),
            vmem(columns, F32),
            vmem(stat, F32),
            vmem(heads, BF16),
            vmem(heads, BF16),
            vmem(columns, F32),
            vmem(heads, F32),
            vmem(heads, F32),
            vmem((2, steps, 4 * TOK, 2 * HD), F32),
            vmem((2, steps, 2 * TOK, 2 * HD), F32),
            vmem((2, steps, 2 * TOK, 2 * HD), BF16),
            vmem((2, steps, 2 * TOK, 2 * HD), BF16),
            vmem((2, TOK, 2 * HD), F32),
            vmem((2, TOK, 2 * HD), BF16),
            vmem((TOK, 2 * HD), BF16),
            dma((8,)),
            dma((8,)),
            dma((2, steps, 2)),
            dma((2, steps, 2)),
            dma((2, steps, 2)),
            dma((2, steps, 2)),
            dma((2, steps, 2)),
            dma((2, steps, 2)),
            dma((2, steps, 2)),
            dma((2, steps, 2)),
            dma((6,)),
        ],
        compiler_params=pltpu.CompilerParams(
            collective_id=0, has_side_effects=True, vmem_limit_bytes=60 * 1024 * 1024
        ),
    )(
        sent_codes[0],
        start_codes,
        sent_grads[0],
        loss_grads,
        w_query[0],
        w_key[0],
        w_value[0],
        w_out[0],
        q_gain,
        k_gain,
        cosines,
        sines,
    )
    return (results[0][None], results[1][None])


def solution(mesh):
    in_specs = (
        P("section", "seq", None),
        P("seq", None),
        P("section", "seq", None),
        P("seq", None),
        P("section", None, None),
        P("section", None, None),
        P("section", None, None),
        P("section", None, None),
        P("section", None),
        P("section", None),
    )
    out_specs = (P("section", "seq", None), P("section", "seq", None))
    return jax.shard_map(local, mesh=mesh, in_specs=in_specs, out_specs=out_specs, check_vma=False)
```

```python
import functools

import jax
import jax.numpy as jnp
from jax import lax
from jax.experimental import pallas as pl
from jax.experimental.pallas import tpu as pltpu
from jax.sharding import PartitionSpec as P

D = 5120
ROPE_BASE = 1000000.0
NORM_EPS = 1e-06
MASK_FILL = -1e30
LOG2_E = 1.4426950408889634
MESH = pl.DeviceIdType.MESH
F32 = jnp.float32
BF16 = jnp.bfloat16
TOK = 128
HD = 128
CUT = 48
CONTRACT_LAST = (((1,), (1,)), ((), ()))
CONTRACT_FIRST = (((0,), (0,)), ((), ()))

CODES, GRADS, KV_X, Q_X, DO_X, ATT_X, DQ_X, DKV_X = range(8)


def dot(a, b):
    return jnp.dot(a, b, preferred_element_type=F32)


def dot_last(a, b):
    return lax.dot_general(a, b, CONTRACT_LAST, preferred_element_type=F32)


def dot_first(a, b):
    return lax.dot_general(a, b, CONTRACT_FIRST, preferred_element_type=F32)


def rows(start, count=TOK):
    return pl.ds(pl.multiple_of(start, TOK), count)


def kernel(
    ring,
    sections,
    sent_codes,
    start_codes,
    sent_grads,
    loss_grads,
    w_query_hbm,
    w_key_hbm,
    w_value_hbm,
    w_out_hbm,
    q_gain,
    k_gain,
    cosines,
    sines,
    out_codes,
    in_grads,
    w_query,
    w_key,
    w_value,
    w_out,
    codes_edge,
    grads_edge,
    codes_buf,
    grads_buf,
    codes_in,
    grads_in,
    q_lin,
    k_lin,
    q_own,
    q_rows,
    q_cols,
    do_own,
    do_rows,
    do_cols,
    kv,
    top,
    total,
    acc,
    delta,
    att_rows,
    att_own,
    dq_cols,
    dq_rows,
    dq_own,
    kept_scores,
    part,
    part_core,
    ring_out,
    ring_in,
    cross_out,
    cross_in,
    kv_grad,
    kv_send,
    kv_peer,
    once_send,
    once_recv,
    gather_send,
    gather_recv,
    core_send,
    core_recv,
    reduce_send,
    reduce_recv,
    swap_send,
    swap_recv,
    relay_send,
    relay_recv,
    cross_send,
    cross_recv,
    load_sems,
):
    half = ring // 2
    sec = lax.axis_index("section")
    me = lax.axis_index("seq")
    x = lax.div(me, 2 * ring)
    z = lax.rem(lax.div(me, 2), ring)
    c = lax.rem(me, 2)

    def device(xx, zz, cc):
        return (sec, (xx * ring + zz) * 2 + cc)

    along = (device(x, lax.rem(z + 1, ring), c), device(x, lax.rem(z + ring - 1, ring), c))
    other_core = device(x, z, 1 - c)
    across = device(1 - x, z, c)
    next_section = (lax.rem(sec + 1, sections), me)
    last_section = (lax.rem(sec + sections - 1, sections), me)

    def copy(src, dst, send, recv, target):
        return pltpu.make_async_remote_copy(
            src_ref=src,
            dst_ref=dst,
            send_sem=send,
            recv_sem=recv,
            device_id=target,
            device_id_type=MESH,
        )

    def copy_once(number, src, dst, target):
        return copy(src, dst, once_send.at[number], once_recv.at[number], target)

    loads = [
        pltpu.make_async_copy(src, dst, load_sems.at[number])
        for number, (src, dst) in enumerate(
            (
                (start_codes, codes_edge),
                (w_key_hbm, w_key),
                (w_value_hbm, w_value),
                (w_query_hbm, w_query),
                (loss_grads, grads_edge),
                (w_out_hbm, w_out),
            )
        )
    ]
    for load in loads:
        load.start()

    barrier = pltpu.get_barrier_semaphore()
    for partner in (along[0], along[1], other_core, across, next_section, last_section):
        pl.semaphore_signal(barrier, inc=1, device_id=partner, device_id_type=MESH)
    pl.semaphore_wait(barrier, 6)

    codes_copy = copy_once(CODES, sent_codes, codes_buf, next_section)
    grads_copy = copy_once(GRADS, sent_grads, grads_buf, last_section)
    codes_copy.start()

    top[...] = jnp.full(top.shape, MASK_FILL, F32)
    total[...] = jnp.zeros(total.shape, F32)
    acc[...] = jnp.zeros(acc.shape, F32)
    dq_cols[...] = jnp.zeros(dq_cols.shape, F32)
    for way, farthest in ((0, half), (1, half - 1)):
        ring_in[way, farthest] = jnp.zeros(ring_in.shape[2:], BF16)

    lane = lax.broadcasted_iota(jnp.int32, (TOK, HD), 1)
    first_half = lane < HD // 2
    cos = cosines[...]
    sin = sines[...]
    sin_turned = jnp.where(first_half, -sin, sin)

    def head_norm(tensor, gain):
        inv = lax.rsqrt(jnp.mean(tensor * tensor, axis=-1, keepdims=True) + NORM_EPS)
        hat = tensor * inv * gain
        return (hat * cos + pltpu.roll(hat, HD // 2, 1) * sin_turned).astype(BF16)

    def norm_back(tensor, gain, rot_grad):
        turned = pltpu.roll(rot_grad * sin, HD // 2, 1)
        hat_grad = rot_grad * cos + jnp.where(first_half, turned, -turned)
        inv = lax.rsqrt(jnp.mean(tensor * tensor, axis=-1, keepdims=True) + NORM_EPS)
        scaled = hat_grad * gain
        inner = jnp.mean(tensor * scaled, axis=-1, keepdims=True)
        return (inv * scaled - tensor * (inv * inv * inv) * inner).astype(BF16)

    def piece_of(piece, zz, cc, xx=None):
        if xx is None:
            xx = x if piece == 0 else 1 - x
        first, count = ((0, TOK), (0, CUT), (CUT, TOK - CUT))[piece]
        start = ((zz * 2 + xx) * 2 + cc) * TOK + first
        return kv.at[pl.ds(pl.multiple_of(start, 16), count)]

    def place(way, step):
        return lax.rem(z + (ring - step if way == 0 else step), ring)

    def gather_copy(way, step, piece, zz):
        ref = piece_of(piece, zz, c)
        sems = (gather_send.at[way, step, piece], gather_recv.at[way, step, piece])
        return copy(ref, ref, *sems, along[way])

    def core_copy(way, step, piece, zz, cc):
        ref = piece_of(piece, zz, cc)
        sems = (core_send.at[way, step, piece], core_recv.at[way, step, piece])
        return copy(ref, ref, *sems, other_core)

    def relay_copy(way, step, zz, xx):
        ref = piece_of(2, zz, c, xx)
        return copy(ref, ref, relay_send.at[way, step], relay_recv.at[way, step], across)

    for load in loads[:3]:
        load.wait()
    codes_copy.wait_recv()

    @pl.when(sec == 0)
    def _():
        codes_in[...] = codes_edge[...]

    @pl.when(sec != 0)
    def _():
        codes_in[...] = codes_buf[...]

    wide = codes_in[...].astype(F32)
    inv_norm = lax.rsqrt(jnp.sum(wide * wide, axis=-1, keepdims=True) / D + NORM_EPS)
    normed = (wide * inv_norm).astype(BF16)
    key_lin = dot(normed, w_key[...])
    k_lin[...] = key_lin
    own = rows(((z * 2 + x) * 2 + c) * TOK)
    kv[own, :HD] = head_norm(key_lin, k_gain[...])
    kv[own, HD:] = dot(normed, w_value[...]).astype(BF16)

    first_piece = piece_of(1, z, c, x)
    kv_copy = copy_once(KV_X, first_piece, first_piece, across)
    kv_copy.start()
    relay_copy(0, 0, z, x).start()
    for way in range(2):
        gather_copy(way, 1, 0, z).start()
    core_copy(0, 0, 0, z, c).start()

    loads[3].wait()
    q_lin[...] = dot(normed, w_query[...])
    for head in range(4):
        q_own[head * TOK : (head + 1) * TOK, :] = head_norm(
            q_lin[:, head * HD : (head + 1) * HD], q_gain[...]
        )
    peer_heads = rows((1 - x) * 2 * TOK, 2 * TOK)
    own_heads = rows(x * 2 * TOK, 2 * TOK)
    q_copy = copy_once(Q_X, q_own.at[peer_heads], q_rows.at[own_heads], across)
    q_copy.start()
    q_rows[own_heads, :] = q_own[own_heads, :]

    kv_copy.wait_recv()
    for way in range(2):
        gather_copy(way, 1, 1, z).start()
    core_copy(0, 0, 1, z, c).start()
    relay_copy(0, 0, z, 1 - x).wait_recv()
    core_copy(0, 0, 2, z, c).start()
    grads_copy.start()

    def turn(src, dst):
        for block in range(4):
            span = slice(block * TOK, (block + 1) * TOK)
            dst[:, span] = src[span, :].T

    q_copy.wait_recv()
    turn(q_rows, q_cols)

    scale = HD ** (-0.5)
    scale_two = scale * LOG2_E

    def own_mask(first_col):
        key = lax.broadcasted_iota(jnp.int32, (2 * TOK, 4 * TOK - first_col), 0)
        col = lax.broadcasted_iota(jnp.int32, (2 * TOK, 4 * TOK - first_col), 1) + first_col
        query = lax.rem(col, TOK) + c * TOK
        visible = key <= query
        if first_col == 0:
            visible = visible | (col >= 2 * TOK)
        return visible

    def forward_tile(way, step, zz, xx, first_col, masked):
        span = slice(first_col, 4 * TOK)
        block = rows((zz * 2 + xx) * 2 * TOK, 2 * TOK)
        scores = dot(kv[block, :HD], q_cols[:, span]) * scale_two
        if masked:
            scores = jnp.where(own_mask(first_col), scores, 2 * MASK_FILL)
        kept_scores[way, step, xx * 2 * TOK : (xx + 1) * 2 * TOK, span] = scores
        top_old = top[:, span]
        top_new = jnp.maximum(top_old, jnp.max(scores, axis=0, keepdims=True))
        weights = jnp.exp2(scores - top_new)
        shrink = jnp.exp2(top_old - top_new)
        total[:, span] = total[:, span] * shrink + jnp.sum(weights, axis=0, keepdims=True)
        acc[:, span] = acc[:, span] * shrink + dot_first(kv[block, HD:], weights.astype(BF16))
        top[:, span] = top_new

    def arrive(way, step, forward):
        zz = place(way, step)
        for piece in range(2):
            gather_copy(way, step, piece, zz).wait_recv()

            @pl.when(forward)
            def _():
                gather_copy(way, step + 1, piece, zz).start()

            if piece == 0:
                relay_copy(way, step, zz, x).start()
            core_copy(way, step, piece, zz, c).start()

    def arrive_across(way, step):
        zz = place(way, step)
        relay_copy(way, step, zz, 1 - x).wait_recv()
        core_copy(way, step, 2, zz, c).start()

    def forward_block(way, step):
        zz = place(way, step)
        for piece in range(3):
            core_copy(way, step, piece, zz, 1 - c).wait_recv()

        @pl.when(zz < z)
        def _():
            forward_tile(way, step, zz, 0, 0, False)
            forward_tile(way, step, zz, 1, 2 * TOK, False)

        @pl.when(zz > z)
        def _():
            forward_tile(way, step, zz, 0, 2 * TOK, False)

    for piece in range(3):
        core_copy(0, 0, piece, z, 1 - c).wait_recv()
    forward_tile(0, 0, z, 0, 0, True)
    arrive(0, 1, half > 1)
    arrive(1, 1, half > 2)
    forward_tile(0, 0, z, 1, 2 * TOK, True)

    for load in loads[4:]:
        load.wait()
    grads_copy.wait_recv()

    @pl.when(sec == sections - 1)
    def _():
        grads_in[...] = grads_edge[...]

    @pl.when(sec != sections - 1)
    def _():
        grads_in[...] = grads_buf[...]

    grad_att = dot_last(grads_in[...], w_out[...]).astype(BF16)
    for head in range(4):
        do_own[head * TOK : (head + 1) * TOK, :] = grad_att[:, head * HD : (head + 1) * HD]
    do_copy = copy_once(DO_X, do_own.at[peer_heads], do_rows.at[own_heads], across)
    do_copy.start()
    do_rows[own_heads, :] = do_own[own_heads, :]

    def forward_step(step, carry):
        arrive(0, step, step < half)
        arrive_across(0, step - 1)

        @pl.when(step > 2)
        def _():
            forward_block(1, step - 2)

        arrive(1, step, step < half - 1)
        arrive_across(1, step - 1)
        forward_block(0, step - 1)
        return carry

    lax.fori_loop(2, half, forward_step, 0)
    arrive(0, half, False)
    arrive_across(0, half - 1)
    if half > 2:
        forward_block(1, half - 2)
    arrive_across(1, half - 1)
    forward_block(0, half - 1)
    arrive_across(0, half)
    forward_block(1, half - 1)
    forward_block(0, half)

    do_copy.wait_recv()
    turn(do_rows, do_cols)
    attended = (acc[...] / total[...]).astype(BF16)
    delta[...] = jnp.sum(
        do_cols[...].astype(F32) * attended.astype(F32), axis=0, keepdims=True
    )
    top[...] = top[...] + jnp.log2(total[...])
    for block in range(4):
        span = slice(block * TOK, (block + 1) * TOK)
        att_rows[span, :] = attended[:, span].T
    att_copy = copy_once(ATT_X, att_rows.at[peer_heads], att_own.at[own_heads], across)
    att_copy.start()
    att_own[own_heads, :] = att_rows[own_heads, :]

    def backward_tile(way, step, came, zz, xx, first_col):
        span = slice(first_col, 4 * TOK)
        block = rows((zz * 2 + xx) * 2 * TOK, 2 * TOK)
        out = slice(xx * 2 * TOK, (xx + 1) * 2 * TOK)
        probs = jnp.exp2(kept_scores[came, step, out, span] - top[:, span])
        grad_prob = dot(kv[block, HD:], do_cols[:, span])
        grad_score = (probs * (grad_prob - delta[:, span]) * scale).astype(BF16)
        part[way, step, out, HD:] = dot(probs.astype(BF16), do_rows[span, :])
        part[way, step, out, :HD] = dot(grad_score, q_rows[span, :])
        dq_cols[:, span] += dot_first(kv[block, :HD], grad_score)

    def swap_copy(way, step, xx):
        return copy(
            part.at[way, step, rows((xx * 2 + 1 - c) * TOK)],
            part_core.at[way, step, rows(xx * TOK)],
            swap_send.at[way, step, xx],
            swap_recv.at[way, step, xx],
            other_core,
        )

    def backward_block(way, step, came=None):
        zz = place(1 - way, step)
        came = 1 - way if came is None else came

        @pl.when(zz < z)
        def _():
            backward_tile(way, step, came, zz, 0, 0)
            backward_tile(way, step, came, zz, 1, 2 * TOK)

        @pl.when(zz > z)
        def _():
            backward_tile(way, step, came, zz, 0, 2 * TOK)
            part[way, step, 2 * TOK :, :] = jnp.zeros((2 * TOK, 2 * HD), F32)

        for xx in range(2):
            swap_copy(way, step, xx).start()

    def pair_sum(way, step, xx, first, count):
        mine = pl.ds(pl.multiple_of((xx * 2 + c) * TOK + first, 16), count)
        theirs = pl.ds(pl.multiple_of(xx * TOK + first, 16), count)
        return part[way, step, mine, :] + part_core[way, step, theirs, :]

    def cross_copy(way, step):
        return copy(
            cross_out.at[way, step],
            cross_in.at[way, step],
            cross_send.at[way, step],
            cross_recv.at[way, step],
            across,
        )

    def cross_step(way, step):
        for xx in range(2):
            swap_copy(way, step, xx).wait_recv()
        cross_out[way, step] = pair_sum(way, step, 1 - x, CUT, TOK - CUT).astype(BF16)
        cross_copy(way, step).start()

    group_rows = (slice(0, TOK), slice(TOK, TOK + CUT))

    def reduce_copy(way, step, group):
        return copy(
            ring_out.at[way, step, group_rows[group]],
            ring_in.at[way, step - 1, group_rows[group]],
            reduce_send.at[way, step, group],
            reduce_recv.at[way, step - 1, group],
            along[way],
        )

    def reduce_step(way, step, farthest):
        def arrived(group):
            @pl.when(step < farthest)
            def _():
                reduce_copy(way, step + 1, group).wait_recv()

        arrived(0)
        ring_out[way, step, :CUT] = (
            pair_sum(way, step, x, 0, CUT) + ring_in[way, step, :CUT].astype(F32)
        ).astype(BF16)
        cross_copy(way, step).wait_recv()
        ring_out[way, step, CUT:TOK] = (
            pair_sum(way, step, x, CUT, TOK - CUT)
            + cross_in[way, step].astype(F32)
            + ring_in[way, step, CUT:TOK].astype(F32)
        ).astype(BF16)
        reduce_copy(way, step, 0).start()
        arrived(1)
        ring_out[way, step, TOK:] = (
            pair_sum(way, step, 1 - x, 0, CUT) + ring_in[way, step, TOK:].astype(F32)
        ).astype(BF16)
        reduce_copy(way, step, 1).start()

    backward_block(0, half, 0)
    backward_block(1, half - 1)
    cross_step(0, half)
    backward_block(0, half - 1)
    cross_step(1, half - 1)
    reduce_step(0, half, half)

    def backward_step(count, carry):
        step = half - count
        backward_block(1, step)
        cross_step(0, step + 1)
        reduce_step(1, step + 1, half - 1)
        backward_block(0, step)
        cross_step(1, step)
        reduce_step(0, step + 1, half)
        return carry

    lax.fori_loop(2, half, backward_step, 0)
    backward_tile(0, 0, 0, z, 0, 0)
    backward_tile(0, 0, 0, z, 1, 2 * TOK)
    for xx in range(2):
        swap_copy(0, 0, xx).start()
    cross_step(0, 1)
    reduce_step(1, 1, half - 1)
    cross_step(0, 0)
    reduce_step(0, 1, half)

    for block in range(4):
        span = slice(block * TOK, (block + 1) * TOK)
        dq_rows[span, :] = dq_cols[:, span].T
    dq_copy = copy_once(DQ_X, dq_rows.at[peer_heads], dq_own.at[own_heads], across)
    dq_copy.start()
    dq_own[own_heads, :] = dq_rows[own_heads, :]

    att_copy.wait_recv()
    result = codes_in[...].astype(F32)
    for head in range(4):
        span = slice(head * TOK, (head + 1) * TOK)
        result = result + dot(att_own[span, :], w_out[span, :])
    out_codes[...] = result.astype(BF16)

    def ring_total(span):
        return ring_in[0, 0, span].astype(F32) + ring_in[1, 0, span].astype(F32)

    for way in range(2):
        reduce_copy(way, 1, 1).wait_recv()
    kv_send[...] = (pair_sum(0, 0, 1 - x, 0, CUT) + ring_total(group_rows[1])).astype(BF16)
    dkv_copy = copy_once(DKV_X, kv_send, kv_peer, across)
    dkv_copy.start()

    dq_copy.wait_recv()
    normed_grad = jnp.zeros((TOK, w_query.shape[0]), F32)
    for head in range(4):
        span = slice(head * TOK, (head + 1) * TOK)
        lin_grad = norm_back(q_lin[:, span], q_gain[...], dq_own[span, :])
        normed_grad = normed_grad + dot_last(lin_grad, w_query[:, span])
    for way in range(2):
        reduce_copy(way, 1, 0).wait_recv()
    cross_copy(0, 0).wait_recv()
    kv_grad[CUT:, :] = (
        pair_sum(0, 0, x, CUT, TOK - CUT) + ring_total(slice(CUT, TOK)) + cross_in[0, 0].astype(F32)
    )
    dkv_copy.wait_recv()
    kv_grad[:CUT, :] = (
        pair_sum(0, 0, x, 0, CUT) + ring_total(slice(0, CUT)) + kv_peer[...].astype(F32)
    )
    key_grad = norm_back(k_lin[...], k_gain[...], kv_grad[:, :HD])
    normed_grad = normed_grad + dot_last(key_grad, w_key[...])
    normed_grad = normed_grad + dot_last(kv_grad[:, HD:].astype(BF16), w_value[...])
    wide = codes_in[...].astype(F32)
    inv_norm = lax.rsqrt(jnp.sum(wide * wide, axis=-1, keepdims=True) / D + NORM_EPS)
    inner = jnp.sum(wide * normed_grad, axis=-1, keepdims=True)
    in_grads[...] = (
        grads_in[...].astype(F32)
        + inv_norm * normed_grad
        - wide * (inv_norm * inv_norm * inv_norm) * inner / D
    ).astype(BF16)

    for once in (codes_copy, grads_copy, kv_copy, q_copy, do_copy, att_copy, dq_copy, dkv_copy):
        once.wait_send()

    def settle(way, step, gathers):
        for group in range(2):
            if gathers:
                gather_copy(way, step, group, z).wait_send()
                reduce_copy(way, step, group).wait_send()
            swap_copy(way, step, group).wait_send()
        for piece in range(3):
            core_copy(way, step, piece, z, c).wait_send()
        relay_copy(way, step, z, x).wait_send()
        cross_copy(way, step).wait_send()

    settle(0, 0, False)

    def settle_both(step, carry):
        settle(0, step, True)
        settle(1, step, True)
        return carry

    lax.fori_loop(1, half, settle_both, 0)
    settle(0, half, True)


def rope_tables(positions, head_dim):
    half_dim = head_dim // 2
    exponent = jnp.arange(half_dim).astype(F32) * (2.0 / head_dim)
    frequency = jnp.power(F32(ROPE_BASE), -exponent)
    angles = positions.astype(F32)[:, None] * frequency[None, :]
    angles = jnp.concatenate([angles, angles], axis=-1)
    return (jnp.cos(angles), jnp.sin(angles))


def local(
    sent_codes, start_codes, sent_grads, loss_grads, w_query, w_key, w_value, w_out, q_gain, k_gain
):
    ring = lax.axis_size("seq") // 4
    sections = lax.axis_size("section")
    steps = ring // 2 + 1
    width = start_codes.shape[1]
    positions = lax.axis_index("seq") * TOK + jnp.arange(TOK, dtype=jnp.int32)
    cosines, sines = rope_tables(positions, HD)
    vmem = pltpu.VMEM
    dma = pltpu.SemaphoreType.DMA
    one_block = (TOK, width)
    heads = (4 * TOK, HD)
    columns = (HD, 4 * TOK)
    stat = (1, 4 * TOK)
    results = pl.pallas_call(
        functools.partial(kernel, ring, sections),
        out_shape=(jax.ShapeDtypeStruct(one_block, BF16),) * 2,
        in_specs=[pl.BlockSpec(memory_space=pltpu.HBM)] * 8 + [pl.BlockSpec(memory_space=vmem)] * 4,
        out_specs=(pl.BlockSpec(memory_space=vmem),) * 2,
        scratch_shapes=[
            vmem(w_query.shape[1:], BF16),
            vmem(w_key.shape[1:], BF16),
            vmem(w_value.shape[1:], BF16),
            vmem(w_out.shape[1:], BF16),
            vmem(one_block, BF16),
            vmem(one_block, BF16),
            vmem(one_block, BF16),
            vmem(one_block, BF16),
            vmem(one_block, BF16),
            vmem(one_block, BF16),
            vmem(one_block, F32),
            vmem((TOK, HD), F32),
            vmem(heads, BF16),
            vmem(heads, BF16),
            vmem(columns, BF16),
            vmem(heads, BF16),
            vmem(heads, BF16),
            vmem(columns, BF16),
            vmem((ring * 4 * TOK, 2 * HD), BF16),
            vmem(stat, F32),
            vmem(stat, F32),
            vmem(columns, F32),
            vmem(stat, F32),
            vmem(heads, BF16),
            vmem(heads, BF16),
            vmem(columns, F32),
            vmem(heads, F32),
            vmem(heads, F32),
            vmem((2, steps, 4 * TOK, 4 * TOK), F32),
            vmem((2, steps, 4 * TOK, 2 * HD), F32),
            vmem((2, steps, 2 * TOK, 2 * HD), F32),
            vmem((2, steps, TOK + CUT, 2 * HD), BF16),
            vmem((2, steps, TOK + CUT, 2 * HD), BF16),
            vmem((2, steps, TOK - CUT, 2 * HD), BF16),
            vmem((2, steps, TOK - CUT, 2 * HD), BF16),
            vmem((TOK, 2 * HD), F32),
            vmem((CUT, 2 * HD), BF16),
            vmem((CUT, 2 * HD), BF16),
            dma((8,)),
            dma((8,)),
            dma((2, steps, 2)),
            dma((2, steps, 2)),
            dma((2, steps, 3)),
            dma((2, steps, 3)),
            dma((2, steps, 2)),
            dma((2, steps, 2)),
            dma((2, steps, 2)),
            dma((2, steps, 2)),
            dma((2, steps)),
            dma((2, steps)),
            dma((2, steps)),
            dma((2, steps)),
            dma((6,)),
        ],
        compiler_params=pltpu.CompilerParams(
            collective_id=0, has_side_effects=True, vmem_limit_bytes=60 * 1024 * 1024
        ),
    )(
        sent_codes[0],
        start_codes,
        sent_grads[0],
        loss_grads,
        w_query[0],
        w_key[0],
        w_value[0],
        w_out[0],
        q_gain,
        k_gain,
        cosines,
        sines,
    )
    return (results[0][None], results[1][None])


def solution(mesh):
    in_specs = (
        P("section", "seq", None),
        P("seq", None),
        P("section", "seq", None),
        P("seq", None),
        P("section", None, None),
        P("section", None, None),
        P("section", None, None),
        P("section", None, None),
        P("section", None),
        P("section", None),
    )
    out_specs = (P("section", "seq", None), P("section", "seq", None))
    return jax.shard_map(local, mesh=mesh, in_specs=in_specs, out_specs=out_specs, check_vma=False)
```

```python
import functools

import jax
import jax.numpy as jnp
from jax import lax
from jax.experimental import pallas as pl
from jax.experimental.pallas import tpu as pltpu
from jax.sharding import PartitionSpec as P

D = 5120
ROPE_BASE = 1000000.0
NORM_EPS = 1e-06
MASK_FILL = -1e30
LOG2_E = 1.4426950408889634
MESH = pl.DeviceIdType.MESH
F32 = jnp.float32
BF16 = jnp.bfloat16
TOK = 128
HD = 128
CUT = 48
CONTRACT_LAST = (((1,), (1,)), ((), ()))
CONTRACT_FIRST = (((0,), (0,)), ((), ()))

CODES, GRADS, KV_X, Q_X, DO_X, ATT_X, DQ_X, DKV_X = range(8)


def dot(a, b):
    return jnp.dot(a, b, preferred_element_type=F32)


def dot_last(a, b):
    return lax.dot_general(a, b, CONTRACT_LAST, preferred_element_type=F32)


def dot_first(a, b):
    return lax.dot_general(a, b, CONTRACT_FIRST, preferred_element_type=F32)


def rows(start, count=TOK):
    return pl.ds(pl.multiple_of(start, TOK), count)


def kernel(
    ring,
    sections,
    sent_codes,
    start_codes,
    sent_grads,
    loss_grads,
    w_query_hbm,
    w_key_hbm,
    w_value_hbm,
    w_out_hbm,
    q_gain,
    k_gain,
    cosines,
    sines,
    out_codes,
    in_grads,
    w_query,
    w_key,
    w_value,
    w_out,
    codes_edge,
    grads_edge,
    codes_buf,
    grads_buf,
    codes_in,
    grads_in,
    q_lin,
    k_lin,
    q_own,
    q_rows,
    q_cols,
    do_own,
    do_rows,
    do_cols,
    kv,
    top,
    total,
    acc,
    delta,
    att_rows,
    att_own,
    dq_cols,
    dq_rows,
    dq_own,
    kept_scores,
    part,
    part_core,
    ring_out,
    ring_in,
    cross_out,
    cross_in,
    kv_grad,
    kv_send,
    kv_peer,
    once_send,
    once_recv,
    gather_send,
    gather_recv,
    core_send,
    core_recv,
    reduce_send,
    reduce_recv,
    swap_send,
    swap_recv,
    relay_send,
    relay_recv,
    cross_send,
    cross_recv,
    load_sems,
):
    half = ring // 2
    sec = lax.axis_index("section")
    me = lax.axis_index("seq")
    x = lax.div(me, 2 * ring)
    z = lax.rem(lax.div(me, 2), ring)
    c = lax.rem(me, 2)

    def device(xx, zz, cc):
        return (sec, (xx * ring + zz) * 2 + cc)

    def along(way):
        return device(x, lax.rem(z + 1 + way * (ring - 2), ring), c)

    other_core = device(x, z, 1 - c)
    across = device(1 - x, z, c)
    next_section = (lax.rem(sec + 1, sections), me)
    last_section = (lax.rem(sec + sections - 1, sections), me)

    def copy(src, dst, send, recv, target):
        return pltpu.make_async_remote_copy(
            src_ref=src,
            dst_ref=dst,
            send_sem=send,
            recv_sem=recv,
            device_id=target,
            device_id_type=MESH,
        )

    def copy_once(number, src, dst, target):
        return copy(src, dst, once_send.at[number], once_recv.at[number], target)

    loads = [
        pltpu.make_async_copy(src, dst, load_sems.at[number])
        for number, (src, dst) in enumerate(
            (
                (start_codes, codes_edge),
                (w_key_hbm, w_key),
                (w_value_hbm, w_value),
                (w_query_hbm, w_query),
                (loss_grads, grads_edge),
                (w_out_hbm, w_out),
            )
        )
    ]
    for load in loads:
        load.start()

    barrier = pltpu.get_barrier_semaphore()
    for partner in (along(0), along(1), other_core, across, next_section, last_section):
        pl.semaphore_signal(barrier, inc=1, device_id=partner, device_id_type=MESH)
    pl.semaphore_wait(barrier, 6)

    codes_copy = copy_once(CODES, sent_codes, codes_buf, next_section)
    grads_copy = copy_once(GRADS, sent_grads, grads_buf, last_section)
    codes_copy.start()

    top[...] = jnp.full(top.shape, MASK_FILL, F32)
    total[...] = jnp.zeros(total.shape, F32)
    acc[...] = jnp.zeros(acc.shape, F32)
    dq_cols[...] = jnp.zeros(dq_cols.shape, F32)
    for way, farthest in ((0, half), (1, half - 1)):
        ring_in[way, farthest] = jnp.zeros(ring_in.shape[2:], BF16)

    lane = lax.broadcasted_iota(jnp.int32, (TOK, HD), 1)
    first_half = lane < HD // 2
    cos = cosines[...]
    sin = sines[...]
    sin_turned = jnp.where(first_half, -sin, sin)

    def head_norm(tensor, gain):
        inv = lax.rsqrt(jnp.mean(tensor * tensor, axis=-1, keepdims=True) + NORM_EPS)
        hat = tensor * inv * gain
        return (hat * cos + pltpu.roll(hat, HD // 2, 1) * sin_turned).astype(BF16)

    def norm_back(tensor, gain, rot_grad):
        turned = pltpu.roll(rot_grad * sin, HD // 2, 1)
        hat_grad = rot_grad * cos + jnp.where(first_half, turned, -turned)
        inv = lax.rsqrt(jnp.mean(tensor * tensor, axis=-1, keepdims=True) + NORM_EPS)
        scaled = hat_grad * gain
        inner = jnp.mean(tensor * scaled, axis=-1, keepdims=True)
        return (inv * scaled - tensor * (inv * inv * inv) * inner).astype(BF16)

    def piece_of(piece, zz, cc, xx=None):
        if xx is None:
            xx = x if piece == 0 else 1 - x
        first, count = ((0, TOK), (0, CUT), (CUT, TOK - CUT))[piece]
        start = ((zz * 2 + xx) * 2 + cc) * TOK + first
        return kv.at[pl.ds(pl.multiple_of(start, 16), count)]

    def place(way, step):
        return lax.rem(z + way * step + (1 - way) * (ring - step), ring)

    def gather_copy(way, step, piece, zz):
        ref = piece_of(piece, zz, c)
        sems = (gather_send.at[way, step, piece], gather_recv.at[way, step, piece])
        return copy(ref, ref, *sems, along(way))

    def core_copy(way, step, piece, zz, cc):
        ref = piece_of(piece, zz, cc)
        sems = (core_send.at[way, step, piece], core_recv.at[way, step, piece])
        return copy(ref, ref, *sems, other_core)

    def relay_copy(way, step, zz, xx):
        ref = piece_of(2, zz, c, xx)
        return copy(ref, ref, relay_send.at[way, step], relay_recv.at[way, step], across)

    for load in loads[:3]:
        load.wait()
    codes_copy.wait_recv()

    @pl.when(sec == 0)
    def _():
        codes_in[...] = codes_edge[...]

    @pl.when(sec != 0)
    def _():
        codes_in[...] = codes_buf[...]

    wide = codes_in[...].astype(F32)
    inv_norm = lax.rsqrt(jnp.sum(wide * wide, axis=-1, keepdims=True) / D + NORM_EPS)
    normed = (wide * inv_norm).astype(BF16)
    key_lin = dot(normed, w_key[...])
    k_lin[...] = key_lin
    own = rows(((z * 2 + x) * 2 + c) * TOK)
    kv[own, :HD] = head_norm(key_lin, k_gain[...])
    kv[own, HD:] = dot(normed, w_value[...]).astype(BF16)

    first_piece = piece_of(1, z, c, x)
    kv_copy = copy_once(KV_X, first_piece, first_piece, across)
    kv_copy.start()
    relay_copy(0, 0, z, x).start()
    for way in range(2):
        gather_copy(way, 1, 0, z).start()
    core_copy(0, 0, 0, z, c).start()

    loads[3].wait()
    q_lin[...] = dot(normed, w_query[...])
    for head in range(4):
        q_own[head * TOK : (head + 1) * TOK, :] = head_norm(
            q_lin[:, head * HD : (head + 1) * HD], q_gain[...]
        )
    peer_heads = rows((1 - x) * 2 * TOK, 2 * TOK)
    own_heads = rows(x * 2 * TOK, 2 * TOK)
    q_copy = copy_once(Q_X, q_own.at[peer_heads], q_rows.at[own_heads], across)
    q_copy.start()
    q_rows[own_heads, :] = q_own[own_heads, :]

    kv_copy.wait_recv()
    for way in range(2):
        gather_copy(way, 1, 1, z).start()
    core_copy(0, 0, 1, z, c).start()
    relay_copy(0, 0, z, 1 - x).wait_recv()
    core_copy(0, 0, 2, z, c).start()
    grads_copy.start()

    def turn(src, dst):
        for block in range(4):
            span = slice(block * TOK, (block + 1) * TOK)
            dst[:, span] = src[span, :].T

    q_copy.wait_recv()
    turn(q_rows, q_cols)

    scale = HD ** (-0.5)
    scale_two = scale * LOG2_E

    def own_mask(first_col):
        key = lax.broadcasted_iota(jnp.int32, (2 * TOK, 4 * TOK - first_col), 0)
        col = lax.broadcasted_iota(jnp.int32, (2 * TOK, 4 * TOK - first_col), 1) + first_col
        query = lax.rem(col, TOK) + c * TOK
        visible = key <= query
        if first_col == 0:
            visible = visible | (col >= 2 * TOK)
        return visible

    def forward_tile(kept, step, zz, xx, first_col, masked):
        span = slice(first_col, 4 * TOK)
        block = rows((zz * 2 + xx) * 2 * TOK, 2 * TOK)
        scores = dot(kv[block, :HD], q_cols[:, span]) * scale_two
        if masked:
            scores = jnp.where(own_mask(first_col), scores, 2 * MASK_FILL)
        kept_scores[kept, step, rows(xx * 2 * TOK, 2 * TOK), span] = scores
        top_old = top[:, span]
        top_new = jnp.maximum(top_old, jnp.max(scores, axis=0, keepdims=True))
        weights = jnp.exp2(scores - top_new)
        shrink = jnp.exp2(top_old - top_new)
        total[:, span] = total[:, span] * shrink + jnp.sum(weights, axis=0, keepdims=True)
        acc[:, span] = acc[:, span] * shrink + dot_first(kv[block, HD:], weights.astype(BF16))
        top[:, span] = top_new

    def arrive(way, step, forward):
        zz = place(way, step)
        for piece in range(2):
            gather_copy(way, step, piece, zz).wait_recv()

            @pl.when(forward)
            def _():
                gather_copy(way, step + 1, piece, zz).start()

            if piece == 0:
                relay_copy(way, step, zz, x).start()
            core_copy(way, step, piece, zz, c).start()

    def arrive_across(way, step):
        zz = place(way, step)
        relay_copy(way, step, zz, 1 - x).wait_recv()
        core_copy(way, step, 2, zz, c).start()

    def gathered(item):
        return lax.rem(item + 1, 2), lax.div(item + 1, 2)

    def forward_block(item):
        way, step = gathered(item)
        zz = place(way, step)
        for piece in range(3):
            core_copy(way, step, piece, zz, 1 - c).wait_recv()
        kept = way + lax.div(step, half)

        @pl.when(zz < z)
        def _():
            forward_tile(kept, step, zz, 0, 0, False)

        forward_tile(kept, step, zz, jnp.where(zz < z, 1, 0), 2 * TOK, False)

    arrive(0, 1, half > 1)
    for piece in range(3):
        core_copy(0, 0, piece, z, 1 - c).wait_recv()
    forward_tile(0, 0, z, 0, 0, True)
    arrive(1, 1, half > 2)
    forward_tile(0, 0, z, 1, 2 * TOK, True)

    for load in loads[4:]:
        load.wait()
    grads_copy.wait_recv()

    @pl.when(sec == sections - 1)
    def _():
        grads_in[...] = grads_edge[...]

    @pl.when(sec != sections - 1)
    def _():
        grads_in[...] = grads_buf[...]

    grad_att = dot_last(grads_in[...], w_out[...]).astype(BF16)
    for head in range(4):
        do_own[head * TOK : (head + 1) * TOK, :] = grad_att[:, head * HD : (head + 1) * HD]
    do_copy = copy_once(DO_X, do_own.at[peer_heads], do_rows.at[own_heads], across)
    do_copy.start()
    do_rows[own_heads, :] = do_own[own_heads, :]

    def forward_step(item, carry):
        @pl.when(item < ring)
        def _():
            way, step = gathered(item)
            arrive(way, step, step < half - way)

        @pl.when(item < ring + 2)
        def _():
            arrive_across(*gathered(item - 2))

        @pl.when(item > 3)
        def _():
            forward_block(item - 3)

        return carry

    lax.fori_loop(3, ring + 3, forward_step, 0)

    do_copy.wait_recv()
    turn(do_rows, do_cols)
    attended = (acc[...] / total[...]).astype(BF16)
    delta[...] = jnp.sum(
        do_cols[...].astype(F32) * attended.astype(F32), axis=0, keepdims=True
    )
    top[...] = top[...] + jnp.log2(total[...])
    for block in range(4):
        span = slice(block * TOK, (block + 1) * TOK)
        att_rows[span, :] = attended[:, span].T
    att_copy = copy_once(ATT_X, att_rows.at[peer_heads], att_own.at[own_heads], across)
    att_copy.start()
    att_own[own_heads, :] = att_rows[own_heads, :]

    def backward_tile(way, step, zz, xx, first_col):
        span = slice(first_col, 4 * TOK)
        block = rows((zz * 2 + xx) * 2 * TOK, 2 * TOK)
        out = rows(xx * 2 * TOK, 2 * TOK)
        probs = jnp.exp2(kept_scores[1 - way, step, out, span] - top[:, span])
        grad_prob = dot(kv[block, HD:], do_cols[:, span])
        grad_score = (probs * (grad_prob - delta[:, span]) * scale).astype(BF16)
        part[way, step, out, HD:] = dot(probs.astype(BF16), do_rows[span, :])
        part[way, step, out, :HD] = dot(grad_score, q_rows[span, :])
        dq_cols[:, span] += dot_first(kv[block, :HD], grad_score)

    def swap_copy(way, step, xx):
        return copy(
            part.at[way, step, rows((xx * 2 + 1 - c) * TOK)],
            part_core.at[way, step, rows(xx * TOK)],
            swap_send.at[way, step, xx],
            swap_recv.at[way, step, xx],
            other_core,
        )

    def leaving(item):
        return lax.rem(item, 2), half - lax.div(item + 1, 2)

    def backward_block(item):
        way, step = leaving(item)
        zz = place(1 - way, step)

        @pl.when(zz <= z)
        def _():
            backward_tile(way, step, zz, 0, 0)

        @pl.when(zz > z)
        def _():
            part[way, step, 2 * TOK :, :] = jnp.zeros((2 * TOK, 2 * HD), F32)

        backward_tile(way, step, zz, jnp.where(zz <= z, 1, 0), 2 * TOK)
        for xx in range(2):
            swap_copy(way, step, xx).start()

    def pair_sum(way, step, xx, first, count):
        mine = pl.ds(pl.multiple_of((xx * 2 + c) * TOK + first, 16), count)
        theirs = pl.ds(pl.multiple_of(xx * TOK + first, 16), count)
        return part[way, step, mine, :] + part_core[way, step, theirs, :]

    def cross_copy(way, step):
        return copy(
            cross_out.at[way, step],
            cross_in.at[way, step],
            cross_send.at[way, step],
            cross_recv.at[way, step],
            across,
        )

    def cross_step(way, step):
        for xx in range(2):
            swap_copy(way, step, xx).wait_recv()
        cross_out[way, step] = pair_sum(way, step, 1 - x, CUT, TOK - CUT).astype(BF16)
        cross_copy(way, step).start()

    group_rows = (slice(0, TOK), slice(TOK, TOK + CUT))

    def reduce_copy(way, step, group):
        return copy(
            ring_out.at[way, step, group_rows[group]],
            ring_in.at[way, step - 1, group_rows[group]],
            reduce_send.at[way, step, group],
            reduce_recv.at[way, step - 1, group],
            along(way),
        )

    def reduce_step(way, step, farthest):
        def arrived(group):
            @pl.when(step < farthest)
            def _():
                reduce_copy(way, step + 1, group).wait_recv()

        arrived(0)
        ring_out[way, step, :CUT] = (
            pair_sum(way, step, x, 0, CUT) + ring_in[way, step, :CUT].astype(F32)
        ).astype(BF16)
        cross_copy(way, step).wait_recv()
        ring_out[way, step, CUT:TOK] = (
            pair_sum(way, step, x, CUT, TOK - CUT)
            + cross_in[way, step].astype(F32)
            + ring_in[way, step, CUT:TOK].astype(F32)
        ).astype(BF16)
        reduce_copy(way, step, 0).start()
        arrived(1)
        ring_out[way, step, TOK:] = (
            pair_sum(way, step, 1 - x, 0, CUT) + ring_in[way, step, TOK:].astype(F32)
        ).astype(BF16)
        reduce_copy(way, step, 1).start()

    def backward_step(item, carry):
        @pl.when(item < ring)
        def _():
            backward_block(item)

        @pl.when(item >= 1)
        def _():
            cross_step(*leaving(item - 1))

        @pl.when(item >= 2)
        def _():
            way, step = leaving(item - 2)
            reduce_step(way, step, half - way)

        return carry

    lax.fori_loop(0, ring + 1, backward_step, 0)

    for block in range(4):
        span = slice(block * TOK, (block + 1) * TOK)
        dq_rows[span, :] = dq_cols[:, span].T
    dq_copy = copy_once(DQ_X, dq_rows.at[peer_heads], dq_own.at[own_heads], across)
    dq_copy.start()
    dq_own[own_heads, :] = dq_rows[own_heads, :]

    att_copy.wait_recv()
    result = codes_in[...].astype(F32)
    for head in range(4):
        span = slice(head * TOK, (head + 1) * TOK)
        result = result + dot(att_own[span, :], w_out[span, :])
    out_codes[...] = result.astype(BF16)

    def ring_total(span):
        return ring_in[0, 0, span].astype(F32) + ring_in[1, 0, span].astype(F32)

    for way in range(2):
        reduce_copy(way, 1, 1).wait_recv()
    kv_send[...] = (pair_sum(1, 0, 1 - x, 0, CUT) + ring_total(group_rows[1])).astype(BF16)
    dkv_copy = copy_once(DKV_X, kv_send, kv_peer, across)
    dkv_copy.start()

    dq_copy.wait_recv()
    normed_grad = jnp.zeros((TOK, w_query.shape[0]), F32)
    for head in range(4):
        span = slice(head * TOK, (head + 1) * TOK)
        lin_grad = norm_back(q_lin[:, span], q_gain[...], dq_own[span, :])
        normed_grad = normed_grad + dot_last(lin_grad, w_query[:, span])
    for way in range(2):
        reduce_copy(way, 1, 0).wait_recv()
    cross_copy(1, 0).wait_recv()
    kv_grad[CUT:, :] = (
        pair_sum(1, 0, x, CUT, TOK - CUT) + ring_total(slice(CUT, TOK)) + cross_in[1, 0].astype(F32)
    )
    dkv_copy.wait_recv()
    kv_grad[:CUT, :] = (
        pair_sum(1, 0, x, 0, CUT) + ring_total(slice(0, CUT)) + kv_peer[...].astype(F32)
    )
    key_grad = norm_back(k_lin[...], k_gain[...], kv_grad[:, :HD])
    normed_grad = normed_grad + dot_last(key_grad, w_key[...])
    normed_grad = normed_grad + dot_last(kv_grad[:, HD:].astype(BF16), w_value[...])
    wide = codes_in[...].astype(F32)
    inv_norm = lax.rsqrt(jnp.sum(wide * wide, axis=-1, keepdims=True) / D + NORM_EPS)
    inner = jnp.sum(wide * normed_grad, axis=-1, keepdims=True)
    in_grads[...] = (
        grads_in[...].astype(F32)
        + inv_norm * normed_grad
        - wide * (inv_norm * inv_norm * inv_norm) * inner / D
    ).astype(BF16)

    for once in (codes_copy, grads_copy, kv_copy, q_copy, do_copy, att_copy, dq_copy, dkv_copy):
        once.wait_send()

    def settle_gather(item, carry):
        way, step = gathered(item)
        for piece in range(3):
            core_copy(way, step, piece, z, c).wait_send()
        relay_copy(way, step, z, x).wait_send()
        for piece in range(2):
            gather_copy(way, step, piece, z).wait_send()
        return carry

    def settle_reduce(item, carry):
        way, step = leaving(item)
        for xx in range(2):
            swap_copy(way, step, xx).wait_send()
        cross_copy(way, step).wait_send()

        @pl.when(step > 0)
        def _():
            for group in range(2):
                reduce_copy(way, step, group).wait_send()

        return carry

    lax.fori_loop(1, ring, settle_gather, 0)
    for piece in range(3):
        core_copy(0, 0, piece, z, c).wait_send()
    relay_copy(0, 0, z, x).wait_send()
    lax.fori_loop(0, ring, settle_reduce, 0)


def rope_tables(positions, head_dim):
    half_dim = head_dim // 2
    exponent = jnp.arange(half_dim).astype(F32) * (2.0 / head_dim)
    frequency = jnp.power(F32(ROPE_BASE), -exponent)
    angles = positions.astype(F32)[:, None] * frequency[None, :]
    angles = jnp.concatenate([angles, angles], axis=-1)
    return (jnp.cos(angles), jnp.sin(angles))


def local(
    sent_codes, start_codes, sent_grads, loss_grads, w_query, w_key, w_value, w_out, q_gain, k_gain
):
    ring = lax.axis_size("seq") // 4
    sections = lax.axis_size("section")
    steps = ring // 2 + 1
    width = start_codes.shape[1]
    positions = lax.axis_index("seq") * TOK + jnp.arange(TOK, dtype=jnp.int32)
    cosines, sines = rope_tables(positions, HD)
    vmem = pltpu.VMEM
    dma = pltpu.SemaphoreType.DMA
    one_block = (TOK, width)
    heads = (4 * TOK, HD)
    columns = (HD, 4 * TOK)
    stat = (1, 4 * TOK)
    results = pl.pallas_call(
        functools.partial(kernel, ring, sections),
        out_shape=(jax.ShapeDtypeStruct(one_block, BF16),) * 2,
        in_specs=[pl.BlockSpec(memory_space=pltpu.HBM)] * 8 + [pl.BlockSpec(memory_space=vmem)] * 4,
        out_specs=(pl.BlockSpec(memory_space=vmem),) * 2,
        scratch_shapes=[
            vmem(w_query.shape[1:], BF16),
            vmem(w_key.shape[1:], BF16),
            vmem(w_value.shape[1:], BF16),
            vmem(w_out.shape[1:], BF16),
            vmem(one_block, BF16),
            vmem(one_block, BF16),
            vmem(one_block, BF16),
            vmem(one_block, BF16),
            vmem(one_block, BF16),
            vmem(one_block, BF16),
            vmem(one_block, F32),
            vmem((TOK, HD), F32),
            vmem(heads, BF16),
            vmem(heads, BF16),
            vmem(columns, BF16),
            vmem(heads, BF16),
            vmem(heads, BF16),
            vmem(columns, BF16),
            vmem((ring * 4 * TOK, 2 * HD), BF16),
            vmem(stat, F32),
            vmem(stat, F32),
            vmem(columns, F32),
            vmem(stat, F32),
            vmem(heads, BF16),
            vmem(heads, BF16),
            vmem(columns, F32),
            vmem(heads, F32),
            vmem(heads, F32),
            vmem((2, steps, 4 * TOK, 4 * TOK), F32),
            vmem((2, steps, 4 * TOK, 2 * HD), F32),
            vmem((2, steps, 2 * TOK, 2 * HD), F32),
            vmem((2, steps, TOK + CUT, 2 * HD), BF16),
            vmem((2, steps, TOK + CUT, 2 * HD), BF16),
            vmem((2, steps, TOK - CUT, 2 * HD), BF16),
            vmem((2, steps, TOK - CUT, 2 * HD), BF16),
            vmem((TOK, 2 * HD), F32),
            vmem((CUT, 2 * HD), BF16),
            vmem((CUT, 2 * HD), BF16),
            dma((8,)),
            dma((8,)),
            dma((2, steps, 2)),
            dma((2, steps, 2)),
            dma((2, steps, 3)),
            dma((2, steps, 3)),
            dma((2, steps, 2)),
            dma((2, steps, 2)),
            dma((2, steps, 2)),
            dma((2, steps, 2)),
            dma((2, steps)),
            dma((2, steps)),
            dma((2, steps)),
            dma((2, steps)),
            dma((6,)),
        ],
        compiler_params=pltpu.CompilerParams(
            collective_id=0, has_side_effects=True, vmem_limit_bytes=60 * 1024 * 1024
        ),
    )(
        sent_codes[0],
        start_codes,
        sent_grads[0],
        loss_grads,
        w_query[0],
        w_key[0],
        w_value[0],
        w_out[0],
        q_gain,
        k_gain,
        cosines,
        sines,
    )
    return (results[0][None], results[1][None])


def solution(mesh):
    in_specs = (
        P("section", "seq", None),
        P("seq", None),
        P("section", "seq", None),
        P("seq", None),
        P("section", None, None),
        P("section", None, None),
        P("section", None, None),
        P("section", None, None),
        P("section", None),
        P("section", None),
    )
    out_specs = (P("section", "seq", None), P("section", "seq", None))
    return jax.shard_map(local, mesh=mesh, in_specs=in_specs, out_specs=out_specs, check_vma=False)
```

```python
import functools

import jax
import jax.numpy as jnp
from jax import lax
from jax.experimental import pallas as pl
from jax.experimental.pallas import tpu as pltpu
from jax.sharding import PartitionSpec as P

D = 5120
ROPE_BASE = 1000000.0
NORM_EPS = 1e-06
MASK_FILL = -1e30
LOG2_E = 1.4426950408889634
MESH = pl.DeviceIdType.MESH
F32 = jnp.float32
BF16 = jnp.bfloat16
TOK = 128
HD = 128
PIECE = 64
CONTRACT_LAST = (((1,), (1,)), ((), ()))
CONTRACT_FIRST = (((0,), (0,)), ((), ()))

CODES, GRADS, KV_X, ATT_X, DQ_X, DKV_X, ACC_C, STATS_C, DQ_C0, DQ_C1 = range(10)
Q_X, Q_C, Q_R, DO_X, DO_C, DO_R = range(10, 16)


def dot(a, b):
    return jnp.dot(a, b, preferred_element_type=F32)


def dot_last(a, b):
    return lax.dot_general(a, b, CONTRACT_LAST, preferred_element_type=F32)


def dot_first(a, b):
    return lax.dot_general(a, b, CONTRACT_FIRST, preferred_element_type=F32)


def rows(start, count=TOK):
    return pl.ds(pl.multiple_of(start, TOK), count)


def kernel(
    ring,
    sections,
    sent_codes,
    start_codes,
    sent_grads,
    loss_grads,
    w_query_hbm,
    w_key_hbm,
    w_value_hbm,
    w_out_hbm,
    q_gain,
    k_gain,
    cosines,
    sines,
    out_codes,
    in_grads,
    w_query,
    w_key,
    w_value,
    w_out,
    codes_edge,
    grads_edge,
    codes_buf,
    grads_buf,
    codes_in,
    grads_in,
    q_lin,
    k_lin,
    q_own,
    q_rows,
    q_cols,
    do_own,
    do_rows,
    do_cols,
    kv,
    stats,
    stats_peer,
    acc,
    acc_peer,
    lse,
    delta,
    att_cols,
    att_rows,
    att_own,
    dq_cols,
    dq_rows,
    dq_core,
    dq_out,
    dq_own,
    kept_scores,
    part,
    ring_out,
    ring_in,
    cross_out,
    cross_in,
    kv_grad,
    kv_send,
    kv_peer,
    once_send,
    once_recv,
    gather_send,
    gather_recv,
    reduce_send,
    reduce_recv,
    relay_send,
    relay_recv,
    cross_send,
    cross_recv,
    load_sems,
):
    half = ring // 2
    sec = lax.axis_index("section")
    me = lax.axis_index("seq")
    x = lax.div(me, 2 * ring)
    z = lax.rem(lax.div(me, 2), ring)
    c = lax.rem(me, 2)

    def device(xx, zz, cc):
        return (sec, (xx * ring + zz) * 2 + cc)

    def along(way):
        return device(x, lax.rem(z + 1 + way * (ring - 2), ring), c)

    other_core = device(x, z, 1 - c)
    across = device(1 - x, z, c)
    next_section = (lax.rem(sec + 1, sections), me)
    last_section = (lax.rem(sec + sections - 1, sections), me)

    def copy(src, dst, send, recv, target):
        return pltpu.make_async_remote_copy(
            src_ref=src,
            dst_ref=dst,
            send_sem=send,
            recv_sem=recv,
            device_id=target,
            device_id_type=MESH,
        )

    def copy_once(number, src, dst, target):
        return copy(src, dst, once_send.at[number], once_recv.at[number], target)

    loads = [
        pltpu.make_async_copy(src, dst, load_sems.at[number])
        for number, (src, dst) in enumerate(
            (
                (start_codes, codes_edge),
                (w_key_hbm, w_key),
                (w_value_hbm, w_value),
                (w_query_hbm, w_query),
                (loss_grads, grads_edge),
                (w_out_hbm, w_out),
            )
        )
    ]
    for load in loads:
        load.start()

    barrier = pltpu.get_barrier_semaphore()
    for partner in (along(0), along(1), other_core, across, next_section, last_section):
        pl.semaphore_signal(barrier, inc=1, device_id=partner, device_id_type=MESH)
    pl.semaphore_wait(barrier, 6)

    codes_copy = copy_once(CODES, sent_codes, codes_buf, next_section)
    grads_copy = copy_once(GRADS, sent_grads, grads_buf, last_section)
    codes_copy.start()

    stats[...] = jnp.where(
        lax.broadcasted_iota(jnp.int32, stats.shape, 0) == 0, F32(MASK_FILL), F32(0.0)
    )
    acc[...] = jnp.zeros(acc.shape, F32)
    dq_cols[...] = jnp.zeros(dq_cols.shape, F32)
    for way, farthest in ((0, half), (1, half - 1)):
        ring_in[way, farthest] = jnp.zeros(ring_in.shape[2:], BF16)

    lane = lax.broadcasted_iota(jnp.int32, (TOK, HD), 1)
    first_half = lane < HD // 2
    cos = cosines[...]
    sin = sines[...]
    sin_turned = jnp.where(first_half, -sin, sin)

    def head_norm(tensor, gain):
        inv = lax.rsqrt(jnp.mean(tensor * tensor, axis=-1, keepdims=True) + NORM_EPS)
        hat = tensor * inv * gain
        return (hat * cos + pltpu.roll(hat, HD // 2, 1) * sin_turned).astype(BF16)

    def norm_back(tensor, gain, rot_grad):
        turned = pltpu.roll(rot_grad * sin, HD // 2, 1)
        hat_grad = rot_grad * cos + jnp.where(first_half, turned, -turned)
        inv = lax.rsqrt(jnp.mean(tensor * tensor, axis=-1, keepdims=True) + NORM_EPS)
        scaled = hat_grad * gain
        inner = jnp.mean(tensor * scaled, axis=-1, keepdims=True)
        return (inv * scaled - tensor * (inv * inv * inv) * inner).astype(BF16)

    def piece_of(piece, zz, xx=None):
        if xx is None:
            xx = x if piece < 2 else 1 - x
        start = (zz * 2 + xx) * TOK + piece % 2 * PIECE
        return kv.at[pl.ds(pl.multiple_of(start, PIECE), PIECE)]

    def place(way, step):
        return lax.rem(z + way * step + (1 - way) * (ring - step), ring)

    def gather_copy(way, step, piece, zz):
        ref = piece_of(piece, zz)
        sems = (gather_send.at[way, step, piece], gather_recv.at[way, step, piece])
        return copy(ref, ref, *sems, along(way))

    def relay_copy(way, step, zz, xx):
        ref = piece_of(3, zz, xx)
        return copy(ref, ref, relay_send.at[way, step], relay_recv.at[way, step], across)

    peer_heads = rows((1 - x) * 2 * TOK, 2 * TOK)
    own_heads = rows(x * 2 * TOK, 2 * TOK)
    own_rows = rows((x * 2 + c) * 2 * TOK, 2 * TOK)
    relay_rows = rows(((1 - x) * 2 + c) * 2 * TOK, 2 * TOK)

    def spread(number, src, dst):
        return (
            copy_once(number, src.at[peer_heads], dst.at[own_rows], across),
            copy_once(number + 1, src.at[own_heads], dst.at[own_rows], other_core),
            copy_once(number + 2, dst.at[relay_rows], dst.at[relay_rows], other_core),
        )

    q_copies = spread(Q_X, q_own, q_rows)
    do_copies = spread(DO_X, do_own, do_rows)

    def turn(src, dst):
        for block in range(src.shape[0] // TOK):
            span = slice(block * TOK, (block + 1) * TOK)
            dst[:, span] = src[span, :].T

    for load in loads[:3]:
        load.wait()
    codes_copy.wait_recv()

    @pl.when(sec == 0)
    def _():
        codes_in[...] = codes_edge[...]

    @pl.when(sec != 0)
    def _():
        codes_in[...] = codes_buf[...]

    wide = codes_in[...].astype(F32)
    inv_norm = lax.rsqrt(jnp.sum(wide * wide, axis=-1, keepdims=True) / D + NORM_EPS)
    normed = (wide * inv_norm).astype(BF16)
    key_lin = dot(normed, w_key[...])
    k_lin[...] = key_lin
    own = rows((z * 2 + x) * TOK)
    kv[own, :HD] = head_norm(key_lin, k_gain[...])
    kv[own, HD:] = dot(normed, w_value[...]).astype(BF16)

    first_piece = piece_of(0, z, x)
    kv_copy = copy_once(KV_X, first_piece, first_piece, across)
    kv_copy.start()
    relay_copy(0, 0, z, x).start()
    for piece in (1, 0):
        for way in range(2):
            gather_copy(way, 1, piece, z).start()

    loads[3].wait()
    q_lin[...] = dot(normed, w_query[...])
    for head in range(4):
        q_own[head * TOK : (head + 1) * TOK, :] = head_norm(
            q_lin[:, head * HD : (head + 1) * HD], q_gain[...]
        )
    q_copies[0].start()
    q_copies[1].start()
    q_rows[own_rows, :] = q_own[own_heads, :]

    kv_copy.wait_recv()
    for way in range(2):
        gather_copy(way, 1, 2, z).start()
    grads_copy.start()
    q_copies[0].wait_recv()
    q_copies[2].start()

    scale = HD ** (-0.5)
    scale_two = scale * LOG2_E
    all_cols = 8 * TOK
    late = 4 * TOK

    def own_mask(first_col):
        shape = (TOK, all_cols - first_col)
        key = lax.broadcasted_iota(jnp.int32, shape, 0) + c * TOK
        col = lax.broadcasted_iota(jnp.int32, shape, 1) + first_col
        query = (col & (TOK - 1)) + ((col & (2 * TOK)) >> 1)
        visible = key <= query
        if first_col == 0:
            visible = visible | (col >= late)
        return visible

    def forward_tile(kept, step, zz, xx, first_col, masked):
        span = slice(first_col, all_cols)
        block = rows((zz * 2 + xx) * TOK)
        scores = dot(kv[block, :HD], q_cols[:, span]) * scale_two
        if masked:
            scores = jnp.where(own_mask(first_col), scores, 2 * MASK_FILL)
        kept_scores[kept, step, rows(xx * TOK), span] = scores
        top_old = stats[0:1, span]
        top_new = jnp.maximum(top_old, jnp.max(scores, axis=0, keepdims=True))
        weights = jnp.exp2(scores - top_new)
        shrink = jnp.exp2(top_old - top_new)
        stats[1:2, span] = stats[1:2, span] * shrink + jnp.sum(weights, axis=0, keepdims=True)
        acc[:, span] = acc[:, span] * shrink + dot_first(kv[block, HD:], weights.astype(BF16))
        stats[0:1, span] = top_new

    def arrive(way, step, forward):
        zz = place(way, step)
        for piece in (1, 0, 2):
            gather_copy(way, step, piece, zz).wait_recv()

            @pl.when(forward)
            def _():
                gather_copy(way, step + 1, piece, zz).start()

            if piece == 1:
                relay_copy(way, step, zz, x).start()

    def gathered(item):
        return lax.rem(item + 1, 2), lax.div(item + 1, 2)

    def forward_block(item):
        way, step = gathered(item)
        zz = place(way, step)
        relay_copy(way, step, zz, 1 - x).wait_recv()
        kept = way + lax.div(step, half)

        @pl.when(zz < z)
        def _():
            forward_tile(kept, step, zz, 0, 0, False)
            forward_tile(kept, step, zz, 1, late, False)

        @pl.when(zz > z)
        def _():
            forward_tile(kept, step, zz, 0, late, False)

    arrive(0, 1, half > 1)
    arrive(1, 1, half > 2)
    q_copies[1].wait_recv()
    q_copies[2].wait_recv()
    turn(q_rows, q_cols)
    relay_copy(0, 0, z, 1 - x).wait_recv()
    forward_tile(0, 0, z, 0, 0, True)
    forward_tile(0, 0, z, 1, late, True)

    def forward_step(item, carry):
        @pl.when(item < ring)
        def _():
            way, step = gathered(item)
            arrive(way, step, step < half - way)

        forward_block(item - 2)

        @pl.when(item == 3 + ring // 4)
        def _():
            for load in loads[4:]:
                load.wait()
            grads_copy.wait_recv()

            @pl.when(sec == sections - 1)
            def _():
                grads_in[...] = grads_edge[...]

            @pl.when(sec != sections - 1)
            def _():
                grads_in[...] = grads_buf[...]

            grad_att = dot_last(grads_in[...], w_out[...]).astype(BF16)
            for head in range(4):
                do_own[head * TOK : (head + 1) * TOK, :] = grad_att[:, head * HD : (head + 1) * HD]
            do_copies[0].start()
            do_copies[1].start()
            do_rows[own_rows, :] = do_own[own_heads, :]

        @pl.when(item == 3 + ring // 2)
        def _():
            do_copies[0].wait_recv()
            do_copies[2].start()

        return carry

    lax.fori_loop(3, ring + 2, forward_step, 0)

    acc_copy = copy_once(ACC_C, acc, acc_peer, other_core)
    stats_copy = copy_once(STATS_C, stats, stats_peer, other_core)
    stats_copy.start()
    acc_copy.start()
    do_copies[1].wait_recv()
    do_copies[2].wait_recv()
    turn(do_rows, do_cols)
    stats_copy.wait_recv()
    top = jnp.maximum(stats[0:1, :], stats_peer[0:1, :])
    shrink = jnp.exp2(stats[0:1, :] - top)
    shrink_peer = jnp.exp2(stats_peer[0:1, :] - top)
    total = stats[1:2, :] * shrink + stats_peer[1:2, :] * shrink_peer
    lse[...] = top + jnp.log2(total)
    acc_copy.wait_recv()
    attended = ((acc[...] * shrink + acc_peer[...] * shrink_peer) / total).astype(BF16)
    delta[...] = jnp.sum(
        do_cols[...].astype(F32) * attended.astype(F32), axis=0, keepdims=True
    )
    att_cols[...] = attended

    def backward_tile(way, step, zz, xx, first_col):
        span = slice(first_col, all_cols)
        block = rows((zz * 2 + xx) * TOK)
        out = rows(xx * TOK)
        probs = jnp.exp2(kept_scores[1 - way, step, out, span] - lse[:, span])
        grad_prob = dot(kv[block, HD:], do_cols[:, span])
        grad_score = (probs * (grad_prob - delta[:, span]) * scale).astype(BF16)
        part[way, step, out, HD:] = dot(probs.astype(BF16), do_rows[span, :])
        part[way, step, out, :HD] = dot(grad_score, q_rows[span, :])
        dq_cols[:, span] += dot_first(kv[block, :HD], grad_score)

    def leaving(item):
        return lax.rem(item, 2), half - lax.div(item + 1, 2)

    def own_part(way, step, piece):
        xx = x if piece < 2 else 1 - x
        return part[way, step, pl.ds(pl.multiple_of(xx * TOK + piece % 2 * PIECE, PIECE), PIECE), :]

    def cross_copy(way, step):
        return copy(
            cross_out.at[way, step],
            cross_in.at[way, step],
            cross_send.at[way, step],
            cross_recv.at[way, step],
            across,
        )

    def backward_block(item):
        way, step = leaving(item)
        zz = place(1 - way, step)

        @pl.when(zz <= z)
        def _():
            backward_tile(way, step, zz, 0, 0)
            backward_tile(way, step, zz, 1, late)

        @pl.when(zz > z)
        def _():
            backward_tile(way, step, zz, 0, late)
            part[way, step, TOK:, :] = jnp.zeros((TOK, 2 * HD), F32)

        cross_out[way, step] = own_part(way, step, 3).astype(BF16)
        cross_copy(way, step).start()

    def reduce_copy(way, step, piece):
        span = slice(piece * PIECE, (piece + 1) * PIECE)
        return copy(
            ring_out.at[way, step, span],
            ring_in.at[way, step - 1, span],
            reduce_send.at[way, step, piece],
            reduce_recv.at[way, step - 1, piece],
            along(way),
        )

    def reduce_step(item):
        way, step = leaving(item)
        for piece in (0, 2, 1):

            @pl.when(step < half - way)
            def _():
                reduce_copy(way, step + 1, piece).wait_recv()

            span = slice(piece * PIECE, (piece + 1) * PIECE)
            summed = own_part(way, step, piece) + ring_in[way, step, span].astype(F32)
            if piece == 1:
                cross_copy(way, step).wait_recv()
                summed = summed + cross_in[way, step].astype(F32)
            ring_out[way, step, span] = summed.astype(BF16)
            reduce_copy(way, step, piece).start()

    def backward_step(pair, carry):
        backward_block(2 * pair)
        backward_block(2 * pair + 1)

        @pl.when(pair > 0)
        def _():
            reduce_step(pair - 1)

        return carry

    def reduce_only(item, carry):
        reduce_step(item)
        return carry

    lax.fori_loop(0, half, backward_step, 0)

    turn_back = [(xx, head) for xx in range(2) for head in range(2)]
    for block in range(8):
        span = slice(block * TOK, (block + 1) * TOK)
        dq_rows[span, :] = dq_cols[:, span].T
    dq_core_copies = [
        copy_once(
            number,
            dq_rows.at[rows((xx * 2 + 1 - c) * 2 * TOK, 2 * TOK)],
            dq_core.at[rows(xx * 2 * TOK, 2 * TOK)],
            other_core,
        )
        for xx, number in enumerate((DQ_C0, DQ_C1))
    ]
    for number in range(2):
        dq_core_copies[number].start()
    reduce_step(half - 1)

    for number in range(2):
        dq_core_copies[number].wait_recv()
    dq_out[...] = dq_rows[relay_rows, :] + dq_core[peer_heads, :]
    dq_copy = copy_once(DQ_X, dq_out, dq_own.at[own_heads], across)
    dq_copy.start()
    dq_own[own_heads, :] = dq_rows[own_rows, :] + dq_core[own_heads, :]

    for xx, head in turn_back:
        cols = rows(((xx * 2 + c) * 2 + head) * TOK)
        att_rows[(xx * 2 + head) * TOK : (xx * 2 + head + 1) * TOK, :] = att_cols[:, cols].T
    att_copy = copy_once(ATT_X, att_rows.at[peer_heads], att_own.at[own_heads], across)
    att_copy.start()
    att_own[own_heads, :] = att_rows[own_heads, :]

    lax.fori_loop(half, ring - 1, reduce_only, 0)

    att_copy.wait_recv()
    result = codes_in[...].astype(F32)
    for head in range(4):
        span = slice(head * TOK, (head + 1) * TOK)
        result = result + dot(att_own[span, :], w_out[span, :])
    out_codes[...] = result.astype(BF16)

    dq_copy.wait_recv()
    normed_grad = jnp.zeros((TOK, w_query.shape[0]), F32)
    for head in range(4):
        span = slice(head * TOK, (head + 1) * TOK)
        lin_grad = norm_back(q_lin[:, span], q_gain[...], dq_own[span, :])
        normed_grad = normed_grad + dot_last(lin_grad, w_query[:, span])

    def own_total(piece):
        for way in range(2):
            reduce_copy(way, 1, piece).wait_recv()
        span = slice(piece * PIECE, (piece + 1) * PIECE)
        ringed = ring_in[0, 0, span].astype(F32) + ring_in[1, 0, span].astype(F32)
        return own_part(1, 0, piece) + ringed

    kv_send[...] = own_total(2).astype(BF16)
    dkv_copy = copy_once(DKV_X, kv_send, kv_peer, across)
    dkv_copy.start()

    cross_copy(1, 0).wait_recv()
    kv_grad[PIECE:, :] = own_total(1) + cross_in[1, 0].astype(F32)
    first_total = own_total(0)
    dkv_copy.wait_recv()
    kv_grad[:PIECE, :] = first_total + kv_peer[...].astype(F32)
    key_grad = norm_back(k_lin[...], k_gain[...], kv_grad[:, :HD])
    normed_grad = normed_grad + dot_last(key_grad, w_key[...])
    normed_grad = normed_grad + dot_last(kv_grad[:, HD:].astype(BF16), w_value[...])
    wide = codes_in[...].astype(F32)
    inv_norm = lax.rsqrt(jnp.sum(wide * wide, axis=-1, keepdims=True) / D + NORM_EPS)
    inner = jnp.sum(wide * normed_grad, axis=-1, keepdims=True)
    in_grads[...] = (
        grads_in[...].astype(F32)
        + inv_norm * normed_grad
        - wide * (inv_norm * inv_norm * inv_norm) * inner / D
    ).astype(BF16)

    for once in (codes_copy, grads_copy, kv_copy, acc_copy, stats_copy, att_copy, dq_copy, dkv_copy):
        once.wait_send()
    for once in (*q_copies, *do_copies, *dq_core_copies):
        once.wait_send()

    def settle_gather(item, carry):
        way, step = gathered(item)
        relay_copy(way, step, z, x).wait_send()
        for piece in range(3):
            gather_copy(way, step, piece, z).wait_send()
        return carry

    def settle_reduce(item, carry):
        way, step = leaving(item)
        cross_copy(way, step).wait_send()

        @pl.when(step > 0)
        def _():
            for piece in range(3):
                reduce_copy(way, step, piece).wait_send()

        return carry

    lax.fori_loop(1, ring, settle_gather, 0)
    relay_copy(0, 0, z, x).wait_send()
    lax.fori_loop(0, ring, settle_reduce, 0)


def rope_tables(positions, head_dim):
    half_dim = head_dim // 2
    exponent = jnp.arange(half_dim).astype(F32) * (2.0 / head_dim)
    frequency = jnp.power(F32(ROPE_BASE), -exponent)
    angles = positions.astype(F32)[:, None] * frequency[None, :]
    angles = jnp.concatenate([angles, angles], axis=-1)
    return (jnp.cos(angles), jnp.sin(angles))


def local(
    sent_codes, start_codes, sent_grads, loss_grads, w_query, w_key, w_value, w_out, q_gain, k_gain
):
    ring = lax.axis_size("seq") // 4
    sections = lax.axis_size("section")
    steps = ring // 2 + 1
    width = start_codes.shape[1]
    positions = lax.axis_index("seq") * TOK + jnp.arange(TOK, dtype=jnp.int32)
    cosines, sines = rope_tables(positions, HD)
    vmem = pltpu.VMEM
    dma = pltpu.SemaphoreType.DMA
    one_block = (TOK, width)
    heads = (4 * TOK, HD)
    all_rows = (8 * TOK, HD)
    columns = (HD, 8 * TOK)
    stat = (1, 8 * TOK)
    results = pl.pallas_call(
        functools.partial(kernel, ring, sections),
        out_shape=(jax.ShapeDtypeStruct(one_block, BF16),) * 2,
        in_specs=[pl.BlockSpec(memory_space=pltpu.HBM)] * 8 + [pl.BlockSpec(memory_space=vmem)] * 4,
        out_specs=(pl.BlockSpec(memory_space=vmem),) * 2,
        scratch_shapes=[
            vmem(w_query.shape[1:], BF16),
            vmem(w_key.shape[1:], BF16),
            vmem(w_value.shape[1:], BF16),
            vmem(w_out.shape[1:], BF16),
            vmem(one_block, BF16),
            vmem(one_block, BF16),
            vmem(one_block, BF16),
            vmem(one_block, BF16),
            vmem(one_block, BF16),
            vmem(one_block, BF16),
            vmem(one_block, F32),
            vmem((TOK, HD), F32),
            vmem(heads, BF16),
            vmem(all_rows, BF16),
            vmem(columns, BF16),
            vmem(heads, BF16),
            vmem(all_rows, BF16),
            vmem(columns, BF16),
            vmem((ring * 2 * TOK, 2 * HD), BF16),
            vmem((8, 8 * TOK), F32),
            vmem((8, 8 * TOK), F32),
            vmem(columns, F32),
            vmem(columns, F32),
            vmem(stat, F32),
            vmem(stat, F32),
            vmem(columns, BF16),
            vmem(heads, BF16),
            vmem(heads, BF16),
            vmem(columns, F32),
            vmem(all_rows, F32),
            vmem(heads, F32),
            vmem((2 * TOK, HD), F32),
            vmem(heads, F32),
            vmem((2, steps, 2 * TOK, 8 * TOK), F32),
            vmem((2, steps, 2 * TOK, 2 * HD), F32),
            vmem((2, steps, 3 * PIECE, 2 * HD), BF16),
            vmem((2, steps, 3 * PIECE, 2 * HD), BF16),
            vmem((2, steps, PIECE, 2 * HD), BF16),
            vmem((2, steps, PIECE, 2 * HD), BF16),
            vmem((TOK, 2 * HD), F32),
            vmem((PIECE, 2 * HD), BF16),
            vmem((PIECE, 2 * HD), BF16),
            dma((16,)),
            dma((16,)),
            dma((2, steps, 3)),
            dma((2, steps, 3)),
            dma((2, steps, 3)),
            dma((2, steps, 3)),
            dma((2, steps)),
            dma((2, steps)),
            dma((2, steps)),
            dma((2, steps)),
            dma((6,)),
        ],
        compiler_params=pltpu.CompilerParams(
            collective_id=0, has_side_effects=True, vmem_limit_bytes=60 * 1024 * 1024
        ),
    )(
        sent_codes[0],
        start_codes,
        sent_grads[0],
        loss_grads,
        w_query[0],
        w_key[0],
        w_value[0],
        w_out[0],
        q_gain,
        k_gain,
        cosines,
        sines,
    )
    return (results[0][None], results[1][None])


def solution(mesh):
    in_specs = (
        P("section", "seq", None),
        P("seq", None),
        P("section", "seq", None),
        P("seq", None),
        P("section", None, None),
        P("section", None, None),
        P("section", None, None),
        P("section", None, None),
        P("section", None),
        P("section", None),
    )
    out_specs = (P("section", "seq", None), P("section", "seq", None))
    return jax.shard_map(local, mesh=mesh, in_specs=in_specs, out_specs=out_specs, check_vma=False)
```

```python
import functools

import jax
import jax.numpy as jnp
from jax import lax
from jax.experimental import pallas as pl
from jax.experimental.pallas import tpu as pltpu
from jax.sharding import PartitionSpec as P

D = 5120
ROPE_BASE = 1000000.0
NORM_EPS = 1e-06
MASK_FILL = -1e30
LOG2_E = 1.4426950408889634
MESH = pl.DeviceIdType.MESH
F32 = jnp.float32
BF16 = jnp.bfloat16
TOK = 128
HD = 128
PIECE = 64
CONTRACT_LAST = (((1,), (1,)), ((), ()))
CONTRACT_FIRST = (((0,), (0,)), ((), ()))

CODES, GRADS, KV_X, ATT_X, DQ_X, DKV_X, ACC_C, STATS_C, DQ_C0, DQ_C1 = range(10)
Q_X, Q_C, Q_R, DO_X, DO_C, DO_R = range(10, 16)


def dot(a, b):
    return jnp.dot(a, b, preferred_element_type=F32)


def dot_last(a, b):
    return lax.dot_general(a, b, CONTRACT_LAST, preferred_element_type=F32)


def dot_first(a, b):
    return lax.dot_general(a, b, CONTRACT_FIRST, preferred_element_type=F32)


def rows(start, count=TOK):
    return pl.ds(pl.multiple_of(start, TOK), count)


def kernel(
    ring,
    sections,
    sent_codes,
    start_codes,
    sent_grads,
    loss_grads,
    w_query_hbm,
    w_key_hbm,
    w_value_hbm,
    w_out_hbm,
    q_gain,
    k_gain,
    cosines,
    sines,
    out_codes,
    in_grads,
    w_query,
    w_key,
    w_value,
    w_out,
    codes_edge,
    grads_edge,
    codes_buf,
    grads_buf,
    codes_in,
    grads_in,
    q_lin,
    k_lin,
    q_own,
    q_rows,
    q_cols,
    do_own,
    do_rows,
    do_cols,
    kv,
    stats,
    stats_peer,
    acc,
    acc_peer,
    lse,
    delta,
    att_cols,
    att_rows,
    att_own,
    dq_cols,
    dq_rows,
    dq_core,
    dq_out,
    dq_own,
    kept_scores,
    part,
    ring_out,
    ring_in,
    cross_out,
    cross_in,
    kv_grad,
    kv_send,
    kv_peer,
    once_send,
    once_recv,
    gather_send,
    gather_recv,
    reduce_send,
    reduce_recv,
    relay_send,
    relay_recv,
    cross_send,
    cross_recv,
    load_sems,
):
    half = ring // 2
    sec = lax.axis_index("section")
    me = lax.axis_index("seq")
    x = lax.div(me, 2 * ring)
    z = lax.rem(lax.div(me, 2), ring)
    c = lax.rem(me, 2)

    def device(xx, zz, cc):
        return (sec, (xx * ring + zz) * 2 + cc)

    def along(way):
        return device(x, lax.rem(z + 1 + way * (ring - 2), ring), c)

    def diagonal(way):
        return device(1 - x, lax.rem(z + 1 + way * (ring - 2), ring), c)

    other_core = device(x, z, 1 - c)
    across = device(1 - x, z, c)
    next_section = (lax.rem(sec + 1, sections), me)
    last_section = (lax.rem(sec + sections - 1, sections), me)

    def copy(src, dst, send, recv, target):
        return pltpu.make_async_remote_copy(
            src_ref=src,
            dst_ref=dst,
            send_sem=send,
            recv_sem=recv,
            device_id=target,
            device_id_type=MESH,
        )

    def copy_once(number, src, dst, target):
        return copy(src, dst, once_send.at[number], once_recv.at[number], target)

    loads = [
        pltpu.make_async_copy(src, dst, load_sems.at[number])
        for number, (src, dst) in enumerate(
            (
                (start_codes, codes_edge),
                (w_key_hbm, w_key),
                (w_value_hbm, w_value),
                (w_query_hbm, w_query),
                (loss_grads, grads_edge),
                (w_out_hbm, w_out),
            )
        )
    ]
    for load in loads:
        load.start()

    barrier = pltpu.get_barrier_semaphore()
    partners = (along(0), along(1), diagonal(0), diagonal(1), other_core, across)
    for partner in (*partners, next_section, last_section):
        pl.semaphore_signal(barrier, inc=1, device_id=partner, device_id_type=MESH)
    pl.semaphore_wait(barrier, 8)

    codes_copy = copy_once(CODES, sent_codes, codes_buf, next_section)
    grads_copy = copy_once(GRADS, sent_grads, grads_buf, last_section)
    codes_copy.start()

    stats[...] = jnp.where(
        lax.broadcasted_iota(jnp.int32, stats.shape, 0) == 0, F32(MASK_FILL), F32(0.0)
    )
    acc[...] = jnp.zeros(acc.shape, F32)
    dq_cols[...] = jnp.zeros(dq_cols.shape, F32)
    for way, farthest in ((0, half), (1, half - 1)):
        ring_in[way, farthest] = jnp.zeros(ring_in.shape[2:], BF16)

    lane = lax.broadcasted_iota(jnp.int32, (TOK, HD), 1)
    first_half = lane < HD // 2
    cos = cosines[...]
    sin = sines[...]
    sin_turned = jnp.where(first_half, -sin, sin)

    def head_norm(tensor, gain):
        inv = lax.rsqrt(jnp.mean(tensor * tensor, axis=-1, keepdims=True) + NORM_EPS)
        hat = tensor * inv * gain
        return (hat * cos + pltpu.roll(hat, HD // 2, 1) * sin_turned).astype(BF16)

    def norm_back(tensor, gain, rot_grad):
        turned = pltpu.roll(rot_grad * sin, HD // 2, 1)
        hat_grad = rot_grad * cos + jnp.where(first_half, turned, -turned)
        inv = lax.rsqrt(jnp.mean(tensor * tensor, axis=-1, keepdims=True) + NORM_EPS)
        scaled = hat_grad * gain
        inner = jnp.mean(tensor * scaled, axis=-1, keepdims=True)
        return (inv * scaled - tensor * (inv * inv * inv) * inner).astype(BF16)

    def piece_of(piece, zz, xx=None):
        if xx is None:
            xx = x if piece < 2 else 1 - x
        start = (zz * 2 + xx) * TOK + piece % 2 * PIECE
        return kv.at[pl.ds(pl.multiple_of(start, PIECE), PIECE)]

    def place(way, step):
        return lax.rem(z + way * step + (1 - way) * (ring - step), ring)

    def gather_copy(way, step, piece, zz):
        ref = piece_of(piece, zz)
        sems = (gather_send.at[way, step, piece], gather_recv.at[way, step, piece])
        return copy(ref, ref, *sems, along(way))

    def relay_copy(way, step, zz, xx):
        ref = piece_of(3, zz, xx)
        return copy(ref, ref, relay_send.at[way, step], relay_recv.at[way, step], across)

    peer_heads = rows((1 - x) * 2 * TOK, 2 * TOK)
    own_heads = rows(x * 2 * TOK, 2 * TOK)
    own_rows = rows((x * 2 + c) * 2 * TOK, 2 * TOK)
    relay_rows = rows(((1 - x) * 2 + c) * 2 * TOK, 2 * TOK)

    def spread(number, src, dst):
        return (
            copy_once(number, src.at[peer_heads], dst.at[own_rows], across),
            copy_once(number + 1, src.at[own_heads], dst.at[own_rows], other_core),
            copy_once(number + 2, dst.at[relay_rows], dst.at[relay_rows], other_core),
        )

    q_copies = spread(Q_X, q_own, q_rows)
    do_copies = spread(DO_X, do_own, do_rows)

    def turn(src, dst):
        for block in range(src.shape[0] // TOK):
            span = slice(block * TOK, (block + 1) * TOK)
            dst[:, span] = src[span, :].T

    for load in loads[:3]:
        load.wait()
    codes_copy.wait_recv()

    @pl.when(sec == 0)
    def _():
        codes_in[...] = codes_edge[...]

    @pl.when(sec != 0)
    def _():
        codes_in[...] = codes_buf[...]

    wide = codes_in[...].astype(F32)
    inv_norm = lax.rsqrt(jnp.sum(wide * wide, axis=-1, keepdims=True) / D + NORM_EPS)
    normed = (wide * inv_norm).astype(BF16)
    key_lin = dot(normed, w_key[...])
    k_lin[...] = key_lin
    own = rows((z * 2 + x) * TOK)
    kv[own, :HD] = head_norm(key_lin, k_gain[...])
    kv[own, HD:] = dot(normed, w_value[...]).astype(BF16)

    first_piece = piece_of(0, z, x)
    for piece in (1, 0):
        for way in range(2):
            gather_copy(way, 1, piece, z).start()
    for way in range(2):
        sems = (gather_send.at[way, 1, 2], gather_recv.at[way, 1, 2])
        copy(first_piece, first_piece, *sems, diagonal(way)).start()
    kv_copy = copy_once(KV_X, first_piece, first_piece, across)
    kv_copy.start()
    relay_copy(0, 0, z, x).start()

    loads[3].wait()
    q_lin[...] = dot(normed, w_query[...])
    for head in range(4):
        q_own[head * TOK : (head + 1) * TOK, :] = head_norm(
            q_lin[:, head * HD : (head + 1) * HD], q_gain[...]
        )
    q_copies[0].start()
    q_copies[1].start()
    q_rows[own_rows, :] = q_own[own_heads, :]

    grads_copy.start()

    scale = HD ** (-0.5)
    scale_two = scale * LOG2_E
    all_cols = 8 * TOK
    late = 4 * TOK

    def own_mask(first_col):
        shape = (TOK, all_cols - first_col)
        key = lax.broadcasted_iota(jnp.int32, shape, 0) + c * TOK
        col = lax.broadcasted_iota(jnp.int32, shape, 1) + first_col
        query = (col & (TOK - 1)) + ((col & (2 * TOK)) >> 1)
        visible = key <= query
        if first_col == 0:
            visible = visible | (col >= late)
        return visible

    def forward_tile(kept, step, zz, xx, first_col, masked):
        span = slice(first_col, all_cols)
        block = rows((zz * 2 + xx) * TOK)
        scores = dot(kv[block, :HD], q_cols[:, span]) * scale_two
        if masked:
            scores = jnp.where(own_mask(first_col), scores, 2 * MASK_FILL)
        kept_scores[kept, step, rows(xx * TOK), span] = scores
        top_old = stats[0:1, span]
        top_new = jnp.maximum(top_old, jnp.max(scores, axis=0, keepdims=True))
        weights = jnp.exp2(scores - top_new)
        shrink = jnp.exp2(top_old - top_new)
        stats[1:2, span] = stats[1:2, span] * shrink + jnp.sum(weights, axis=0, keepdims=True)
        acc[:, span] = acc[:, span] * shrink + dot_first(kv[block, HD:], weights.astype(BF16))
        stats[0:1, span] = top_new

    def arrive(way, step, forward):
        zz = place(way, step)
        for piece in (1, 0, 2):
            gather_copy(way, step, piece, zz).wait_recv()

            @pl.when(forward)
            def _():
                gather_copy(way, step + 1, piece, zz).start()

            if piece == 1:
                relay_copy(way, step, zz, x).start()

    def gathered(item):
        return lax.rem(item + 1, 2), lax.div(item + 1, 2)

    def forward_block(item):
        way, step = gathered(item)
        zz = place(way, step)
        relay_copy(way, step, zz, 1 - x).wait_recv()
        kept = way + lax.div(step, half)

        @pl.when(zz < z)
        def _():
            forward_tile(kept, step, zz, 0, 0, False)
            forward_tile(kept, step, zz, 1, late, False)

        @pl.when(zz > z)
        def _():
            forward_tile(kept, step, zz, 0, late, False)

    def arrive_item(item):
        way, step = gathered(item)
        arrive(way, step, step < half - way)

    arrive_item(1)
    arrive_item(2)
    q_copies[0].wait_recv()
    q_copies[2].start()
    arrive_item(3)
    if ring > 4:
        arrive_item(4)
    q_copies[1].wait_recv()
    q_copies[2].wait_recv()
    turn(q_rows, q_cols)
    kv_copy.wait_recv()
    relay_copy(0, 0, z, 1 - x).wait_recv()
    forward_tile(0, 0, z, 0, 0, True)
    forward_tile(0, 0, z, 1, late, True)

    def forward_step(item, carry):
        @pl.when(item < ring)
        def _():
            arrive_item(item)

        forward_block(item - 4)

        @pl.when(item == 5 + ring // 4)
        def _():
            for load in loads[4:]:
                load.wait()
            grads_copy.wait_recv()

            @pl.when(sec == sections - 1)
            def _():
                grads_in[...] = grads_edge[...]

            @pl.when(sec != sections - 1)
            def _():
                grads_in[...] = grads_buf[...]

            grad_att = dot_last(grads_in[...], w_out[...]).astype(BF16)
            for head in range(4):
                do_own[head * TOK : (head + 1) * TOK, :] = grad_att[:, head * HD : (head + 1) * HD]
            do_copies[0].start()
            do_copies[1].start()
            do_rows[own_rows, :] = do_own[own_heads, :]

        @pl.when(item == 5 + ring // 2)
        def _():
            do_copies[0].wait_recv()
            do_copies[2].start()

        return carry

    lax.fori_loop(5, ring + 4, forward_step, 0)

    acc_copy = copy_once(ACC_C, acc, acc_peer, other_core)
    stats_copy = copy_once(STATS_C, stats, stats_peer, other_core)
    stats_copy.start()
    acc_copy.start()
    do_copies[1].wait_recv()
    do_copies[2].wait_recv()
    turn(do_rows, do_cols)
    stats_copy.wait_recv()
    top = jnp.maximum(stats[0:1, :], stats_peer[0:1, :])
    shrink = jnp.exp2(stats[0:1, :] - top)
    shrink_peer = jnp.exp2(stats_peer[0:1, :] - top)
    total = stats[1:2, :] * shrink + stats_peer[1:2, :] * shrink_peer
    lse[...] = top + jnp.log2(total)
    acc_copy.wait_recv()
    attended = (
        acc[...] * (shrink / total) + acc_peer[...] * (shrink_peer / total)
    ).astype(BF16)
    delta[...] = jnp.sum(
        do_cols[...].astype(F32) * attended.astype(F32), axis=0, keepdims=True
    )
    att_cols[...] = attended

    def backward_tile(way, step, zz, xx, first_col):
        span = slice(first_col, all_cols)
        block = rows((zz * 2 + xx) * TOK)
        out = rows(xx * TOK)
        probs = jnp.exp2(kept_scores[1 - way, step, out, span] - lse[:, span])
        grad_prob = dot(kv[block, HD:], do_cols[:, span])
        grad_score = (probs * (grad_prob - delta[:, span]) * scale).astype(BF16)
        part[way, step, out, HD:] = dot(probs.astype(BF16), do_rows[span, :])
        part[way, step, out, :HD] = dot(grad_score, q_rows[span, :])
        dq_cols[:, span] += dot_first(kv[block, :HD], grad_score)

    def leaving(item):
        return lax.rem(item, 2), half - lax.div(item + 1, 2)

    def own_part(way, step, piece):
        xx = x if piece < 2 else 1 - x
        return part[way, step, pl.ds(pl.multiple_of(xx * TOK + piece % 2 * PIECE, PIECE), PIECE), :]

    def cross_copy(way, step):
        return copy(
            cross_out.at[way, step],
            cross_in.at[way, step],
            cross_send.at[way, step],
            cross_recv.at[way, step],
            across,
        )

    def backward_block(item):
        way, step = leaving(item)
        zz = place(1 - way, step)

        @pl.when(zz <= z)
        def _():
            backward_tile(way, step, zz, 0, 0)
            backward_tile(way, step, zz, 1, late)

        @pl.when(zz > z)
        def _():
            backward_tile(way, step, zz, 0, late)
            part[way, step, TOK:, :] = jnp.zeros((TOK, 2 * HD), F32)

        cross_out[way, step] = own_part(way, step, 3).astype(BF16)
        cross_copy(way, step).start()

    def reduce_copy(way, step, piece, target=None):
        span = slice(piece * PIECE, (piece + 1) * PIECE)
        return copy(
            ring_out.at[way, step, span],
            ring_in.at[way, step - 1, span],
            reduce_send.at[way, step, piece],
            reduce_recv.at[way, step - 1, piece],
            along(way) if target is None else target,
        )

    def reduce_step(item, last=False):
        way, step = leaving(item)
        for piece in (0, 2, 1):

            @pl.when(step < half - way)
            def _():
                reduce_copy(way, step + 1, piece).wait_recv()

            span = slice(piece * PIECE, (piece + 1) * PIECE)
            summed = own_part(way, step, piece) + ring_in[way, step, span].astype(F32)
            if piece == 1:
                cross_copy(way, step).wait_recv()
                summed = summed + cross_in[way, step].astype(F32)
            ring_out[way, step, span] = summed.astype(BF16)
            target = diagonal(way) if last and piece == 2 else None
            reduce_copy(way, step, piece, target).start()

    def backward_step(pair, carry):
        backward_block(2 * pair)
        backward_block(2 * pair + 1)

        @pl.when(pair > 0)
        def _():
            reduce_step(pair - 1)

        return carry

    def reduce_only(item, carry):
        reduce_step(item)
        return carry

    lax.fori_loop(0, half, backward_step, 0)

    kv_send[...] = own_part(1, 0, 2).astype(BF16)
    dkv_copy = copy_once(DKV_X, kv_send, kv_peer, across)
    dkv_copy.start()
    turn_back = [(xx, head) for xx in range(2) for head in range(2)]
    for block in range(8):
        span = slice(block * TOK, (block + 1) * TOK)
        dq_rows[span, :] = dq_cols[:, span].T
    dq_core_copies = [
        copy_once(
            number,
            dq_rows.at[rows((xx * 2 + 1 - c) * 2 * TOK, 2 * TOK)],
            dq_core.at[rows(xx * 2 * TOK, 2 * TOK)],
            other_core,
        )
        for xx, number in enumerate((DQ_C0, DQ_C1))
    ]
    for number in range(2):
        dq_core_copies[number].start()
    reduce_step(half - 1, half - 1 >= ring - 3)

    def settle_gather(item, carry):
        way, step = gathered(item)
        relay_copy(way, step, z, x).wait_send()
        for piece in range(3):
            gather_copy(way, step, piece, z).wait_send()
        return carry

    def settle_reduce(item, carry):
        way, step = leaving(item)
        cross_copy(way, step).wait_send()

        @pl.when(step > 0)
        def _():
            for piece in range(3):
                reduce_copy(way, step, piece).wait_send()

        return carry

    lax.fori_loop(1, ring, settle_gather, 0)
    for number in range(2):
        dq_core_copies[number].wait_recv()
    dq_out[...] = dq_rows[relay_rows, :] + dq_core[peer_heads, :]
    dq_copy = copy_once(DQ_X, dq_out, dq_own.at[own_heads], across)
    dq_copy.start()
    dq_own[own_heads, :] = dq_rows[own_rows, :] + dq_core[own_heads, :]

    for xx, head in turn_back:
        cols = rows(((xx * 2 + c) * 2 + head) * TOK)
        att_rows[(xx * 2 + head) * TOK : (xx * 2 + head + 1) * TOK, :] = att_cols[:, cols].T
    att_copy = copy_once(ATT_X, att_rows.at[peer_heads], att_own.at[own_heads], across)
    att_copy.start()
    att_own[own_heads, :] = att_rows[own_heads, :]

    lax.fori_loop(half, ring - 3, reduce_only, 0)
    for item in range(max(half, ring - 3), ring - 1):
        reduce_step(item, True)
    lax.fori_loop(0, ring - 3, settle_reduce, 0)

    att_copy.wait_recv()
    result = codes_in[...].astype(F32)
    for head in range(4):
        span = slice(head * TOK, (head + 1) * TOK)
        result = result + dot(att_own[span, :], w_out[span, :])
    out_codes[...] = result.astype(BF16)

    dq_copy.wait_recv()
    normed_grad = jnp.zeros((TOK, w_query.shape[0]), F32)
    for head in range(4):
        span = slice(head * TOK, (head + 1) * TOK)
        lin_grad = norm_back(q_lin[:, span], q_gain[...], dq_own[span, :])
        normed_grad = normed_grad + dot_last(lin_grad, w_query[:, span])

    def ringed(piece):
        for way in range(2):
            reduce_copy(way, 1, piece).wait_recv()
        span = slice(piece * PIECE, (piece + 1) * PIECE)
        return ring_in[0, 0, span].astype(F32) + ring_in[1, 0, span].astype(F32)

    cross_copy(1, 0).wait_recv()
    dkv_copy.wait_recv()
    first_part = own_part(1, 0, 0) + kv_peer[...].astype(F32)
    second_part = own_part(1, 0, 1) + cross_in[1, 0].astype(F32)
    kv_grad[:PIECE, :] = first_part + ringed(0) + ringed(2)
    kv_grad[PIECE:, :] = second_part + ringed(1)
    key_grad = norm_back(k_lin[...], k_gain[...], kv_grad[:, :HD])
    normed_grad = normed_grad + dot_last(key_grad, w_key[...])
    normed_grad = normed_grad + dot_last(kv_grad[:, HD:].astype(BF16), w_value[...])
    wide = codes_in[...].astype(F32)
    inv_norm = lax.rsqrt(jnp.sum(wide * wide, axis=-1, keepdims=True) / D + NORM_EPS)
    inner = jnp.sum(wide * normed_grad, axis=-1, keepdims=True)
    in_grads[...] = (
        grads_in[...].astype(F32)
        + inv_norm * normed_grad
        - wide * (inv_norm * inv_norm * inv_norm) * inner / D
    ).astype(BF16)

    for once in (codes_copy, grads_copy, kv_copy, acc_copy, stats_copy, att_copy, dq_copy, dkv_copy):
        once.wait_send()
    for once in (*q_copies, *do_copies, *dq_core_copies):
        once.wait_send()

    relay_copy(0, 0, z, x).wait_send()
    lax.fori_loop(ring - 3, ring, settle_reduce, 0)


def rope_tables(positions, head_dim):
    half_dim = head_dim // 2
    exponent = jnp.arange(half_dim).astype(F32) * (2.0 / head_dim)
    frequency = jnp.power(F32(ROPE_BASE), -exponent)
    angles = positions.astype(F32)[:, None] * frequency[None, :]
    angles = jnp.concatenate([angles, angles], axis=-1)
    return (jnp.cos(angles), jnp.sin(angles))


def local(
    sent_codes, start_codes, sent_grads, loss_grads, w_query, w_key, w_value, w_out, q_gain, k_gain
):
    ring = lax.axis_size("seq") // 4
    sections = lax.axis_size("section")
    steps = ring // 2 + 1
    width = start_codes.shape[1]
    positions = lax.axis_index("seq") * TOK + jnp.arange(TOK, dtype=jnp.int32)
    cosines, sines = rope_tables(positions, HD)
    vmem = pltpu.VMEM
    dma = pltpu.SemaphoreType.DMA
    one_block = (TOK, width)
    heads = (4 * TOK, HD)
    all_rows = (8 * TOK, HD)
    columns = (HD, 8 * TOK)
    stat = (1, 8 * TOK)
    results = pl.pallas_call(
        functools.partial(kernel, ring, sections),
        out_shape=(jax.ShapeDtypeStruct(one_block, BF16),) * 2,
        in_specs=[pl.BlockSpec(memory_space=pltpu.HBM)] * 8 + [pl.BlockSpec(memory_space=vmem)] * 4,
        out_specs=(pl.BlockSpec(memory_space=vmem),) * 2,
        scratch_shapes=[
            vmem(w_query.shape[1:], BF16),
            vmem(w_key.shape[1:], BF16),
            vmem(w_value.shape[1:], BF16),
            vmem(w_out.shape[1:], BF16),
            vmem(one_block, BF16),
            vmem(one_block, BF16),
            vmem(one_block, BF16),
            vmem(one_block, BF16),
            vmem(one_block, BF16),
            vmem(one_block, BF16),
            vmem(one_block, F32),
            vmem((TOK, HD), F32),
            vmem(heads, BF16),
            vmem(all_rows, BF16),
            vmem(columns, BF16),
            vmem(heads, BF16),
            vmem(all_rows, BF16),
            vmem(columns, BF16),
            vmem((ring * 2 * TOK, 2 * HD), BF16),
            vmem((8, 8 * TOK), F32),
            vmem((8, 8 * TOK), F32),
            vmem(columns, F32),
            vmem(columns, F32),
            vmem(stat, F32),
            vmem(stat, F32),
            vmem(columns, BF16),
            vmem(heads, BF16),
            vmem(heads, BF16),
            vmem(columns, F32),
            vmem(all_rows, F32),
            vmem(heads, F32),
            vmem((2 * TOK, HD), F32),
            vmem(heads, F32),
            vmem((2, steps, 2 * TOK, 8 * TOK), F32),
            vmem((2, steps, 2 * TOK, 2 * HD), F32),
            vmem((2, steps, 3 * PIECE, 2 * HD), BF16),
            vmem((2, steps, 3 * PIECE, 2 * HD), BF16),
            vmem((2, steps, PIECE, 2 * HD), BF16),
            vmem((2, steps, PIECE, 2 * HD), BF16),
            vmem((TOK, 2 * HD), F32),
            vmem((PIECE, 2 * HD), BF16),
            vmem((PIECE, 2 * HD), BF16),
            dma((16,)),
            dma((16,)),
            dma((2, steps, 3)),
            dma((2, steps, 3)),
            dma((2, steps, 3)),
            dma((2, steps, 3)),
            dma((2, steps)),
            dma((2, steps)),
            dma((2, steps)),
            dma((2, steps)),
            dma((6,)),
        ],
        compiler_params=pltpu.CompilerParams(
            collective_id=0, has_side_effects=True, vmem_limit_bytes=60 * 1024 * 1024
        ),
    )(
        sent_codes[0],
        start_codes,
        sent_grads[0],
        loss_grads,
        w_query[0],
        w_key[0],
        w_value[0],
        w_out[0],
        q_gain,
        k_gain,
        cosines,
        sines,
    )
    return (results[0][None], results[1][None])


def solution(mesh):
    in_specs = (
        P("section", "seq", None),
        P("seq", None),
        P("section", "seq", None),
        P("seq", None),
        P("section", None, None),
        P("section", None, None),
        P("section", None, None),
        P("section", None, None),
        P("section", None),
        P("section", None),
    )
    out_specs = (P("section", "seq", None), P("section", "seq", None))
    return jax.shard_map(local, mesh=mesh, in_specs=in_specs, out_specs=out_specs, check_vma=False)
```

```python
import functools

import jax
import jax.numpy as jnp
from jax import lax
from jax.experimental import pallas as pl
from jax.experimental.pallas import tpu as pltpu
from jax.sharding import PartitionSpec as P

D = 5120
ROPE_BASE = 1000000.0
NORM_EPS = 1e-06
MASK_FILL = -1e30
LOG2_E = 1.4426950408889634
MESH = pl.DeviceIdType.MESH
F32 = jnp.float32
BF16 = jnp.bfloat16
TOK = 128
HD = 128
PIECE = 64
CONTRACT_LAST = (((1,), (1,)), ((), ()))
CONTRACT_FIRST = (((0,), (0,)), ((), ()))

CODES, GRADS, KV_X, ATT_X, DQ_X, DKV_X, ACC_C, STATS_C, DQ_C0, DQ_C1 = range(10)
Q_X, Q_C, Q_R, DO_X, DO_C, DO_R = range(10, 16)


def dot(a, b):
    return jnp.dot(a, b, preferred_element_type=F32)


def dot_last(a, b):
    return lax.dot_general(a, b, CONTRACT_LAST, preferred_element_type=F32)


def dot_first(a, b):
    return lax.dot_general(a, b, CONTRACT_FIRST, preferred_element_type=F32)


def rows(start, count=TOK):
    return pl.ds(pl.multiple_of(start, TOK), count)


def kernel(
    ring,
    sections,
    sent_codes,
    start_codes,
    sent_grads,
    loss_grads,
    w_query_hbm,
    w_key_hbm,
    w_value_hbm,
    w_out_hbm,
    q_gain,
    k_gain,
    cosines,
    sines,
    out_codes,
    in_grads,
    w_query,
    w_key,
    w_value,
    w_out,
    codes_edge,
    grads_edge,
    codes_buf,
    grads_buf,
    codes_in,
    grads_in,
    q_lin,
    k_lin,
    q_own,
    q_rows,
    q_cols,
    do_own,
    do_rows,
    do_cols,
    kv,
    stats,
    stats_peer,
    acc,
    acc_peer,
    lse,
    delta,
    att_cols,
    att_rows,
    att_own,
    dq_cols,
    dq_rows,
    dq_core,
    dq_out,
    dq_own,
    kept_weights,
    kept_tops,
    part,
    ring_out,
    ring_in,
    cross_out,
    cross_in,
    kv_grad,
    kv_send,
    kv_peer,
    once_send,
    once_recv,
    gather_send,
    gather_recv,
    reduce_send,
    reduce_recv,
    relay_send,
    relay_recv,
    cross_send,
    cross_recv,
    load_sems,
):
    half = ring // 2
    sec = lax.axis_index("section")
    me = lax.axis_index("seq")
    x = lax.div(me, 2 * ring)
    z = lax.rem(lax.div(me, 2), ring)
    c = lax.rem(me, 2)

    def device(xx, zz, cc):
        return (sec, (xx * ring + zz) * 2 + cc)

    def along(way):
        return device(x, lax.rem(z + 1 + way * (ring - 2), ring), c)

    def diagonal(way):
        return device(1 - x, lax.rem(z + 1 + way * (ring - 2), ring), c)

    other_core = device(x, z, 1 - c)
    across = device(1 - x, z, c)
    next_section = (lax.rem(sec + 1, sections), me)
    last_section = (lax.rem(sec + sections - 1, sections), me)

    def copy(src, dst, send, recv, target):
        return pltpu.make_async_remote_copy(
            src_ref=src,
            dst_ref=dst,
            send_sem=send,
            recv_sem=recv,
            device_id=target,
            device_id_type=MESH,
        )

    def copy_once(number, src, dst, target):
        return copy(src, dst, once_send.at[number], once_recv.at[number], target)

    loads = [
        pltpu.make_async_copy(src, dst, load_sems.at[number])
        for number, (src, dst) in enumerate(
            (
                (start_codes, codes_edge),
                (w_key_hbm, w_key),
                (w_value_hbm, w_value),
                (w_query_hbm, w_query),
                (loss_grads, grads_edge),
                (w_out_hbm, w_out),
            )
        )
    ]
    for load in loads:
        load.start()

    barrier = pltpu.get_barrier_semaphore()
    partners = (along(0), along(1), diagonal(0), diagonal(1), other_core, across)
    for partner in (*partners, next_section, last_section):
        pl.semaphore_signal(barrier, inc=1, device_id=partner, device_id_type=MESH)
    pl.semaphore_wait(barrier, 8)

    codes_copy = copy_once(CODES, sent_codes, codes_buf, next_section)
    grads_copy = copy_once(GRADS, sent_grads, grads_buf, last_section)
    codes_copy.start()

    stats[...] = jnp.where(
        lax.broadcasted_iota(jnp.int32, stats.shape, 0) == 0, F32(MASK_FILL), F32(0.0)
    )
    acc[...] = jnp.zeros(acc.shape, F32)
    dq_cols[...] = jnp.zeros(dq_cols.shape, F32)
    for way, farthest in ((0, half), (1, half - 1)):
        ring_in[way, farthest] = jnp.zeros(ring_in.shape[2:], BF16)

    lane = lax.broadcasted_iota(jnp.int32, (TOK, HD), 1)
    first_half = lane < HD // 2

    def unpack_table(packed):
        turned = pltpu.roll(packed, HD // 2, 1)
        left = first_half[: TOK // 2]
        return jnp.concatenate(
            [jnp.where(left, packed, turned), jnp.where(left, turned, packed)], axis=0
        )

    cos = unpack_table(cosines[...])
    sin = unpack_table(sines[...])
    sin_turned = jnp.where(first_half, -sin, sin)

    def head_norm(tensor, gain):
        inv = lax.rsqrt(jnp.mean(tensor * tensor, axis=-1, keepdims=True) + NORM_EPS)
        hat = tensor * inv * gain
        return (hat * cos + pltpu.roll(hat, HD // 2, 1) * sin_turned).astype(BF16)

    def norm_back(tensor, gain, rot_grad):
        turned = pltpu.roll(rot_grad * sin, HD // 2, 1)
        hat_grad = rot_grad * cos + jnp.where(first_half, turned, -turned)
        inv = lax.rsqrt(jnp.mean(tensor * tensor, axis=-1, keepdims=True) + NORM_EPS)
        scaled = hat_grad * gain
        inner = jnp.mean(tensor * scaled, axis=-1, keepdims=True)
        return (inv * scaled - tensor * (inv * inv * inv) * inner).astype(BF16)

    def piece_of(piece, zz, xx=None):
        if xx is None:
            xx = x if piece < 2 else 1 - x
        start = (zz * 2 + xx) * TOK + piece % 2 * PIECE
        return kv.at[pl.ds(pl.multiple_of(start, PIECE), PIECE)]

    def place(way, step):
        return lax.rem(z + way * step + (1 - way) * (ring - step), ring)

    def gather_copy(way, step, piece, zz):
        ref = piece_of(piece, zz)
        sems = (gather_send.at[way, step, piece], gather_recv.at[way, step, piece])
        return copy(ref, ref, *sems, along(way))

    def relay_copy(way, step, zz, xx):
        ref = piece_of(3, zz, xx)
        return copy(ref, ref, relay_send.at[way, step], relay_recv.at[way, step], across)

    peer_heads = rows((1 - x) * 2 * TOK, 2 * TOK)
    own_heads = rows(x * 2 * TOK, 2 * TOK)
    own_rows = rows((x * 2 + c) * 2 * TOK, 2 * TOK)
    relay_rows = rows(((1 - x) * 2 + c) * 2 * TOK, 2 * TOK)

    def spread(number, src, dst):
        return (
            copy_once(number, src.at[peer_heads], dst.at[own_rows], across),
            copy_once(number + 1, src.at[own_heads], dst.at[own_rows], other_core),
            copy_once(number + 2, dst.at[relay_rows], dst.at[relay_rows], other_core),
        )

    q_copies = spread(Q_X, q_own, q_rows)
    do_copies = spread(DO_X, do_own, do_rows)

    def turn(src, dst):
        for block in range(src.shape[0] // TOK):
            span = slice(block * TOK, (block + 1) * TOK)
            dst[:, span] = src[span, :].T

    for load in loads[:3]:
        load.wait()
    codes_copy.wait_recv()

    @pl.when(sec == 0)
    def _():
        codes_in[...] = codes_edge[...]

    @pl.when(sec != 0)
    def _():
        codes_in[...] = codes_buf[...]

    wide = codes_in[...].astype(F32)
    inv_norm = lax.rsqrt(jnp.sum(wide * wide, axis=-1, keepdims=True) / D + NORM_EPS)
    normed = (wide * inv_norm).astype(BF16)
    key_lin = dot(normed, w_key[...])
    k_lin[...] = key_lin
    own = rows((z * 2 + x) * TOK)
    kv[own, :HD] = head_norm(key_lin, k_gain[...])
    kv[own, HD:] = dot(normed, w_value[...]).astype(BF16)

    first_piece = piece_of(0, z, x)
    for piece in (1, 0):
        for way in range(2):
            gather_copy(way, 1, piece, z).start()
    for way in range(2):
        sems = (gather_send.at[way, 1, 2], gather_recv.at[way, 1, 2])
        copy(first_piece, first_piece, *sems, diagonal(way)).start()
    kv_copy = copy_once(KV_X, first_piece, first_piece, across)
    kv_copy.start()
    relay_copy(0, 0, z, x).start()

    loads[3].wait()
    q_lin[...] = dot(normed, w_query[...])
    for head in range(4):
        q_own[head * TOK : (head + 1) * TOK, :] = head_norm(
            q_lin[:, head * HD : (head + 1) * HD], q_gain[...]
        )
    q_copies[0].start()
    q_copies[1].start()
    q_rows[own_rows, :] = q_own[own_heads, :]

    grads_copy.start()

    scale = HD ** (-0.5)
    scale_two = scale * LOG2_E
    all_cols = 8 * TOK
    late = 4 * TOK

    def own_mask(first_col):
        shape = (TOK, all_cols - first_col)
        key = lax.broadcasted_iota(jnp.int32, shape, 0) + c * TOK
        col = lax.broadcasted_iota(jnp.int32, shape, 1) + first_col
        query = (col & (TOK - 1)) + ((col & (2 * TOK)) >> 1)
        visible = key <= query
        if first_col == 0:
            visible = visible | (col >= late)
        return visible

    def forward_tile(kept, step, zz, xx, first_col, masked):
        span = slice(first_col, all_cols)
        block = rows((zz * 2 + xx) * TOK)
        scores = dot(kv[block, :HD], q_cols[:, span]) * scale_two
        if masked:
            scores = jnp.where(own_mask(first_col), scores, 2 * MASK_FILL)
        top_old = stats[0:1, span]
        top_new = jnp.maximum(top_old, jnp.max(scores, axis=0, keepdims=True))
        weights = jnp.exp2(scores - top_new)
        kept_weights[kept, step, rows(xx * TOK), span] = weights
        kept_tops[kept, step, xx : xx + 1, span] = top_new
        shrink = jnp.exp2(top_old - top_new)
        stats[1:2, span] = stats[1:2, span] * shrink + jnp.sum(weights, axis=0, keepdims=True)
        acc[:, span] = acc[:, span] * shrink + dot_first(kv[block, HD:], weights.astype(BF16))
        stats[0:1, span] = top_new

    def arrive(way, step, forward):
        zz = place(way, step)
        for piece in (1, 0, 2):
            gather_copy(way, step, piece, zz).wait_recv()

            @pl.when(forward)
            def _():
                gather_copy(way, step + 1, piece, zz).start()

            if piece == 1:
                relay_copy(way, step, zz, x).start()

    def gathered(item):
        return lax.rem(item + 1, 2), lax.div(item + 1, 2)

    def forward_block(item):
        way, step = gathered(item)
        zz = place(way, step)
        relay_copy(way, step, zz, 1 - x).wait_recv()
        kept = way + lax.div(step, half)

        @pl.when(zz < z)
        def _():
            forward_tile(kept, step, zz, 0, 0, False)
            forward_tile(kept, step, zz, 1, late, False)

        @pl.when(zz > z)
        def _():
            forward_tile(kept, step, zz, 0, late, False)

    def arrive_item(item):
        way, step = gathered(item)
        arrive(way, step, step < half - way)

    arrive_item(1)
    arrive_item(2)
    q_copies[0].wait_recv()
    q_copies[2].start()
    arrive_item(3)
    if ring > 4:
        arrive_item(4)
    q_copies[1].wait_recv()
    q_copies[2].wait_recv()
    turn(q_rows, q_cols)
    kv_copy.wait_recv()
    relay_copy(0, 0, z, 1 - x).wait_recv()
    forward_tile(0, 0, z, 0, 0, True)
    forward_tile(0, 0, z, 1, late, True)

    def forward_step(item, carry):
        @pl.when(item < ring)
        def _():
            arrive_item(item)

        forward_block(item - 4)

        @pl.when(item == 5 + ring // 4)
        def _():
            for load in loads[4:]:
                load.wait()
            grads_copy.wait_recv()

            @pl.when(sec == sections - 1)
            def _():
                grads_in[...] = grads_edge[...]

            @pl.when(sec != sections - 1)
            def _():
                grads_in[...] = grads_buf[...]

            grad_att = dot_last(grads_in[...], w_out[...]).astype(BF16)
            for head in range(4):
                do_own[head * TOK : (head + 1) * TOK, :] = grad_att[:, head * HD : (head + 1) * HD]
            do_copies[0].start()
            do_copies[1].start()
            do_rows[own_rows, :] = do_own[own_heads, :]

        @pl.when(item == 5 + ring // 2)
        def _():
            do_copies[0].wait_recv()
            do_copies[2].start()

        return carry

    lax.fori_loop(5, ring + 4, forward_step, 0)

    acc_copy = copy_once(ACC_C, acc, acc_peer, other_core)
    stats_copy = copy_once(STATS_C, stats, stats_peer, other_core)
    stats_copy.start()
    acc_copy.start()
    do_copies[1].wait_recv()
    do_copies[2].wait_recv()
    turn(do_rows, do_cols)
    stats_copy.wait_recv()
    top = jnp.maximum(stats[0:1, :], stats_peer[0:1, :])
    shrink = jnp.exp2(stats[0:1, :] - top)
    shrink_peer = jnp.exp2(stats_peer[0:1, :] - top)
    total = stats[1:2, :] * shrink + stats_peer[1:2, :] * shrink_peer
    lse[...] = top + jnp.log2(total)
    acc_copy.wait_recv()
    attended = (
        acc[...] * (shrink / total) + acc_peer[...] * (shrink_peer / total)
    ).astype(BF16)
    delta[...] = jnp.sum(
        do_cols[...].astype(F32) * attended.astype(F32), axis=0, keepdims=True
    )
    att_cols[...] = attended

    def backward_tile(way, step, zz, xx, first_col):
        span = slice(first_col, all_cols)
        block = rows((zz * 2 + xx) * TOK)
        out = rows(xx * TOK)
        factor = jnp.exp2(kept_tops[1 - way, step, xx : xx + 1, span] - lse[:, span])
        probs = kept_weights[1 - way, step, out, span] * factor
        grad_prob = dot(kv[block, HD:], do_cols[:, span])
        grad_score = (probs * (grad_prob - delta[:, span]) * scale).astype(BF16)
        part[way, step, out, HD:] = dot(probs.astype(BF16), do_rows[span, :])
        part[way, step, out, :HD] = dot(grad_score, q_rows[span, :])
        dq_cols[:, span] += dot_first(kv[block, :HD], grad_score)

    def leaving(item):
        return lax.rem(item, 2), half - lax.div(item + 1, 2)

    def own_part(way, step, piece):
        xx = x if piece < 2 else 1 - x
        return part[way, step, pl.ds(pl.multiple_of(xx * TOK + piece % 2 * PIECE, PIECE), PIECE), :]

    def cross_copy(way, step):
        return copy(
            cross_out.at[way, step],
            cross_in.at[way, step],
            cross_send.at[way, step],
            cross_recv.at[way, step],
            across,
        )

    def backward_block(item):
        way, step = leaving(item)
        zz = place(1 - way, step)

        @pl.when(zz <= z)
        def _():
            backward_tile(way, step, zz, 0, 0)
            backward_tile(way, step, zz, 1, late)

        @pl.when(zz > z)
        def _():
            backward_tile(way, step, zz, 0, late)
            part[way, step, TOK:, :] = jnp.zeros((TOK, 2 * HD), F32)

        cross_out[way, step] = own_part(way, step, 3).astype(BF16)
        cross_copy(way, step).start()

    def reduce_copy(way, step, piece, target=None):
        span = slice(piece * PIECE, (piece + 1) * PIECE)
        return copy(
            ring_out.at[way, step, span],
            ring_in.at[way, step - 1, span],
            reduce_send.at[way, step, piece],
            reduce_recv.at[way, step - 1, piece],
            along(way) if target is None else target,
        )

    def reduce_step(item, last=False):
        way, step = leaving(item)
        for piece in (0, 2, 1):

            @pl.when(step < half - way)
            def _():
                reduce_copy(way, step + 1, piece).wait_recv()

            span = slice(piece * PIECE, (piece + 1) * PIECE)
            summed = own_part(way, step, piece) + ring_in[way, step, span].astype(F32)
            if piece == 1:
                cross_copy(way, step).wait_recv()
                summed = summed + cross_in[way, step].astype(F32)
            ring_out[way, step, span] = summed.astype(BF16)
            target = diagonal(way) if last and piece == 2 else None
            reduce_copy(way, step, piece, target).start()

    def backward_step(count, carry):
        block = 2 + 3 * count
        backward_block(block)
        reduce_step(2 * count)
        backward_block(block + 1)
        reduce_step(2 * count + 1)
        backward_block(block + 2)
        return carry

    def reduce_only(item, carry):
        reduce_step(item)
        return carry

    rounds = (ring - 4) // 3
    reduced = 2 * rounds
    backward_block(0)
    backward_block(1)
    lax.fori_loop(0, rounds, backward_step, 0)
    backward_block(ring - 2)
    reduce_step(reduced)
    backward_block(ring - 1)

    kv_send[...] = own_part(1, 0, 2).astype(BF16)
    dkv_copy = copy_once(DKV_X, kv_send, kv_peer, across)
    dkv_copy.start()
    turn_back = [(xx, head) for xx in range(2) for head in range(2)]
    for block in range(8):
        span = slice(block * TOK, (block + 1) * TOK)
        dq_rows[span, :] = dq_cols[:, span].T
    dq_core_copies = [
        copy_once(
            number,
            dq_rows.at[rows((xx * 2 + 1 - c) * 2 * TOK, 2 * TOK)],
            dq_core.at[rows(xx * 2 * TOK, 2 * TOK)],
            other_core,
        )
        for xx, number in enumerate((DQ_C0, DQ_C1))
    ]
    for number in range(2):
        dq_core_copies[number].start()
    reduce_step(reduced + 1, reduced + 1 >= ring - 3)

    def settle_gather(item, carry):
        way, step = gathered(item)
        relay_copy(way, step, z, x).wait_send()
        for piece in range(3):
            gather_copy(way, step, piece, z).wait_send()
        return carry

    def settle_reduce(item, carry):
        way, step = leaving(item)
        cross_copy(way, step).wait_send()

        @pl.when(step > 0)
        def _():
            for piece in range(3):
                reduce_copy(way, step, piece).wait_send()

        return carry

    lax.fori_loop(1, ring, settle_gather, 0)
    for number in range(2):
        dq_core_copies[number].wait_recv()
    dq_out[...] = dq_rows[relay_rows, :] + dq_core[peer_heads, :]
    dq_copy = copy_once(DQ_X, dq_out, dq_own.at[own_heads], across)
    dq_copy.start()
    dq_own[own_heads, :] = dq_rows[own_rows, :] + dq_core[own_heads, :]

    for xx, head in turn_back:
        cols = rows(((xx * 2 + c) * 2 + head) * TOK)
        att_rows[(xx * 2 + head) * TOK : (xx * 2 + head + 1) * TOK, :] = att_cols[:, cols].T
    att_copy = copy_once(ATT_X, att_rows.at[peer_heads], att_own.at[own_heads], across)
    att_copy.start()
    att_own[own_heads, :] = att_rows[own_heads, :]

    lax.fori_loop(reduced + 2, ring - 3, reduce_only, 0)
    for item in range(max(reduced + 2, ring - 3), ring - 1):
        reduce_step(item, True)
    lax.fori_loop(0, ring - 3, settle_reduce, 0)

    att_copy.wait_recv()
    result = codes_in[...].astype(F32)
    for head in range(4):
        span = slice(head * TOK, (head + 1) * TOK)
        result = result + dot(att_own[span, :], w_out[span, :])
    out_codes[...] = result.astype(BF16)

    dq_copy.wait_recv()
    normed_grad = jnp.zeros((TOK, w_query.shape[0]), F32)
    for head in range(4):
        span = slice(head * TOK, (head + 1) * TOK)
        lin_grad = norm_back(q_lin[:, span], q_gain[...], dq_own[span, :])
        normed_grad = normed_grad + dot_last(lin_grad, w_query[:, span])

    def ringed(piece):
        for way in range(2):
            reduce_copy(way, 1, piece).wait_recv()
        span = slice(piece * PIECE, (piece + 1) * PIECE)
        return ring_in[0, 0, span].astype(F32) + ring_in[1, 0, span].astype(F32)

    cross_copy(1, 0).wait_recv()
    dkv_copy.wait_recv()
    first_part = own_part(1, 0, 0) + kv_peer[...].astype(F32)
    second_part = own_part(1, 0, 1) + cross_in[1, 0].astype(F32)
    kv_grad[:PIECE, :] = first_part + ringed(0) + ringed(2)
    kv_grad[PIECE:, :] = second_part + ringed(1)
    key_grad = norm_back(k_lin[...], k_gain[...], kv_grad[:, :HD])
    normed_grad = normed_grad + dot_last(key_grad, w_key[...])
    normed_grad = normed_grad + dot_last(kv_grad[:, HD:].astype(BF16), w_value[...])
    wide = codes_in[...].astype(F32)
    inv_norm = lax.rsqrt(jnp.sum(wide * wide, axis=-1, keepdims=True) / D + NORM_EPS)
    inner = jnp.sum(wide * normed_grad, axis=-1, keepdims=True)
    in_grads[...] = (
        grads_in[...].astype(F32)
        + inv_norm * normed_grad
        - wide * (inv_norm * inv_norm * inv_norm) * inner / D
    ).astype(BF16)

    for once in (codes_copy, grads_copy, kv_copy, acc_copy, stats_copy, att_copy, dq_copy, dkv_copy):
        once.wait_send()
    for once in (*q_copies, *do_copies, *dq_core_copies):
        once.wait_send()

    relay_copy(0, 0, z, x).wait_send()
    lax.fori_loop(ring - 3, ring, settle_reduce, 0)


def rope_tables(first_pos):
    half_dim = HD // 2
    exponent = jnp.arange(half_dim).astype(F32) * (2.0 / HD)
    frequency = jnp.power(F32(ROPE_BASE), -exponent)
    frequency = jnp.concatenate([frequency, frequency])
    shape = (TOK // 2, HD)
    lane = lax.broadcasted_iota(jnp.int32, shape, 1)
    offset = lax.broadcasted_iota(jnp.int32, shape, 0) + jnp.where(lane < half_dim, 0, TOK // 2)
    angles = (first_pos + offset).astype(F32) * frequency[None, :]
    return (jnp.cos(angles), jnp.sin(angles))


def local(
    sent_codes, start_codes, sent_grads, loss_grads, w_query, w_key, w_value, w_out, q_gain, k_gain
):
    ring = lax.axis_size("seq") // 4
    sections = lax.axis_size("section")
    steps = ring // 2 + 1
    width = start_codes.shape[1]
    cosines, sines = rope_tables(lax.axis_index("seq") * TOK)
    vmem = pltpu.VMEM
    dma = pltpu.SemaphoreType.DMA
    one_block = (TOK, width)
    heads = (4 * TOK, HD)
    all_rows = (8 * TOK, HD)
    columns = (HD, 8 * TOK)
    stat = (1, 8 * TOK)
    results = pl.pallas_call(
        functools.partial(kernel, ring, sections),
        out_shape=(jax.ShapeDtypeStruct(one_block, BF16),) * 2,
        in_specs=[pl.BlockSpec(memory_space=pltpu.HBM)] * 8 + [pl.BlockSpec(memory_space=vmem)] * 4,
        out_specs=(pl.BlockSpec(memory_space=vmem),) * 2,
        scratch_shapes=[
            vmem(w_query.shape[1:], BF16),
            vmem(w_key.shape[1:], BF16),
            vmem(w_value.shape[1:], BF16),
            vmem(w_out.shape[1:], BF16),
            vmem(one_block, BF16),
            vmem(one_block, BF16),
            vmem(one_block, BF16),
            vmem(one_block, BF16),
            vmem(one_block, BF16),
            vmem(one_block, BF16),
            vmem(one_block, F32),
            vmem((TOK, HD), F32),
            vmem(heads, BF16),
            vmem(all_rows, BF16),
            vmem(columns, BF16),
            vmem(heads, BF16),
            vmem(all_rows, BF16),
            vmem(columns, BF16),
            vmem((ring * 2 * TOK, 2 * HD), BF16),
            vmem((8, 8 * TOK), F32),
            vmem((8, 8 * TOK), F32),
            vmem(columns, F32),
            vmem(columns, F32),
            vmem(stat, F32),
            vmem(stat, F32),
            vmem(columns, BF16),
            vmem(heads, BF16),
            vmem(heads, BF16),
            vmem(columns, F32),
            vmem(all_rows, F32),
            vmem(heads, F32),
            vmem((2 * TOK, HD), F32),
            vmem(heads, F32),
            vmem((2, steps, 2 * TOK, 8 * TOK), F32),
            vmem((2, steps, 8, 8 * TOK), F32),
            vmem((2, steps, 2 * TOK, 2 * HD), F32),
            vmem((2, steps, 3 * PIECE, 2 * HD), BF16),
            vmem((2, steps, 3 * PIECE, 2 * HD), BF16),
            vmem((2, steps, PIECE, 2 * HD), BF16),
            vmem((2, steps, PIECE, 2 * HD), BF16),
            vmem((TOK, 2 * HD), F32),
            vmem((PIECE, 2 * HD), BF16),
            vmem((PIECE, 2 * HD), BF16),
            dma((16,)),
            dma((16,)),
            dma((2, steps, 3)),
            dma((2, steps, 3)),
            dma((2, steps, 3)),
            dma((2, steps, 3)),
            dma((2, steps)),
            dma((2, steps)),
            dma((2, steps)),
            dma((2, steps)),
            dma((6,)),
        ],
        compiler_params=pltpu.CompilerParams(
            collective_id=0, has_side_effects=True, vmem_limit_bytes=60 * 1024 * 1024
        ),
    )(
        sent_codes[0],
        start_codes,
        sent_grads[0],
        loss_grads,
        w_query[0],
        w_key[0],
        w_value[0],
        w_out[0],
        q_gain,
        k_gain,
        cosines,
        sines,
    )
    return (results[0][None], results[1][None])


def solution(mesh):
    in_specs = (
        P("section", "seq", None),
        P("seq", None),
        P("section", "seq", None),
        P("seq", None),
        P("section", None, None),
        P("section", None, None),
        P("section", None, None),
        P("section", None, None),
        P("section", None),
        P("section", None),
    )
    out_specs = (P("section", "seq", None), P("section", "seq", None))
    return jax.shard_map(local, mesh=mesh, in_specs=in_specs, out_specs=out_specs, check_vma=False)
```

```python
import functools

import jax
import jax.numpy as jnp
from jax import lax
from jax.experimental import pallas as pl
from jax.experimental.pallas import tpu as pltpu
from jax.sharding import PartitionSpec as P

D = 5120
ROPE_BASE = 1000000.0
NORM_EPS = 1e-06
MASK_FILL = -1e30
LOG2_E = 1.4426950408889634
MESH = pl.DeviceIdType.MESH
F32 = jnp.float32
BF16 = jnp.bfloat16
TOK = 128
HD = 128
PIECE = 64
CONTRACT_LAST = (((1,), (1,)), ((), ()))
CONTRACT_FIRST = (((0,), (0,)), ((), ()))

CODES, GRADS, KV_X, ATT_X, DQ_X, DKV_X, ACC_C, STATS_C, DQ_C0, DQ_C1 = range(10)
Q_X, Q_C, Q_R, DO_X, DO_C, DO_R = range(10, 16)


def dot(a, b):
    return jnp.dot(a, b, preferred_element_type=F32)


def dot_last(a, b):
    return lax.dot_general(a, b, CONTRACT_LAST, preferred_element_type=F32)


def dot_first(a, b):
    return lax.dot_general(a, b, CONTRACT_FIRST, preferred_element_type=F32)


def rows(start, count=TOK):
    return pl.ds(pl.multiple_of(start, TOK), count)


def kernel(
    ring,
    sections,
    sent_codes,
    start_codes,
    sent_grads,
    loss_grads,
    w_query_hbm,
    w_key_hbm,
    w_value_hbm,
    w_out_hbm,
    q_gain,
    k_gain,
    cosines,
    sines,
    out_codes,
    in_grads,
    w_query,
    w_key,
    w_value,
    w_out,
    codes_edge,
    grads_edge,
    codes_buf,
    grads_buf,
    codes_in,
    grads_in,
    q_lin,
    k_lin,
    q_own,
    q_rows,
    q_cols,
    do_own,
    do_rows,
    do_cols,
    kv,
    stats,
    stats_peer,
    acc,
    acc_peer,
    lse,
    delta,
    att_cols,
    att_rows,
    att_own,
    dq_cols,
    dq_rows,
    dq_core,
    dq_out,
    dq_own,
    kept_weights,
    kept_tops,
    part,
    ring_out,
    ring_in,
    cross_out,
    cross_in,
    kv_grad,
    kv_send,
    kv_peer,
    once_send,
    once_recv,
    gather_send,
    gather_recv,
    reduce_send,
    reduce_recv,
    relay_send,
    relay_recv,
    cross_send,
    cross_recv,
    load_sems,
):
    half = ring // 2
    sec = lax.axis_index("section")
    me = lax.axis_index("seq")
    x = lax.div(me, 2 * ring)
    z = lax.rem(lax.div(me, 2), ring)
    c = lax.rem(me, 2)

    def device(xx, zz, cc):
        return (sec, (xx * ring + zz) * 2 + cc)

    def along(way):
        return device(x, lax.rem(z + 1 + way * (ring - 2), ring), c)

    def diagonal(way):
        return device(1 - x, lax.rem(z + 1 + way * (ring - 2), ring), c)

    other_core = device(x, z, 1 - c)
    across = device(1 - x, z, c)
    next_section = (lax.rem(sec + 1, sections), me)
    last_section = (lax.rem(sec + sections - 1, sections), me)

    def copy(src, dst, send, recv, target):
        return pltpu.make_async_remote_copy(
            src_ref=src,
            dst_ref=dst,
            send_sem=send,
            recv_sem=recv,
            device_id=target,
            device_id_type=MESH,
        )

    def copy_once(number, src, dst, target):
        return copy(src, dst, once_send.at[number], once_recv.at[number], target)

    loads = [
        pltpu.make_async_copy(src, dst, load_sems.at[number])
        for number, (src, dst) in enumerate(
            (
                (start_codes, codes_edge),
                (w_key_hbm, w_key),
                (w_value_hbm, w_value),
                (w_query_hbm, w_query),
                (loss_grads, grads_edge),
                (w_out_hbm, w_out),
            )
        )
    ]
    for load in loads:
        load.start()

    barrier = pltpu.get_barrier_semaphore()
    partners = (along(0), along(1), diagonal(0), diagonal(1), other_core, across)
    for partner in (*partners, next_section, last_section):
        pl.semaphore_signal(barrier, inc=1, device_id=partner, device_id_type=MESH)
    pl.semaphore_wait(barrier, 8)

    codes_copy = copy_once(CODES, sent_codes, codes_buf, next_section)
    grads_copy = copy_once(GRADS, sent_grads, grads_buf, last_section)
    codes_copy.start()

    stats[...] = jnp.where(
        lax.broadcasted_iota(jnp.int32, stats.shape, 0) == 0, F32(MASK_FILL), F32(0.0)
    )
    acc[...] = jnp.zeros(acc.shape, F32)
    dq_cols[...] = jnp.zeros(dq_cols.shape, F32)
    for way, farthest in ((0, half), (1, half - 1)):
        ring_in[way, farthest] = jnp.zeros(ring_in.shape[2:], BF16)

    lane = lax.broadcasted_iota(jnp.int32, (TOK, HD), 1)
    first_half = lane < HD // 2

    def unpack_table(packed):
        turned = pltpu.roll(packed, HD // 2, 1)
        left = first_half[: TOK // 2]
        return jnp.concatenate(
            [jnp.where(left, packed, turned), jnp.where(left, turned, packed)], axis=0
        )

    cos = unpack_table(cosines[...])
    sin = unpack_table(sines[...])
    sin_turned = jnp.where(first_half, -sin, sin)

    def head_norm(tensor, gain):
        inv = lax.rsqrt(jnp.mean(tensor * tensor, axis=-1, keepdims=True) + NORM_EPS)
        hat = tensor * inv * gain
        return (hat * cos + pltpu.roll(hat, HD // 2, 1) * sin_turned).astype(BF16)

    def norm_back(tensor, gain, rot_grad):
        turned = pltpu.roll(rot_grad * sin, HD // 2, 1)
        hat_grad = rot_grad * cos + jnp.where(first_half, turned, -turned)
        inv = lax.rsqrt(jnp.mean(tensor * tensor, axis=-1, keepdims=True) + NORM_EPS)
        scaled = hat_grad * gain
        inner = jnp.mean(tensor * scaled, axis=-1, keepdims=True)
        return (inv * scaled - tensor * (inv * inv * inv) * inner).astype(BF16)

    def piece_of(piece, zz, xx=None):
        if xx is None:
            xx = x if piece < 2 else 1 - x
        start = (zz * 2 + xx) * TOK + piece % 2 * PIECE
        return kv.at[pl.ds(pl.multiple_of(start, PIECE), PIECE)]

    def place(way, step):
        return lax.rem(z + way * step + (1 - way) * (ring - step), ring)

    def gather_copy(way, step, piece, zz):
        ref = piece_of(piece, zz)
        sems = (gather_send.at[way, step, piece], gather_recv.at[way, step, piece])
        return copy(ref, ref, *sems, along(way))

    def relay_copy(way, step, zz, xx):
        ref = piece_of(3, zz, xx)
        return copy(ref, ref, relay_send.at[way, step], relay_recv.at[way, step], across)

    peer_heads = rows((1 - x) * 2 * TOK, 2 * TOK)
    own_heads = rows(x * 2 * TOK, 2 * TOK)
    own_rows = rows((x * 2 + c) * 2 * TOK, 2 * TOK)
    relay_rows = rows(((1 - x) * 2 + c) * 2 * TOK, 2 * TOK)

    def spread(number, src, dst):
        return (
            copy_once(number, src.at[peer_heads], dst.at[own_rows], across),
            copy_once(number + 1, src.at[own_heads], dst.at[own_rows], other_core),
            copy_once(number + 2, dst.at[relay_rows], dst.at[relay_rows], other_core),
        )

    q_copies = spread(Q_X, q_own, q_rows)
    do_copies = spread(DO_X, do_own, do_rows)

    def turn(src, dst):
        for block in range(src.shape[0] // TOK):
            span = slice(block * TOK, (block + 1) * TOK)
            dst[:, span] = src[span, :].T

    for load in loads[:3]:
        load.wait()
    codes_copy.wait_recv()

    @pl.when(sec == 0)
    def _():
        codes_in[...] = codes_edge[...]

    @pl.when(sec != 0)
    def _():
        codes_in[...] = codes_buf[...]

    wide = codes_in[...].astype(F32)
    inv_norm = lax.rsqrt(jnp.sum(wide * wide, axis=-1, keepdims=True) / D + NORM_EPS)
    normed = (wide * inv_norm).astype(BF16)
    key_lin = dot(normed, w_key[...])
    k_lin[...] = key_lin
    own = rows((z * 2 + x) * TOK)
    kv[own, :HD] = head_norm(key_lin, k_gain[...])
    kv[own, HD:] = dot(normed, w_value[...]).astype(BF16)

    first_piece = piece_of(0, z, x)
    for piece in (1, 0):
        for way in range(2):
            gather_copy(way, 1, piece, z).start()
    for way in range(2):
        sems = (gather_send.at[way, 1, 2], gather_recv.at[way, 1, 2])
        copy(first_piece, first_piece, *sems, diagonal(way)).start()
    kv_copy = copy_once(KV_X, first_piece, first_piece, across)
    kv_copy.start()
    relay_copy(0, 0, z, x).start()

    loads[3].wait()
    q_lin[...] = dot(normed, w_query[...])
    for head in range(4):
        q_own[head * TOK : (head + 1) * TOK, :] = head_norm(
            q_lin[:, head * HD : (head + 1) * HD], q_gain[...]
        )
    q_copies[0].start()
    q_copies[1].start()
    q_rows[own_rows, :] = q_own[own_heads, :]

    grads_copy.start()

    scale = HD ** (-0.5)
    scale_two = scale * LOG2_E
    late = 4 * TOK

    def tile_cols(half_of):
        return slice(half_of * late, (half_of + 1) * late)

    def own_mask(half_of, keys):
        shape = (keys, late)
        key = lax.broadcasted_iota(jnp.int32, shape, 0)
        col = lax.broadcasted_iota(jnp.int32, shape, 1)
        query = (col & (TOK - 1)) + ((col & (2 * TOK)) >> 1)
        if half_of == 0:
            return key + c * TOK <= query
        return (key < TOK) | (key - TOK + c * TOK <= query)

    def forward_tile(kept, step, zz, half_of, keys, masked):
        span = tile_cols(half_of)
        block = rows(zz * 2 * TOK, keys)
        scores = dot(kv[block, :HD], q_cols[:, span]) * scale_two
        if masked:
            scores = jnp.where(own_mask(half_of, keys), scores, 2 * MASK_FILL)
        top_old = stats[0:1, span]
        top_new = jnp.maximum(top_old, jnp.max(scores, axis=0, keepdims=True))
        weights = jnp.exp2(scores - top_new)
        kept_weights[kept, step, :keys, span] = weights
        kept_tops[kept, step, half_of : half_of + 1, span] = top_new
        shrink = jnp.exp2(top_old - top_new)
        stats[1:2, span] = stats[1:2, span] * shrink + jnp.sum(weights, axis=0, keepdims=True)
        acc[:, span] = acc[:, span] * shrink + dot_first(kv[block, HD:], weights.astype(BF16))
        stats[0:1, span] = top_new

    def arrive(way, step, forward):
        zz = place(way, step)
        for piece in (1, 0, 2):
            gather_copy(way, step, piece, zz).wait_recv()

            @pl.when(forward)
            def _():
                gather_copy(way, step + 1, piece, zz).start()

            if piece == 1:
                relay_copy(way, step, zz, x).start()

    def gathered(item):
        return lax.rem(item + 1, 2), lax.div(item + 1, 2)

    def forward_block(item):
        way, step = gathered(item)
        zz = place(way, step)
        relay_copy(way, step, zz, 1 - x).wait_recv()
        kept = way + lax.div(step, half)

        @pl.when(zz < z)
        def _():
            forward_tile(kept, step, zz, 1, 2 * TOK, False)
            forward_tile(kept, step, zz, 0, TOK, False)

        @pl.when(zz > z)
        def _():
            forward_tile(kept, step, zz, 1, TOK, False)

    def arrive_item(item):
        way, step = gathered(item)
        arrive(way, step, step < half - way)

    arrive_item(1)
    arrive_item(2)
    q_copies[0].wait_recv()
    q_copies[2].start()
    arrive_item(3)
    if ring > 4:
        arrive_item(4)
    q_copies[1].wait_recv()
    q_copies[2].wait_recv()
    turn(q_rows, q_cols)
    kv_copy.wait_recv()
    relay_copy(0, 0, z, 1 - x).wait_recv()
    forward_tile(0, 0, z, 1, 2 * TOK, True)
    forward_tile(0, 0, z, 0, TOK, True)

    catches = (5 + ring // 4, 4 + ring // 2) if ring >= 16 else ()

    def caught_up(item):
        return sum(jnp.where(item >= catch, 1, 0) for catch in catches)

    def forward_step(item, carry):
        @pl.when(item < ring)
        def _():
            arrive_item(item)

        forward_block(item - 4 + caught_up(item - 1))

        if catches:

            @pl.when(caught_up(item) > caught_up(item - 1))
            def _():
                forward_block(item - 3 + caught_up(item - 1))

        @pl.when(item == 5 + ring // 4)
        def _():
            for load in loads[4:]:
                load.wait()
            grads_copy.wait_recv()

            @pl.when(sec == sections - 1)
            def _():
                grads_in[...] = grads_edge[...]

            @pl.when(sec != sections - 1)
            def _():
                grads_in[...] = grads_buf[...]

            grad_att = dot_last(grads_in[...], w_out[...]).astype(BF16)
            for head in range(4):
                do_own[head * TOK : (head + 1) * TOK, :] = grad_att[:, head * HD : (head + 1) * HD]
            do_copies[0].start()
            do_copies[1].start()
            do_rows[own_rows, :] = do_own[own_heads, :]

        @pl.when(item == 5 + ring // 2)
        def _():
            do_copies[0].wait_recv()
            do_copies[2].start()

        return carry

    lax.fori_loop(5, ring + 4 - len(catches), forward_step, 0)

    acc_copy = copy_once(ACC_C, acc, acc_peer, other_core)
    stats_copy = copy_once(STATS_C, stats, stats_peer, other_core)
    stats_copy.start()
    acc_copy.start()
    do_copies[1].wait_recv()
    do_copies[2].wait_recv()
    turn(do_rows, do_cols)
    stats_copy.wait_recv()
    top = jnp.maximum(stats[0:1, :], stats_peer[0:1, :])
    shrink = jnp.exp2(stats[0:1, :] - top)
    shrink_peer = jnp.exp2(stats_peer[0:1, :] - top)
    total = stats[1:2, :] * shrink + stats_peer[1:2, :] * shrink_peer
    lse[...] = top + jnp.log2(total)
    acc_copy.wait_recv()
    attended = (
        acc[...] * (shrink / total) + acc_peer[...] * (shrink_peer / total)
    ).astype(BF16)
    delta[...] = jnp.sum(
        do_cols[...].astype(F32) * attended.astype(F32), axis=0, keepdims=True
    )
    att_cols[...] = attended

    def backward_tile(way, step, zz, half_of, keys):
        span = tile_cols(half_of)
        block = rows(zz * 2 * TOK, keys)
        factor = jnp.exp2(kept_tops[1 - way, step, half_of : half_of + 1, span] - lse[:, span])
        probs = kept_weights[1 - way, step, :keys, span] * factor
        grad_prob = dot(kv[block, HD:], do_cols[:, span])
        grad_score = (probs * (grad_prob - delta[:, span]) * scale).astype(BF16)
        value_grad = dot(probs.astype(BF16), do_rows[span, :])
        key_grad = dot(grad_score, q_rows[span, :])
        if half_of == 1:
            part[way, step, :keys, HD:] = value_grad
            part[way, step, :keys, :HD] = key_grad
        else:
            part[way, step, :keys, HD:] += value_grad
            part[way, step, :keys, :HD] += key_grad
        dq_cols[:, span] += dot_first(kv[block, :HD], grad_score)

    def leaving(item):
        return lax.rem(item, 2), half - lax.div(item + 1, 2)

    def own_part(way, step, piece):
        xx = x if piece < 2 else 1 - x
        return part[way, step, pl.ds(pl.multiple_of(xx * TOK + piece % 2 * PIECE, PIECE), PIECE), :]

    def cross_copy(way, step):
        return copy(
            cross_out.at[way, step],
            cross_in.at[way, step],
            cross_send.at[way, step],
            cross_recv.at[way, step],
            across,
        )

    def backward_block(item):
        way, step = leaving(item)
        zz = place(1 - way, step)

        @pl.when(zz <= z)
        def _():
            backward_tile(way, step, zz, 1, 2 * TOK)
            backward_tile(way, step, zz, 0, TOK)

        @pl.when(zz > z)
        def _():
            backward_tile(way, step, zz, 1, TOK)
            part[way, step, TOK:, :] = jnp.zeros((TOK, 2 * HD), F32)

        cross_out[way, step] = own_part(way, step, 3).astype(BF16)
        cross_copy(way, step).start()

    def reduce_copy(way, step, piece, target=None):
        span = slice(piece * PIECE, (piece + 1) * PIECE)
        return copy(
            ring_out.at[way, step, span],
            ring_in.at[way, step - 1, span],
            reduce_send.at[way, step, piece],
            reduce_recv.at[way, step - 1, piece],
            along(way) if target is None else target,
        )

    def reduce_step(item, last=False):
        way, step = leaving(item)
        for piece in (0, 2, 1):

            @pl.when(step < half - way)
            def _():
                reduce_copy(way, step + 1, piece).wait_recv()

            span = slice(piece * PIECE, (piece + 1) * PIECE)
            summed = own_part(way, step, piece) + ring_in[way, step, span].astype(F32)
            if piece == 1:
                cross_copy(way, step).wait_recv()
                summed = summed + cross_in[way, step].astype(F32)
            ring_out[way, step, span] = summed.astype(BF16)
            target = diagonal(way) if last and piece == 2 else None
            reduce_copy(way, step, piece, target).start()

    def backward_step(count, carry):
        block = 2 + 3 * count
        backward_block(block)
        reduce_step(2 * count)
        backward_block(block + 1)
        reduce_step(2 * count + 1)
        backward_block(block + 2)
        return carry

    def reduce_only(item, carry):
        reduce_step(item)
        return carry

    rounds = (ring - 4) // 3
    reduced = 2 * rounds
    backward_block(0)
    backward_block(1)
    lax.fori_loop(0, rounds, backward_step, 0)
    backward_block(ring - 2)
    reduce_step(reduced)
    backward_block(ring - 1)

    kv_send[...] = own_part(1, 0, 2).astype(BF16)
    dkv_copy = copy_once(DKV_X, kv_send, kv_peer, across)
    dkv_copy.start()
    turn_back = [(xx, head) for xx in range(2) for head in range(2)]
    for block in range(8):
        span = slice(block * TOK, (block + 1) * TOK)
        dq_rows[span, :] = dq_cols[:, span].T
    dq_core_copies = [
        copy_once(
            number,
            dq_rows.at[rows((xx * 2 + 1 - c) * 2 * TOK, 2 * TOK)],
            dq_core.at[rows(xx * 2 * TOK, 2 * TOK)],
            other_core,
        )
        for xx, number in enumerate((DQ_C0, DQ_C1))
    ]
    for number in range(2):
        dq_core_copies[number].start()
    reduce_step(reduced + 1, reduced + 1 >= ring - 3)

    def settle_gather(item, carry):
        way, step = gathered(item)
        relay_copy(way, step, z, x).wait_send()
        for piece in range(3):
            gather_copy(way, step, piece, z).wait_send()
        return carry

    def settle_reduce(item, carry):
        way, step = leaving(item)
        cross_copy(way, step).wait_send()

        @pl.when(step > 0)
        def _():
            for piece in range(3):
                reduce_copy(way, step, piece).wait_send()

        return carry

    lax.fori_loop(1, ring, settle_gather, 0)
    for number in range(2):
        dq_core_copies[number].wait_recv()
    dq_out[...] = dq_rows[relay_rows, :] + dq_core[peer_heads, :]
    dq_copy = copy_once(DQ_X, dq_out, dq_own.at[own_heads], across)
    dq_copy.start()
    dq_own[own_heads, :] = dq_rows[own_rows, :] + dq_core[own_heads, :]

    for xx, head in turn_back:
        cols = rows(((xx * 2 + c) * 2 + head) * TOK)
        att_rows[(xx * 2 + head) * TOK : (xx * 2 + head + 1) * TOK, :] = att_cols[:, cols].T
    att_copy = copy_once(ATT_X, att_rows.at[peer_heads], att_own.at[own_heads], across)
    att_copy.start()
    att_own[own_heads, :] = att_rows[own_heads, :]

    lax.fori_loop(reduced + 2, ring - 3, reduce_only, 0)
    for item in range(max(reduced + 2, ring - 3), ring - 1):
        reduce_step(item, True)
    lax.fori_loop(0, ring - 3, settle_reduce, 0)

    att_copy.wait_recv()
    result = codes_in[...].astype(F32)
    for head in range(4):
        span = slice(head * TOK, (head + 1) * TOK)
        result = result + dot(att_own[span, :], w_out[span, :])
    out_codes[...] = result.astype(BF16)

    dq_copy.wait_recv()
    normed_grad = jnp.zeros((TOK, w_query.shape[0]), F32)
    for head in range(4):
        span = slice(head * TOK, (head + 1) * TOK)
        lin_grad = norm_back(q_lin[:, span], q_gain[...], dq_own[span, :])
        normed_grad = normed_grad + dot_last(lin_grad, w_query[:, span])

    def ringed(piece):
        for way in range(2):
            reduce_copy(way, 1, piece).wait_recv()
        span = slice(piece * PIECE, (piece + 1) * PIECE)
        return ring_in[0, 0, span].astype(F32) + ring_in[1, 0, span].astype(F32)

    cross_copy(1, 0).wait_recv()
    dkv_copy.wait_recv()
    first_part = own_part(1, 0, 0) + kv_peer[...].astype(F32)
    second_part = own_part(1, 0, 1) + cross_in[1, 0].astype(F32)
    kv_grad[:PIECE, :] = first_part + ringed(0) + ringed(2)
    kv_grad[PIECE:, :] = second_part + ringed(1)
    key_grad = norm_back(k_lin[...], k_gain[...], kv_grad[:, :HD])
    normed_grad = normed_grad + dot_last(key_grad, w_key[...])
    normed_grad = normed_grad + dot_last(kv_grad[:, HD:].astype(BF16), w_value[...])
    wide = codes_in[...].astype(F32)
    inv_norm = lax.rsqrt(jnp.sum(wide * wide, axis=-1, keepdims=True) / D + NORM_EPS)
    inner = jnp.sum(wide * normed_grad, axis=-1, keepdims=True)
    in_grads[...] = (
        grads_in[...].astype(F32)
        + inv_norm * normed_grad
        - wide * (inv_norm * inv_norm * inv_norm) * inner / D
    ).astype(BF16)

    for once in (codes_copy, grads_copy, kv_copy, acc_copy, stats_copy, att_copy, dq_copy, dkv_copy):
        once.wait_send()
    for once in (*q_copies, *do_copies, *dq_core_copies):
        once.wait_send()

    relay_copy(0, 0, z, x).wait_send()
    lax.fori_loop(ring - 3, ring, settle_reduce, 0)


def hand_over(codes, grads, out_codes, in_grads, sems):
    pairs = ((codes, out_codes), (grads, in_grads))
    copies = [pltpu.make_async_copy(src, dst, sems.at[i]) for i, (src, dst) in enumerate(pairs)]
    for one in copies:
        one.start()
    for one in copies:
        one.wait()


def rope_tables(first_pos):
    half_dim = HD // 2
    exponent = jnp.arange(half_dim).astype(F32) * (2.0 / HD)
    frequency = jnp.power(F32(ROPE_BASE), -exponent)
    frequency = jnp.concatenate([frequency, frequency])
    shape = (TOK // 2, HD)
    lane = lax.broadcasted_iota(jnp.int32, shape, 1)
    offset = lax.broadcasted_iota(jnp.int32, shape, 0) + jnp.where(lane < half_dim, 0, TOK // 2)
    angles = (first_pos + offset).astype(F32) * frequency[None, :]
    return (jnp.cos(angles), jnp.sin(angles))


def local(
    sent_codes, start_codes, sent_grads, loss_grads, w_query, w_key, w_value, w_out, q_gain, k_gain
):
    ring = lax.axis_size("seq") // 4
    sections = lax.axis_size("section")
    steps = ring // 2 + 1
    width = start_codes.shape[1]
    cosines, sines = rope_tables(lax.axis_index("seq") * TOK)
    vmem = pltpu.VMEM
    dma = pltpu.SemaphoreType.DMA
    one_block = (TOK, width)
    heads = (4 * TOK, HD)
    all_rows = (8 * TOK, HD)
    columns = (HD, 8 * TOK)
    stat = (1, 8 * TOK)
    results = pl.pallas_call(
        functools.partial(kernel, ring, sections),
        out_shape=(jax.ShapeDtypeStruct(one_block, BF16),) * 2,
        in_specs=[pl.BlockSpec(memory_space=pltpu.HBM)] * 8 + [pl.BlockSpec(memory_space=vmem)] * 4,
        out_specs=(pl.BlockSpec(memory_space=vmem),) * 2,
        scratch_shapes=[
            vmem(w_query.shape[1:], BF16),
            vmem(w_key.shape[1:], BF16),
            vmem(w_value.shape[1:], BF16),
            vmem(w_out.shape[1:], BF16),
            vmem(one_block, BF16),
            vmem(one_block, BF16),
            vmem(one_block, BF16),
            vmem(one_block, BF16),
            vmem(one_block, BF16),
            vmem(one_block, BF16),
            vmem(one_block, F32),
            vmem((TOK, HD), F32),
            vmem(heads, BF16),
            vmem(all_rows, BF16),
            vmem(columns, BF16),
            vmem(heads, BF16),
            vmem(all_rows, BF16),
            vmem(columns, BF16),
            vmem((ring * 2 * TOK, 2 * HD), BF16),
            vmem((8, 8 * TOK), F32),
            vmem((8, 8 * TOK), F32),
            vmem(columns, F32),
            vmem(columns, F32),
            vmem(stat, F32),
            vmem(stat, F32),
            vmem(columns, BF16),
            vmem(heads, BF16),
            vmem(heads, BF16),
            vmem(columns, F32),
            vmem(all_rows, F32),
            vmem(heads, F32),
            vmem((2 * TOK, HD), F32),
            vmem(heads, F32),
            vmem((2, steps, 2 * TOK, 8 * TOK), F32),
            vmem((2, steps, 8, 8 * TOK), F32),
            vmem((2, steps, 2 * TOK, 2 * HD), F32),
            vmem((2, steps, 3 * PIECE, 2 * HD), BF16),
            vmem((2, steps, 3 * PIECE, 2 * HD), BF16),
            vmem((2, steps, PIECE, 2 * HD), BF16),
            vmem((2, steps, PIECE, 2 * HD), BF16),
            vmem((TOK, 2 * HD), F32),
            vmem((PIECE, 2 * HD), BF16),
            vmem((PIECE, 2 * HD), BF16),
            dma((16,)),
            dma((16,)),
            dma((2, steps, 3)),
            dma((2, steps, 3)),
            dma((2, steps, 3)),
            dma((2, steps, 3)),
            dma((2, steps)),
            dma((2, steps)),
            dma((2, steps)),
            dma((2, steps)),
            dma((6,)),
        ],
        compiler_params=pltpu.CompilerParams(
            collective_id=0, has_side_effects=True, vmem_limit_bytes=60 * 1024 * 1024
        ),
    )(
        sent_codes[0],
        start_codes,
        sent_grads[0],
        loss_grads,
        w_query[0],
        w_key[0],
        w_value[0],
        w_out[0],
        q_gain,
        k_gain,
        cosines,
        sines,
    )
    results = pl.pallas_call(
        hand_over,
        out_shape=(jax.ShapeDtypeStruct(one_block, BF16),) * 2,
        in_specs=[pl.BlockSpec(memory_space=pl.ANY)] * 2,
        out_specs=(pl.BlockSpec(memory_space=pl.ANY),) * 2,
        scratch_shapes=[dma((2,))],
        compiler_params=pltpu.CompilerParams(vmem_limit_bytes=60 * 1024 * 1024),
    )(*results)
    return (results[0][None], results[1][None])


def solution(mesh):
    in_specs = (
        P("section", "seq", None),
        P("seq", None),
        P("section", "seq", None),
        P("seq", None),
        P("section", None, None),
        P("section", None, None),
        P("section", None, None),
        P("section", None, None),
        P("section", None),
        P("section", None),
    )
    out_specs = (P("section", "seq", None), P("section", "seq", None))
    return jax.shard_map(local, mesh=mesh, in_specs=in_specs, out_specs=out_specs, check_vma=False)
```

```python
import functools

import jax
import jax.numpy as jnp
from jax import lax
from jax.experimental import pallas as pl
from jax.experimental.pallas import tpu as pltpu
from jax.sharding import PartitionSpec as P

D = 5120
ROPE_BASE = 1000000.0
NORM_EPS = 1e-06
MASK_FILL = -1e30
LOG2_E = 1.4426950408889634
MESH = pl.DeviceIdType.MESH
F32 = jnp.float32
BF16 = jnp.bfloat16
TOK = 128
HD = 128
PIECE = 64
CONTRACT_LAST = (((1,), (1,)), ((), ()))
CONTRACT_FIRST = (((0,), (0,)), ((), ()))

CODES, GRADS, KV_X, ATT_X, DQ_X, DKV_X, ACC_C, STATS_C, DQ_C0, DQ_C1 = range(10)
Q_X, Q_C, Q_R, DO_X, DO_C, DO_R = range(10, 16)


def dot(a, b):
    return jnp.dot(a, b, preferred_element_type=F32)


def dot_last(a, b):
    return lax.dot_general(a, b, CONTRACT_LAST, preferred_element_type=F32)


def dot_first(a, b):
    return lax.dot_general(a, b, CONTRACT_FIRST, preferred_element_type=F32)


def rows(start, count=TOK):
    return pl.ds(pl.multiple_of(start, TOK), count)


def kernel(
    ring,
    sections,
    sent_codes,
    start_codes,
    sent_grads,
    loss_grads,
    w_query_hbm,
    w_key_hbm,
    w_value_hbm,
    w_out_hbm,
    q_gain,
    k_gain,
    cosines,
    sines,
    out_codes,
    in_grads,
    w_query,
    w_key,
    w_value,
    w_out,
    codes_out,
    grads_out,
    codes_edge,
    grads_edge,
    codes_buf,
    grads_buf,
    codes_in,
    grads_in,
    q_lin,
    k_lin,
    q_own,
    q_rows,
    q_cols,
    do_own,
    do_rows,
    do_cols,
    kv,
    stats,
    stats_peer,
    acc,
    acc_peer,
    lse,
    delta,
    att_cols,
    att_rows,
    att_own,
    dq_cols,
    dq_rows,
    dq_core,
    dq_out,
    dq_own,
    kept_weights,
    kept_tops,
    part,
    ring_out,
    ring_in,
    cross_out,
    cross_in,
    kv_grad,
    kv_send,
    kv_peer,
    once_send,
    once_recv,
    gather_send,
    gather_recv,
    reduce_send,
    reduce_recv,
    relay_send,
    relay_recv,
    cross_send,
    cross_recv,
    load_sems,
):
    half = ring // 2
    sec = lax.axis_index("section")
    me = lax.axis_index("seq")
    x = lax.div(me, 2 * ring)
    z = lax.rem(lax.div(me, 2), ring)
    c = lax.rem(me, 2)

    def device(xx, zz, cc):
        return (sec, (xx * ring + zz) * 2 + cc)

    def along(way):
        return device(x, lax.rem(z + 1 + way * (ring - 2), ring), c)

    def diagonal(way):
        return device(1 - x, lax.rem(z + 1 + way * (ring - 2), ring), c)

    other_core = device(x, z, 1 - c)
    across = device(1 - x, z, c)
    next_section = (lax.rem(sec + 1, sections), me)
    last_section = (lax.rem(sec + sections - 1, sections), me)

    def copy(src, dst, send, recv, target):
        return pltpu.make_async_remote_copy(
            src_ref=src,
            dst_ref=dst,
            send_sem=send,
            recv_sem=recv,
            device_id=target,
            device_id_type=MESH,
        )

    def copy_once(number, src, dst, target):
        return copy(src, dst, once_send.at[number], once_recv.at[number], target)

    loads = [
        pltpu.make_async_copy(src, dst, load_sems.at[number])
        for number, (src, dst) in enumerate(
            (
                (sent_codes, codes_out),
                (start_codes, codes_edge),
                (w_key_hbm, w_key),
                (w_value_hbm, w_value),
                (w_query_hbm, w_query),
                (sent_grads, grads_out),
                (loss_grads, grads_edge),
                (w_out_hbm, w_out),
            )
        )
    ]
    for load in loads:
        load.start()

    barrier = pltpu.get_barrier_semaphore()
    partners = (along(0), along(1), diagonal(0), diagonal(1), other_core, across)
    for partner in (*partners, next_section, last_section):
        pl.semaphore_signal(barrier, inc=1, device_id=partner, device_id_type=MESH)
    pl.semaphore_wait(barrier, 8)

    codes_copy = copy_once(CODES, codes_out, codes_buf, next_section)
    grads_copy = copy_once(GRADS, grads_out, grads_buf, last_section)
    loads[0].wait()
    codes_copy.start()

    stats[...] = jnp.where(
        lax.broadcasted_iota(jnp.int32, stats.shape, 0) == 0, F32(MASK_FILL), F32(0.0)
    )
    acc[...] = jnp.zeros(acc.shape, F32)
    dq_cols[...] = jnp.zeros(dq_cols.shape, F32)
    for way, farthest in ((0, half), (1, half - 1)):
        ring_in[way, farthest] = jnp.zeros(ring_in.shape[2:], BF16)

    lane = lax.broadcasted_iota(jnp.int32, (TOK, HD), 1)
    first_half = lane < HD // 2

    def unpack_table(packed):
        turned = pltpu.roll(packed, HD // 2, 1)
        left = first_half[: TOK // 2]
        return jnp.concatenate(
            [jnp.where(left, packed, turned), jnp.where(left, turned, packed)], axis=0
        )

    cos = unpack_table(cosines[...])
    sin = unpack_table(sines[...])
    sin_turned = jnp.where(first_half, -sin, sin)

    def head_norm(tensor, gain):
        inv = lax.rsqrt(jnp.mean(tensor * tensor, axis=-1, keepdims=True) + NORM_EPS)
        hat = tensor * inv * gain
        return (hat * cos + pltpu.roll(hat, HD // 2, 1) * sin_turned).astype(BF16)

    def norm_back(tensor, gain, rot_grad):
        turned = pltpu.roll(rot_grad * sin, HD // 2, 1)
        hat_grad = rot_grad * cos + jnp.where(first_half, turned, -turned)
        inv = lax.rsqrt(jnp.mean(tensor * tensor, axis=-1, keepdims=True) + NORM_EPS)
        scaled = hat_grad * gain
        inner = jnp.mean(tensor * scaled, axis=-1, keepdims=True)
        return (inv * scaled - tensor * (inv * inv * inv) * inner).astype(BF16)

    def piece_of(piece, zz, xx=None):
        if xx is None:
            xx = x if piece < 2 else 1 - x
        start = (zz * 2 + xx) * TOK + piece % 2 * PIECE
        return kv.at[pl.ds(pl.multiple_of(start, PIECE), PIECE)]

    def place(way, step):
        return lax.rem(z + way * step + (1 - way) * (ring - step), ring)

    def gather_copy(way, step, piece, zz):
        ref = piece_of(piece, zz)
        sems = (gather_send.at[way, step, piece], gather_recv.at[way, step, piece])
        return copy(ref, ref, *sems, along(way))

    def relay_copy(way, step, zz, xx):
        ref = piece_of(3, zz, xx)
        return copy(ref, ref, relay_send.at[way, step], relay_recv.at[way, step], across)

    peer_heads = rows((1 - x) * 2 * TOK, 2 * TOK)
    own_heads = rows(x * 2 * TOK, 2 * TOK)
    own_rows = rows((x * 2 + c) * 2 * TOK, 2 * TOK)
    relay_rows = rows(((1 - x) * 2 + c) * 2 * TOK, 2 * TOK)

    def spread(number, src, dst):
        return (
            copy_once(number, src.at[peer_heads], dst.at[own_rows], across),
            copy_once(number + 1, src.at[own_heads], dst.at[own_rows], other_core),
            copy_once(number + 2, dst.at[relay_rows], dst.at[relay_rows], other_core),
        )

    q_copies = spread(Q_X, q_own, q_rows)
    do_copies = spread(DO_X, do_own, do_rows)

    def turn(src, dst):
        for block in range(src.shape[0] // TOK):
            span = slice(block * TOK, (block + 1) * TOK)
            dst[:, span] = src[span, :].T

    for load in loads[1:4]:
        load.wait()
    codes_copy.wait_recv()

    @pl.when(sec == 0)
    def _():
        codes_in[...] = codes_edge[...]

    @pl.when(sec != 0)
    def _():
        codes_in[...] = codes_buf[...]

    wide = codes_in[...].astype(F32)
    inv_norm = lax.rsqrt(jnp.sum(wide * wide, axis=-1, keepdims=True) / D + NORM_EPS)
    normed = (wide * inv_norm).astype(BF16)
    key_lin = dot(normed, w_key[...])
    k_lin[...] = key_lin
    own = rows((z * 2 + x) * TOK)
    kv[own, :HD] = head_norm(key_lin, k_gain[...])
    kv[own, HD:] = dot(normed, w_value[...]).astype(BF16)

    first_piece = piece_of(0, z, x)
    for piece in (1, 0):
        for way in range(2):
            gather_copy(way, 1, piece, z).start()
    for way in range(2):
        sems = (gather_send.at[way, 1, 2], gather_recv.at[way, 1, 2])
        copy(first_piece, first_piece, *sems, diagonal(way)).start()
    kv_copy = copy_once(KV_X, first_piece, first_piece, across)
    kv_copy.start()
    relay_copy(0, 0, z, x).start()

    loads[4].wait()
    q_lin[...] = dot(normed, w_query[...])
    for head in range(4):
        q_own[head * TOK : (head + 1) * TOK, :] = head_norm(
            q_lin[:, head * HD : (head + 1) * HD], q_gain[...]
        )
    q_copies[0].start()
    q_copies[1].start()
    q_rows[own_rows, :] = q_own[own_heads, :]

    loads[5].wait()
    grads_copy.start()

    scale = HD ** (-0.5)
    scale_two = scale * LOG2_E
    late = 4 * TOK

    def tile_cols(half_of):
        return slice(half_of * late, (half_of + 1) * late)

    def own_mask(half_of, keys):
        shape = (keys, late)
        key = lax.broadcasted_iota(jnp.int32, shape, 0)
        col = lax.broadcasted_iota(jnp.int32, shape, 1)
        query = (col & (TOK - 1)) + ((col & (2 * TOK)) >> 1)
        if half_of == 0:
            return key + c * TOK <= query
        return (key < TOK) | (key - TOK + c * TOK <= query)

    def forward_tile(kept, step, zz, half_of, keys, masked):
        span = tile_cols(half_of)
        block = rows(zz * 2 * TOK, keys)
        scores = dot(kv[block, :HD], q_cols[:, span]) * scale_two
        if masked:
            scores = jnp.where(own_mask(half_of, keys), scores, 2 * MASK_FILL)
        top_old = stats[0:1, span]
        top_new = jnp.maximum(top_old, jnp.max(scores, axis=0, keepdims=True))
        weights = jnp.exp2(scores - top_new)
        kept_weights[kept, step, :keys, span] = weights
        kept_tops[kept, step, half_of : half_of + 1, span] = top_new
        shrink = jnp.exp2(top_old - top_new)
        stats[1:2, span] = stats[1:2, span] * shrink + jnp.sum(weights, axis=0, keepdims=True)
        acc[:, span] = acc[:, span] * shrink + dot_first(kv[block, HD:], weights.astype(BF16))
        stats[0:1, span] = top_new

    def arrive(way, step, forward):
        zz = place(way, step)
        for piece in (1, 0, 2):
            gather_copy(way, step, piece, zz).wait_recv()

            @pl.when(forward)
            def _():
                gather_copy(way, step + 1, piece, zz).start()

            if piece == 1:
                relay_copy(way, step, zz, x).start()

    def gathered(item):
        return lax.rem(item + 1, 2), lax.div(item + 1, 2)

    def forward_block(item):
        way, step = gathered(item)
        zz = place(way, step)
        relay_copy(way, step, zz, 1 - x).wait_recv()
        kept = way + lax.div(step, half)

        @pl.when(zz < z)
        def _():
            forward_tile(kept, step, zz, 1, 2 * TOK, False)
            forward_tile(kept, step, zz, 0, TOK, False)

        @pl.when(zz > z)
        def _():
            forward_tile(kept, step, zz, 1, TOK, False)

    def arrive_item(item):
        way, step = gathered(item)
        arrive(way, step, step < half - way)

    arrive_item(1)
    arrive_item(2)
    q_copies[0].wait_recv()
    q_copies[2].start()
    arrive_item(3)
    if ring > 4:
        arrive_item(4)
    q_copies[1].wait_recv()
    q_copies[2].wait_recv()
    turn(q_rows, q_cols)
    kv_copy.wait_recv()
    relay_copy(0, 0, z, 1 - x).wait_recv()
    forward_tile(0, 0, z, 1, 2 * TOK, True)
    forward_tile(0, 0, z, 0, TOK, True)

    catches = (5 + ring // 4, 4 + ring // 2) if ring >= 16 else ()

    def caught_up(item):
        return sum(jnp.where(item >= catch, 1, 0) for catch in catches)

    def forward_step(item, carry):
        @pl.when(item < ring)
        def _():
            arrive_item(item)

        forward_block(item - 4 + caught_up(item - 1))

        if catches:

            @pl.when(caught_up(item) > caught_up(item - 1))
            def _():
                forward_block(item - 3 + caught_up(item - 1))

        @pl.when(item == 5 + ring // 4)
        def _():
            for load in loads[6:]:
                load.wait()
            grads_copy.wait_recv()

            @pl.when(sec == sections - 1)
            def _():
                grads_in[...] = grads_edge[...]

            @pl.when(sec != sections - 1)
            def _():
                grads_in[...] = grads_buf[...]

            grad_att = dot_last(grads_in[...], w_out[...]).astype(BF16)
            for head in range(4):
                do_own[head * TOK : (head + 1) * TOK, :] = grad_att[:, head * HD : (head + 1) * HD]
            do_copies[0].start()
            do_copies[1].start()
            do_rows[own_rows, :] = do_own[own_heads, :]

        @pl.when(item == 5 + ring // 2)
        def _():
            do_copies[0].wait_recv()
            do_copies[2].start()

        return carry

    lax.fori_loop(5, ring + 4 - len(catches), forward_step, 0)

    acc_copy = copy_once(ACC_C, acc, acc_peer, other_core)
    stats_copy = copy_once(STATS_C, stats, stats_peer, other_core)
    stats_copy.start()
    acc_copy.start()
    do_copies[1].wait_recv()
    do_copies[2].wait_recv()
    turn(do_rows, do_cols)
    stats_copy.wait_recv()
    top = jnp.maximum(stats[0:1, :], stats_peer[0:1, :])
    shrink = jnp.exp2(stats[0:1, :] - top)
    shrink_peer = jnp.exp2(stats_peer[0:1, :] - top)
    total = stats[1:2, :] * shrink + stats_peer[1:2, :] * shrink_peer
    lse[...] = top + jnp.log2(total)
    acc_copy.wait_recv()
    attended = (
        acc[...] * (shrink / total) + acc_peer[...] * (shrink_peer / total)
    ).astype(BF16)
    delta[...] = jnp.sum(
        do_cols[...].astype(F32) * attended.astype(F32), axis=0, keepdims=True
    )
    att_cols[...] = attended

    def backward_tile(way, step, zz, half_of, keys):
        span = tile_cols(half_of)
        block = rows(zz * 2 * TOK, keys)
        factor = jnp.exp2(kept_tops[1 - way, step, half_of : half_of + 1, span] - lse[:, span])
        probs = kept_weights[1 - way, step, :keys, span] * factor
        grad_prob = dot(kv[block, HD:], do_cols[:, span])
        grad_score = (probs * (grad_prob - delta[:, span]) * scale).astype(BF16)
        value_grad = dot(probs.astype(BF16), do_rows[span, :])
        key_grad = dot(grad_score, q_rows[span, :])
        if half_of == 1:
            part[way, step, :keys, HD:] = value_grad
            part[way, step, :keys, :HD] = key_grad
        else:
            part[way, step, :keys, HD:] += value_grad
            part[way, step, :keys, :HD] += key_grad
        dq_cols[:, span] += dot_first(kv[block, :HD], grad_score)

    def leaving(item):
        return lax.rem(item, 2), half - lax.div(item + 1, 2)

    def own_part(way, step, piece):
        xx = x if piece < 2 else 1 - x
        return part[way, step, pl.ds(pl.multiple_of(xx * TOK + piece % 2 * PIECE, PIECE), PIECE), :]

    def cross_copy(way, step):
        return copy(
            cross_out.at[way, step],
            cross_in.at[way, step],
            cross_send.at[way, step],
            cross_recv.at[way, step],
            across,
        )

    def backward_block(item):
        way, step = leaving(item)
        zz = place(1 - way, step)

        @pl.when(zz <= z)
        def _():
            backward_tile(way, step, zz, 1, 2 * TOK)
            backward_tile(way, step, zz, 0, TOK)

        @pl.when(zz > z)
        def _():
            backward_tile(way, step, zz, 1, TOK)
            part[way, step, TOK:, :] = jnp.zeros((TOK, 2 * HD), F32)

        cross_out[way, step] = own_part(way, step, 3).astype(BF16)
        cross_copy(way, step).start()

    def reduce_copy(way, step, piece, target=None):
        span = slice(piece * PIECE, (piece + 1) * PIECE)
        return copy(
            ring_out.at[way, step, span],
            ring_in.at[way, step - 1, span],
            reduce_send.at[way, step, piece],
            reduce_recv.at[way, step - 1, piece],
            along(way) if target is None else target,
        )

    def reduce_step(item, last=False):
        way, step = leaving(item)
        for piece in (0, 2, 1):

            @pl.when(step < half - way)
            def _():
                reduce_copy(way, step + 1, piece).wait_recv()

            span = slice(piece * PIECE, (piece + 1) * PIECE)
            summed = own_part(way, step, piece) + ring_in[way, step, span].astype(F32)
            if piece == 1:
                cross_copy(way, step).wait_recv()
                summed = summed + cross_in[way, step].astype(F32)
            ring_out[way, step, span] = summed.astype(BF16)
            target = diagonal(way) if last and piece == 2 else None
            reduce_copy(way, step, piece, target).start()

    def backward_step(count, carry):
        block = 2 + 3 * count
        backward_block(block)
        reduce_step(2 * count)
        backward_block(block + 1)
        reduce_step(2 * count + 1)
        backward_block(block + 2)
        return carry

    def reduce_only(item, carry):
        reduce_step(item)
        return carry

    rounds = (ring - 4) // 3
    reduced = 2 * rounds
    backward_block(0)
    backward_block(1)
    lax.fori_loop(0, rounds, backward_step, 0)
    backward_block(ring - 2)
    reduce_step(reduced)
    backward_block(ring - 1)

    kv_send[...] = own_part(1, 0, 2).astype(BF16)
    dkv_copy = copy_once(DKV_X, kv_send, kv_peer, across)
    dkv_copy.start()
    turn_back = [(xx, head) for xx in range(2) for head in range(2)]
    for block in range(8):
        span = slice(block * TOK, (block + 1) * TOK)
        dq_rows[span, :] = dq_cols[:, span].T
    dq_core_copies = [
        copy_once(
            number,
            dq_rows.at[rows((xx * 2 + 1 - c) * 2 * TOK, 2 * TOK)],
            dq_core.at[rows(xx * 2 * TOK, 2 * TOK)],
            other_core,
        )
        for xx, number in enumerate((DQ_C0, DQ_C1))
    ]
    for number in range(2):
        dq_core_copies[number].start()
    reduce_step(reduced + 1, reduced + 1 >= ring - 3)

    def settle_gather(item, carry):
        way, step = gathered(item)
        relay_copy(way, step, z, x).wait_send()
        for piece in range(3):
            gather_copy(way, step, piece, z).wait_send()
        return carry

    def settle_reduce(item, carry):
        way, step = leaving(item)
        cross_copy(way, step).wait_send()

        @pl.when(step > 0)
        def _():
            for piece in range(3):
                reduce_copy(way, step, piece).wait_send()

        return carry

    lax.fori_loop(1, ring, settle_gather, 0)
    for number in range(2):
        dq_core_copies[number].wait_recv()
    dq_out[...] = dq_rows[relay_rows, :] + dq_core[peer_heads, :]
    dq_copy = copy_once(DQ_X, dq_out, dq_own.at[own_heads], across)
    dq_copy.start()
    dq_own[own_heads, :] = dq_rows[own_rows, :] + dq_core[own_heads, :]

    for xx, head in turn_back:
        cols = rows(((xx * 2 + c) * 2 + head) * TOK)
        att_rows[(xx * 2 + head) * TOK : (xx * 2 + head + 1) * TOK, :] = att_cols[:, cols].T
    att_copy = copy_once(ATT_X, att_rows.at[peer_heads], att_own.at[own_heads], across)
    att_copy.start()
    att_own[own_heads, :] = att_rows[own_heads, :]

    lax.fori_loop(reduced + 2, ring - 3, reduce_only, 0)
    for item in range(max(reduced + 2, ring - 3), ring - 1):
        reduce_step(item, True)
    lax.fori_loop(0, ring - 3, settle_reduce, 0)

    att_copy.wait_recv()
    result = codes_in[...].astype(F32)
    for head in range(4):
        span = slice(head * TOK, (head + 1) * TOK)
        result = result + dot(att_own[span, :], w_out[span, :])
    out_codes[...] = result.astype(BF16)

    dq_copy.wait_recv()
    normed_grad = jnp.zeros((TOK, w_query.shape[0]), F32)
    for head in range(4):
        span = slice(head * TOK, (head + 1) * TOK)
        lin_grad = norm_back(q_lin[:, span], q_gain[...], dq_own[span, :])
        normed_grad = normed_grad + dot_last(lin_grad, w_query[:, span])

    def ringed(piece):
        for way in range(2):
            reduce_copy(way, 1, piece).wait_recv()
        span = slice(piece * PIECE, (piece + 1) * PIECE)
        return ring_in[0, 0, span].astype(F32) + ring_in[1, 0, span].astype(F32)

    cross_copy(1, 0).wait_recv()
    dkv_copy.wait_recv()
    first_part = own_part(1, 0, 0) + kv_peer[...].astype(F32)
    second_part = own_part(1, 0, 1) + cross_in[1, 0].astype(F32)
    kv_grad[:PIECE, :] = first_part + ringed(0) + ringed(2)
    kv_grad[PIECE:, :] = second_part + ringed(1)
    key_grad = norm_back(k_lin[...], k_gain[...], kv_grad[:, :HD])
    normed_grad = normed_grad + dot_last(key_grad, w_key[...])
    normed_grad = normed_grad + dot_last(kv_grad[:, HD:].astype(BF16), w_value[...])
    wide = codes_in[...].astype(F32)
    inv_norm = lax.rsqrt(jnp.sum(wide * wide, axis=-1, keepdims=True) / D + NORM_EPS)
    inner = jnp.sum(wide * normed_grad, axis=-1, keepdims=True)
    in_grads[...] = (
        grads_in[...].astype(F32)
        + inv_norm * normed_grad
        - wide * (inv_norm * inv_norm * inv_norm) * inner / D
    ).astype(BF16)

    for once in (codes_copy, grads_copy, kv_copy, acc_copy, stats_copy, att_copy, dq_copy, dkv_copy):
        once.wait_send()
    for once in (*q_copies, *do_copies, *dq_core_copies):
        once.wait_send()

    relay_copy(0, 0, z, x).wait_send()
    lax.fori_loop(ring - 3, ring, settle_reduce, 0)


def rope_tables(first_pos):
    half_dim = HD // 2
    exponent = jnp.arange(half_dim).astype(F32) * (2.0 / HD)
    frequency = jnp.power(F32(ROPE_BASE), -exponent)
    frequency = jnp.concatenate([frequency, frequency])
    shape = (TOK // 2, HD)
    lane = lax.broadcasted_iota(jnp.int32, shape, 1)
    offset = lax.broadcasted_iota(jnp.int32, shape, 0) + jnp.where(lane < half_dim, 0, TOK // 2)
    angles = (first_pos + offset).astype(F32) * frequency[None, :]
    return (jnp.cos(angles), jnp.sin(angles))


def local(
    sent_codes, start_codes, sent_grads, loss_grads, w_query, w_key, w_value, w_out, q_gain, k_gain
):
    ring = lax.axis_size("seq") // 4
    sections = lax.axis_size("section")
    steps = ring // 2 + 1
    width = start_codes.shape[1]
    cosines, sines = rope_tables(lax.axis_index("seq") * TOK)
    vmem = pltpu.VMEM
    dma = pltpu.SemaphoreType.DMA
    one_block = (TOK, width)
    heads = (4 * TOK, HD)
    all_rows = (8 * TOK, HD)
    columns = (HD, 8 * TOK)
    stat = (1, 8 * TOK)
    results = pl.pallas_call(
        functools.partial(kernel, ring, sections),
        out_shape=(jax.ShapeDtypeStruct(one_block, BF16),) * 2,
        in_specs=[pl.BlockSpec(memory_space=pltpu.HBM)] * 8 + [pl.BlockSpec(memory_space=vmem)] * 4,
        out_specs=(pl.BlockSpec(memory_space=vmem),) * 2,
        scratch_shapes=[
            vmem(w_query.shape[1:], BF16),
            vmem(w_key.shape[1:], BF16),
            vmem(w_value.shape[1:], BF16),
            vmem(w_out.shape[1:], BF16),
            vmem(one_block, BF16),
            vmem(one_block, BF16),
            vmem(one_block, BF16),
            vmem(one_block, BF16),
            vmem(one_block, BF16),
            vmem(one_block, BF16),
            vmem(one_block, BF16),
            vmem(one_block, BF16),
            vmem(one_block, F32),
            vmem((TOK, HD), F32),
            vmem(heads, BF16),
            vmem(all_rows, BF16),
            vmem(columns, BF16),
            vmem(heads, BF16),
            vmem(all_rows, BF16),
            vmem(columns, BF16),
            vmem((ring * 2 * TOK, 2 * HD), BF16),
            vmem((8, 8 * TOK), F32),
            vmem((8, 8 * TOK), F32),
            vmem(columns, F32),
            vmem(columns, F32),
            vmem(stat, F32),
            vmem(stat, F32),
            vmem(columns, BF16),
            vmem(heads, BF16),
            vmem(heads, BF16),
            vmem(columns, F32),
            vmem(all_rows, F32),
            vmem(heads, F32),
            vmem((2 * TOK, HD), F32),
            vmem(heads, F32),
            vmem((2, steps, 2 * TOK, 8 * TOK), F32),
            vmem((2, steps, 8, 8 * TOK), F32),
            vmem((2, steps, 2 * TOK, 2 * HD), F32),
            vmem((2, steps, 3 * PIECE, 2 * HD), BF16),
            vmem((2, steps, 3 * PIECE, 2 * HD), BF16),
            vmem((2, steps, PIECE, 2 * HD), BF16),
            vmem((2, steps, PIECE, 2 * HD), BF16),
            vmem((TOK, 2 * HD), F32),
            vmem((PIECE, 2 * HD), BF16),
            vmem((PIECE, 2 * HD), BF16),
            dma((16,)),
            dma((16,)),
            dma((2, steps, 3)),
            dma((2, steps, 3)),
            dma((2, steps, 3)),
            dma((2, steps, 3)),
            dma((2, steps)),
            dma((2, steps)),
            dma((2, steps)),
            dma((2, steps)),
            dma((8,)),
        ],
        compiler_params=pltpu.CompilerParams(
            collective_id=0, has_side_effects=True, vmem_limit_bytes=60 * 1024 * 1024
        ),
    )(
        sent_codes[0],
        start_codes,
        sent_grads[0],
        loss_grads,
        w_query[0],
        w_key[0],
        w_value[0],
        w_out[0],
        q_gain,
        k_gain,
        cosines,
        sines,
    )
    return (results[0][None], results[1][None])


def solution(mesh):
    in_specs = (
        P("section", "seq", None),
        P("seq", None),
        P("section", "seq", None),
        P("seq", None),
        P("section", None, None),
        P("section", None, None),
        P("section", None, None),
        P("section", None, None),
        P("section", None),
        P("section", None),
    )
    out_specs = (P("section", "seq", None), P("section", "seq", None))
    return jax.shard_map(local, mesh=mesh, in_specs=in_specs, out_specs=out_specs, check_vma=False)
```

```python
import functools

import jax
import jax.numpy as jnp
from jax import lax
from jax.experimental import pallas as pl
from jax.experimental.pallas import tpu as pltpu
from jax.sharding import PartitionSpec as P

D = 5120
ROPE_BASE = 1000000.0
NORM_EPS = 1e-06
MASK_FILL = -1e30
LOG2_E = 1.4426950408889634
MESH = pl.DeviceIdType.MESH
F32 = jnp.float32
BF16 = jnp.bfloat16
TOK = 128
HD = 128
PIECE = 64
CONTRACT_LAST = (((1,), (1,)), ((), ()))
CONTRACT_FIRST = (((0,), (0,)), ((), ()))

CODES, GRADS, KV_X, ATT_X, DQ_X, DKV_X, ACC_C, STATS_C, DQ_C0, DQ_C1 = range(10)
Q_X, Q_C, Q_R, DO_X, DO_C, DO_R = range(10, 16)


def dot(a, b):
    return jnp.dot(a, b, preferred_element_type=F32)


def dot_last(a, b):
    return lax.dot_general(a, b, CONTRACT_LAST, preferred_element_type=F32)


def dot_first(a, b):
    return lax.dot_general(a, b, CONTRACT_FIRST, preferred_element_type=F32)


def rows(start, count=TOK):
    return pl.ds(pl.multiple_of(start, TOK), count)


def kernel(
    ring,
    sections,
    sent_codes,
    start_codes,
    sent_grads,
    loss_grads,
    w_query_hbm,
    w_key_hbm,
    w_value_hbm,
    w_out_hbm,
    q_gain,
    k_gain,
    cosines,
    sines,
    out_codes,
    in_grads,
    w_query,
    w_key,
    w_value,
    w_out,
    codes_out,
    grads_out,
    codes_edge,
    grads_edge,
    codes_buf,
    grads_buf,
    codes_in,
    grads_in,
    q_lin,
    k_lin,
    q_own,
    q_rows,
    q_cols,
    do_own,
    do_rows,
    do_cols,
    kv,
    stats,
    stats_peer,
    acc,
    acc_peer,
    lse,
    delta,
    att_cols,
    att_rows,
    att_own,
    dq_cols,
    dq_rows,
    dq_core,
    dq_out,
    dq_own,
    kept_weights,
    kept_tops,
    part,
    ring_out,
    ring_in,
    cross_out,
    cross_in,
    kv_grad,
    kv_send,
    kv_peer,
    once_send,
    once_recv,
    gather_send,
    gather_recv,
    reduce_send,
    reduce_recv,
    relay_send,
    relay_recv,
    cross_send,
    cross_recv,
    load_sems,
):
    half = ring // 2
    sec = lax.axis_index("section")
    me = lax.axis_index("seq")
    x = lax.div(me, 2 * ring)
    z = lax.rem(lax.div(me, 2), ring)
    c = lax.rem(me, 2)

    def device(xx, zz, cc):
        return (sec, (xx * ring + zz) * 2 + cc)

    def along(way, hops=1):
        return device(x, lax.rem(z + hops + way * (ring - 2 * hops), ring), c)

    def diagonal(way, hops=1):
        return device(1 - x, lax.rem(z + hops + way * (ring - 2 * hops), ring), c)

    other_core = device(x, z, 1 - c)
    across = device(1 - x, z, c)
    next_section = (lax.rem(sec + 1, sections), me)
    last_section = (lax.rem(sec + sections - 1, sections), me)

    def copy(src, dst, send, recv, target):
        return pltpu.make_async_remote_copy(
            src_ref=src,
            dst_ref=dst,
            send_sem=send,
            recv_sem=recv,
            device_id=target,
            device_id_type=MESH,
        )

    def copy_once(number, src, dst, target):
        return copy(src, dst, once_send.at[number], once_recv.at[number], target)

    loads = [
        pltpu.make_async_copy(src, dst, load_sems.at[number])
        for number, (src, dst) in enumerate(
            (
                (sent_codes, codes_out),
                (start_codes, codes_edge),
                (w_key_hbm, w_key),
                (w_value_hbm, w_value),
                (w_query_hbm, w_query),
                (sent_grads, grads_out),
                (loss_grads, grads_edge),
                (w_out_hbm, w_out),
            )
        )
    ]
    for load in loads:
        load.start()

    barrier = pltpu.get_barrier_semaphore()
    near = [(way, hops) for way in range(2) for hops in (1, 2)]
    partners = [along(*one) for one in near] + [diagonal(*one) for one in near]
    for partner in (*partners, other_core, across, next_section, last_section):
        pl.semaphore_signal(barrier, inc=1, device_id=partner, device_id_type=MESH)
    pl.semaphore_wait(barrier, 12)

    codes_copy = copy_once(CODES, codes_out, codes_buf, next_section)
    grads_copy = copy_once(GRADS, grads_out, grads_buf, last_section)
    loads[0].wait()
    codes_copy.start()

    stats[...] = jnp.where(
        lax.broadcasted_iota(jnp.int32, stats.shape, 0) == 0, F32(MASK_FILL), F32(0.0)
    )
    acc[...] = jnp.zeros(acc.shape, F32)
    dq_cols[...] = jnp.zeros(dq_cols.shape, F32)
    for way, farthest in ((0, half), (1, half - 1)):
        if farthest > 1:
            ring_in[way, farthest] = jnp.zeros(ring_in.shape[2:], BF16)

    lane = lax.broadcasted_iota(jnp.int32, (TOK, HD), 1)
    first_half = lane < HD // 2

    def unpack_table(packed):
        turned = pltpu.roll(packed, HD // 2, 1)
        left = first_half[: TOK // 2]
        return jnp.concatenate(
            [jnp.where(left, packed, turned), jnp.where(left, turned, packed)], axis=0
        )

    cos = unpack_table(cosines[...])
    sin = unpack_table(sines[...])
    sin_turned = jnp.where(first_half, -sin, sin)

    def head_norm(tensor, gain):
        inv = lax.rsqrt(jnp.mean(tensor * tensor, axis=-1, keepdims=True) + NORM_EPS)
        hat = tensor * inv * gain
        return (hat * cos + pltpu.roll(hat, HD // 2, 1) * sin_turned).astype(BF16)

    def norm_back(tensor, gain, rot_grad):
        turned = pltpu.roll(rot_grad * sin, HD // 2, 1)
        hat_grad = rot_grad * cos + jnp.where(first_half, turned, -turned)
        inv = lax.rsqrt(jnp.mean(tensor * tensor, axis=-1, keepdims=True) + NORM_EPS)
        scaled = hat_grad * gain
        inner = jnp.mean(tensor * scaled, axis=-1, keepdims=True)
        return (inv * scaled - tensor * (inv * inv * inv) * inner).astype(BF16)

    def piece_of(piece, zz, xx=None):
        if xx is None:
            xx = x if piece < 2 else 1 - x
        start = (zz * 2 + xx) * TOK + piece % 2 * PIECE
        return kv.at[pl.ds(pl.multiple_of(start, PIECE), PIECE)]

    def place(way, step):
        return lax.rem(z + way * step + (1 - way) * (ring - step), ring)

    def gather_copy(way, step, piece, zz, hops=1):
        ref = piece_of(piece, zz)
        sems = (gather_send.at[way, step, piece], gather_recv.at[way, step, piece])
        return copy(ref, ref, *sems, along(way, hops))

    def relay_copy(way, step, zz, xx):
        ref = piece_of(3, zz, xx)
        return copy(ref, ref, relay_send.at[way, step], relay_recv.at[way, step], across)

    peer_heads = rows((1 - x) * 2 * TOK, 2 * TOK)
    own_heads = rows(x * 2 * TOK, 2 * TOK)
    own_rows = rows((x * 2 + c) * 2 * TOK, 2 * TOK)
    relay_rows = rows(((1 - x) * 2 + c) * 2 * TOK, 2 * TOK)

    def spread(number, src, dst):
        return (
            copy_once(number, src.at[peer_heads], dst.at[own_rows], across),
            copy_once(number + 1, src.at[own_heads], dst.at[own_rows], other_core),
            copy_once(number + 2, dst.at[relay_rows], dst.at[relay_rows], other_core),
        )

    q_copies = spread(Q_X, q_own, q_rows)
    do_copies = spread(DO_X, do_own, do_rows)

    def turn(src, dst):
        for block in range(src.shape[0] // TOK):
            span = slice(block * TOK, (block + 1) * TOK)
            dst[:, span] = src[span, :].T

    for load in loads[1:4]:
        load.wait()
    codes_copy.wait_recv()

    @pl.when(sec == 0)
    def _():
        codes_in[...] = codes_edge[...]

    @pl.when(sec != 0)
    def _():
        codes_in[...] = codes_buf[...]

    wide = codes_in[...].astype(F32)
    inv_norm = lax.rsqrt(jnp.sum(wide * wide, axis=-1, keepdims=True) / D + NORM_EPS)
    normed = (wide * inv_norm).astype(BF16)
    key_lin = dot(normed, w_key[...])
    k_lin[...] = key_lin
    own = rows((z * 2 + x) * TOK)
    kv[own, :HD] = head_norm(key_lin, k_gain[...])
    kv[own, HD:] = dot(normed, w_value[...]).astype(BF16)

    first_piece = piece_of(0, z, x)
    reached = [(way, hops) for hops in (1, 2) for way in range(2) if hops <= half - way]
    for way, hops in reached:
        for piece in (1, 0):
            gather_copy(way, hops, piece, z, hops).start()
        sems = (gather_send.at[way, hops, 2], gather_recv.at[way, hops, 2])
        copy(first_piece, first_piece, *sems, diagonal(way, hops)).start()
    kv_copy = copy_once(KV_X, first_piece, first_piece, across)
    kv_copy.start()
    relay_copy(0, 0, z, x).start()

    loads[4].wait()
    q_lin[...] = dot(normed, w_query[...])
    for head in range(4):
        q_own[head * TOK : (head + 1) * TOK, :] = head_norm(
            q_lin[:, head * HD : (head + 1) * HD], q_gain[...]
        )
    q_copies[0].start()
    q_copies[1].start()
    q_rows[own_rows, :] = q_own[own_heads, :]

    loads[5].wait()
    grads_copy.start()

    scale = HD ** (-0.5)
    scale_two = scale * LOG2_E
    late = 4 * TOK

    def tile_cols(half_of):
        return slice(half_of * late, (half_of + 1) * late)

    def own_mask(half_of, keys):
        shape = (keys, late)
        key = lax.broadcasted_iota(jnp.int32, shape, 0)
        col = lax.broadcasted_iota(jnp.int32, shape, 1)
        query = (col & (TOK - 1)) + ((col & (2 * TOK)) >> 1)
        if half_of == 0:
            return key + c * TOK <= query
        return (key < TOK) | (key - TOK + c * TOK <= query)

    def forward_tile(kept, step, zz, half_of, keys, masked):
        span = tile_cols(half_of)
        block = rows(zz * 2 * TOK, keys)
        scores = dot(kv[block, :HD], q_cols[:, span]) * scale_two
        if masked:
            scores = jnp.where(own_mask(half_of, keys), scores, 2 * MASK_FILL)
        top_old = stats[0:1, span]
        top_new = jnp.maximum(top_old, jnp.max(scores, axis=0, keepdims=True))
        weights = jnp.exp2(scores - top_new)
        kept_weights[kept, step, :keys, span] = weights
        kept_tops[kept, step, half_of : half_of + 1, span] = top_new
        shrink = jnp.exp2(top_old - top_new)
        stats[1:2, span] = stats[1:2, span] * shrink + jnp.sum(weights, axis=0, keepdims=True)
        acc[:, span] = acc[:, span] * shrink + dot_first(kv[block, HD:], weights.astype(BF16))
        stats[0:1, span] = top_new

    def arrive(way, step, forward):
        zz = place(way, step)
        for piece in (1, 0, 2):
            gather_copy(way, step, piece, zz).wait_recv()

            @pl.when(forward)
            def _():
                gather_copy(way, step + 1, piece, zz).start()

            if piece == 1:
                relay_copy(way, step, zz, x).start()

    def gathered(item):
        return lax.rem(item + 1, 2), lax.div(item + 1, 2)

    def forward_block(item):
        way, step = gathered(item)
        zz = place(way, step)
        relay_copy(way, step, zz, 1 - x).wait_recv()
        kept = way + lax.div(step, half)

        @pl.when(zz < z)
        def _():
            forward_tile(kept, step, zz, 1, 2 * TOK, False)
            forward_tile(kept, step, zz, 0, TOK, False)

        @pl.when(zz > z)
        def _():
            forward_tile(kept, step, zz, 1, TOK, False)

    def arrive_item(item):
        way, step = gathered(item)
        arrive(way, step, (step > 1) & (step < half - way))

    arrive_item(1)
    arrive_item(2)
    q_copies[0].wait_recv()
    q_copies[2].start()
    arrive_item(3)
    if ring > 4:
        arrive_item(4)
    q_copies[1].wait_recv()
    q_copies[2].wait_recv()
    turn(q_rows, q_cols)
    kv_copy.wait_recv()
    relay_copy(0, 0, z, 1 - x).wait_recv()
    forward_tile(0, 0, z, 1, 2 * TOK, True)
    forward_tile(0, 0, z, 0, TOK, True)

    catches = (5 + ring // 4, 4 + ring // 2) if ring >= 16 else ()

    def caught_up(item):
        return sum(jnp.where(item >= catch, 1, 0) for catch in catches)

    def forward_step(item, carry):
        @pl.when(item < ring)
        def _():
            arrive_item(item)

        forward_block(item - 4 + caught_up(item - 1))

        if catches:

            @pl.when(caught_up(item) > caught_up(item - 1))
            def _():
                forward_block(item - 3 + caught_up(item - 1))

        @pl.when(item == 5 + ring // 4)
        def _():
            for load in loads[6:]:
                load.wait()
            grads_copy.wait_recv()

            @pl.when(sec == sections - 1)
            def _():
                grads_in[...] = grads_edge[...]

            @pl.when(sec != sections - 1)
            def _():
                grads_in[...] = grads_buf[...]

            grad_att = dot_last(grads_in[...], w_out[...]).astype(BF16)
            for head in range(4):
                do_own[head * TOK : (head + 1) * TOK, :] = grad_att[:, head * HD : (head + 1) * HD]
            do_copies[0].start()
            do_copies[1].start()
            do_rows[own_rows, :] = do_own[own_heads, :]

        @pl.when(item == 5 + ring // 2)
        def _():
            do_copies[0].wait_recv()
            do_copies[2].start()

        return carry

    lax.fori_loop(5, ring + 4 - len(catches), forward_step, 0)

    acc_copy = copy_once(ACC_C, acc, acc_peer, other_core)
    stats_copy = copy_once(STATS_C, stats, stats_peer, other_core)
    stats_copy.start()
    acc_copy.start()
    do_copies[1].wait_recv()
    do_copies[2].wait_recv()
    turn(do_rows, do_cols)
    stats_copy.wait_recv()
    top = jnp.maximum(stats[0:1, :], stats_peer[0:1, :])
    shrink = jnp.exp2(stats[0:1, :] - top)
    shrink_peer = jnp.exp2(stats_peer[0:1, :] - top)
    total = stats[1:2, :] * shrink + stats_peer[1:2, :] * shrink_peer
    lse[...] = top + jnp.log2(total)
    acc_copy.wait_recv()
    attended = (
        acc[...] * (shrink / total) + acc_peer[...] * (shrink_peer / total)
    ).astype(BF16)
    delta[...] = jnp.sum(
        do_cols[...].astype(F32) * attended.astype(F32), axis=0, keepdims=True
    )
    att_cols[...] = attended

    def backward_tile(way, step, zz, half_of, keys):
        span = tile_cols(half_of)
        block = rows(zz * 2 * TOK, keys)
        factor = jnp.exp2(kept_tops[1 - way, step, half_of : half_of + 1, span] - lse[:, span])
        probs = kept_weights[1 - way, step, :keys, span] * factor
        grad_prob = dot(kv[block, HD:], do_cols[:, span])
        grad_score = (probs * (grad_prob - delta[:, span]) * scale).astype(BF16)
        value_grad = dot(probs.astype(BF16), do_rows[span, :])
        key_grad = dot(grad_score, q_rows[span, :])
        if half_of == 1:
            part[way, step, :keys, HD:] = value_grad
            part[way, step, :keys, :HD] = key_grad
        else:
            part[way, step, :keys, HD:] += value_grad
            part[way, step, :keys, :HD] += key_grad
        dq_cols[:, span] += dot_first(kv[block, :HD], grad_score)

    def leaving(item):
        return lax.rem(item, 2), half - lax.div(item + 1, 2)

    def own_part(way, step, piece):
        xx = x if piece < 2 else 1 - x
        return part[way, step, pl.ds(pl.multiple_of(xx * TOK + piece % 2 * PIECE, PIECE), PIECE), :]

    def cross_copy(way, step):
        return copy(
            cross_out.at[way, step],
            cross_in.at[way, step],
            cross_send.at[way, step],
            cross_recv.at[way, step],
            across,
        )

    def backward_block(item):
        way, step = leaving(item)
        zz = place(1 - way, step)

        @pl.when(zz <= z)
        def _():
            backward_tile(way, step, zz, 1, 2 * TOK)
            backward_tile(way, step, zz, 0, TOK)

        @pl.when(zz > z)
        def _():
            backward_tile(way, step, zz, 1, TOK)
            part[way, step, TOK:, :] = jnp.zeros((TOK, 2 * HD), F32)

        cross_out[way, step] = own_part(way, step, 3).astype(BF16)
        cross_copy(way, step).start()

    def reduce_copy(way, step, piece, near=None):
        span = slice(piece * PIECE, (piece + 1) * PIECE)
        if near is None:
            slot, target = step - 1, along(way)
        else:
            slot, target = 2 - near, (diagonal if piece == 2 else along)(way, near)
        return copy(
            ring_out.at[way, step, span],
            ring_in.at[way, slot, span],
            reduce_send.at[way, step, piece],
            reduce_recv.at[way, slot, piece],
            target,
        )

    def reduce_step(item, static=False):
        way, step = leaving(item)
        near = None
        if static and item >= ring - 5:
            near = 2 if item < ring - 3 else 1
        for piece in (0, 2, 1):
            span = slice(piece * PIECE, (piece + 1) * PIECE)
            summed = own_part(way, step, piece)
            if near != 1:

                @pl.when(step < half - way)
                def _():
                    reduce_copy(way, step + 1, piece).wait_recv()

                summed = summed + ring_in[way, step, span].astype(F32)
            if piece == 1:
                cross_copy(way, step).wait_recv()
                summed = summed + cross_in[way, step].astype(F32)
            ring_out[way, step, span] = summed.astype(BF16)
            reduce_copy(way, step, piece, near).start()

    def backward_step(count, carry):
        block = 2 + 3 * count
        backward_block(block)
        reduce_step(2 * count)
        backward_block(block + 1)
        reduce_step(2 * count + 1)
        backward_block(block + 2)
        return carry

    def reduce_only(item, carry):
        reduce_step(item)
        return carry

    rounds = (ring - 4) // 3
    reduced = 2 * rounds
    backward_block(0)
    backward_block(1)
    lax.fori_loop(0, rounds, backward_step, 0)
    backward_block(ring - 2)
    reduce_step(reduced, True)
    backward_block(ring - 1)

    kv_send[...] = own_part(1, 0, 2).astype(BF16)
    dkv_copy = copy_once(DKV_X, kv_send, kv_peer, across)
    dkv_copy.start()
    turn_back = [(xx, head) for xx in range(2) for head in range(2)]
    for block in range(8):
        span = slice(block * TOK, (block + 1) * TOK)
        dq_rows[span, :] = dq_cols[:, span].T
    dq_core_copies = [
        copy_once(
            number,
            dq_rows.at[rows((xx * 2 + 1 - c) * 2 * TOK, 2 * TOK)],
            dq_core.at[rows(xx * 2 * TOK, 2 * TOK)],
            other_core,
        )
        for xx, number in enumerate((DQ_C0, DQ_C1))
    ]
    for number in range(2):
        dq_core_copies[number].start()
    reduce_step(reduced + 1, True)

    def settle_gather(item, carry):
        way, step = gathered(item)
        relay_copy(way, step, z, x).wait_send()
        for piece in range(3):
            gather_copy(way, step, piece, z).wait_send()
        return carry

    def settle_reduce(item, carry):
        way, step = leaving(item)
        cross_copy(way, step).wait_send()

        @pl.when(step > 0)
        def _():
            for piece in range(3):
                reduce_copy(way, step, piece).wait_send()

        return carry

    lax.fori_loop(1, ring, settle_gather, 0)
    for number in range(2):
        dq_core_copies[number].wait_recv()
    dq_out[...] = dq_rows[relay_rows, :] + dq_core[peer_heads, :]
    dq_copy = copy_once(DQ_X, dq_out, dq_own.at[own_heads], across)
    dq_copy.start()
    dq_own[own_heads, :] = dq_rows[own_rows, :] + dq_core[own_heads, :]

    for xx, head in turn_back:
        cols = rows(((xx * 2 + c) * 2 + head) * TOK)
        att_rows[(xx * 2 + head) * TOK : (xx * 2 + head + 1) * TOK, :] = att_cols[:, cols].T
    att_copy = copy_once(ATT_X, att_rows.at[peer_heads], att_own.at[own_heads], across)
    att_copy.start()
    att_own[own_heads, :] = att_rows[own_heads, :]

    lax.fori_loop(reduced + 2, ring - 5, reduce_only, 0)
    for item in range(max(reduced + 2, ring - 5), ring - 1):
        reduce_step(item, True)
    lax.fori_loop(0, ring - 3, settle_reduce, 0)

    att_copy.wait_recv()
    result = codes_in[...].astype(F32)
    for head in range(4):
        span = slice(head * TOK, (head + 1) * TOK)
        result = result + dot(att_own[span, :], w_out[span, :])
    out_codes[...] = result.astype(BF16)

    dq_copy.wait_recv()
    normed_grad = jnp.zeros((TOK, w_query.shape[0]), F32)
    for head in range(4):
        span = slice(head * TOK, (head + 1) * TOK)
        lin_grad = norm_back(q_lin[:, span], q_gain[...], dq_own[span, :])
        normed_grad = normed_grad + dot_last(lin_grad, w_query[:, span])

    def ringed(piece):
        span = slice(piece * PIECE, (piece + 1) * PIECE)
        summed = 0.0
        for way, hops in reached:
            reduce_copy(way, hops, piece, hops).wait_recv()
            summed = summed + ring_in[way, 2 - hops, span].astype(F32)
        return summed

    cross_copy(1, 0).wait_recv()
    dkv_copy.wait_recv()
    first_part = own_part(1, 0, 0) + kv_peer[...].astype(F32)
    second_part = own_part(1, 0, 1) + cross_in[1, 0].astype(F32)
    kv_grad[:PIECE, :] = first_part + ringed(0) + ringed(2)
    kv_grad[PIECE:, :] = second_part + ringed(1)
    key_grad = norm_back(k_lin[...], k_gain[...], kv_grad[:, :HD])
    normed_grad = normed_grad + dot_last(key_grad, w_key[...])
    normed_grad = normed_grad + dot_last(kv_grad[:, HD:].astype(BF16), w_value[...])
    wide = codes_in[...].astype(F32)
    inv_norm = lax.rsqrt(jnp.sum(wide * wide, axis=-1, keepdims=True) / D + NORM_EPS)
    inner = jnp.sum(wide * normed_grad, axis=-1, keepdims=True)
    in_grads[...] = (
        grads_in[...].astype(F32)
        + inv_norm * normed_grad
        - wide * (inv_norm * inv_norm * inv_norm) * inner / D
    ).astype(BF16)

    for once in (codes_copy, grads_copy, kv_copy, acc_copy, stats_copy, att_copy, dq_copy, dkv_copy):
        once.wait_send()
    for once in (*q_copies, *do_copies, *dq_core_copies):
        once.wait_send()

    relay_copy(0, 0, z, x).wait_send()
    lax.fori_loop(ring - 3, ring, settle_reduce, 0)


def rope_tables(first_pos):
    half_dim = HD // 2
    exponent = jnp.arange(half_dim).astype(F32) * (2.0 / HD)
    frequency = jnp.power(F32(ROPE_BASE), -exponent)
    frequency = jnp.concatenate([frequency, frequency])
    shape = (TOK // 2, HD)
    lane = lax.broadcasted_iota(jnp.int32, shape, 1)
    offset = lax.broadcasted_iota(jnp.int32, shape, 0) + jnp.where(lane < half_dim, 0, TOK // 2)
    angles = (first_pos + offset).astype(F32) * frequency[None, :]
    return (jnp.cos(angles), jnp.sin(angles))


def local(
    sent_codes, start_codes, sent_grads, loss_grads, w_query, w_key, w_value, w_out, q_gain, k_gain
):
    ring = lax.axis_size("seq") // 4
    sections = lax.axis_size("section")
    steps = ring // 2 + 1
    width = start_codes.shape[1]
    cosines, sines = rope_tables(lax.axis_index("seq") * TOK)
    vmem = pltpu.VMEM
    dma = pltpu.SemaphoreType.DMA
    one_block = (TOK, width)
    heads = (4 * TOK, HD)
    all_rows = (8 * TOK, HD)
    columns = (HD, 8 * TOK)
    stat = (1, 8 * TOK)
    results = pl.pallas_call(
        functools.partial(kernel, ring, sections),
        out_shape=(jax.ShapeDtypeStruct(one_block, BF16),) * 2,
        in_specs=[pl.BlockSpec(memory_space=pltpu.HBM)] * 8 + [pl.BlockSpec(memory_space=vmem)] * 4,
        out_specs=(pl.BlockSpec(memory_space=vmem),) * 2,
        scratch_shapes=[
            vmem(w_query.shape[1:], BF16),
            vmem(w_key.shape[1:], BF16),
            vmem(w_value.shape[1:], BF16),
            vmem(w_out.shape[1:], BF16),
            vmem(one_block, BF16),
            vmem(one_block, BF16),
            vmem(one_block, BF16),
            vmem(one_block, BF16),
            vmem(one_block, BF16),
            vmem(one_block, BF16),
            vmem(one_block, BF16),
            vmem(one_block, BF16),
            vmem(one_block, F32),
            vmem((TOK, HD), F32),
            vmem(heads, BF16),
            vmem(all_rows, BF16),
            vmem(columns, BF16),
            vmem(heads, BF16),
            vmem(all_rows, BF16),
            vmem(columns, BF16),
            vmem((ring * 2 * TOK, 2 * HD), BF16),
            vmem((8, 8 * TOK), F32),
            vmem((8, 8 * TOK), F32),
            vmem(columns, F32),
            vmem(columns, F32),
            vmem(stat, F32),
            vmem(stat, F32),
            vmem(columns, BF16),
            vmem(heads, BF16),
            vmem(heads, BF16),
            vmem(columns, F32),
            vmem(all_rows, F32),
            vmem(heads, F32),
            vmem((2 * TOK, HD), F32),
            vmem(heads, F32),
            vmem((2, steps, 2 * TOK, 8 * TOK), F32),
            vmem((2, steps, 8, 8 * TOK), F32),
            vmem((2, steps, 2 * TOK, 2 * HD), F32),
            vmem((2, steps, 3 * PIECE, 2 * HD), BF16),
            vmem((2, steps, 3 * PIECE, 2 * HD), BF16),
            vmem((2, steps, PIECE, 2 * HD), BF16),
            vmem((2, steps, PIECE, 2 * HD), BF16),
            vmem((TOK, 2 * HD), F32),
            vmem((PIECE, 2 * HD), BF16),
            vmem((PIECE, 2 * HD), BF16),
            dma((16,)),
            dma((16,)),
            dma((2, steps, 3)),
            dma((2, steps, 3)),
            dma((2, steps, 3)),
            dma((2, steps, 3)),
            dma((2, steps)),
            dma((2, steps)),
            dma((2, steps)),
            dma((2, steps)),
            dma((8,)),
        ],
        compiler_params=pltpu.CompilerParams(
            collective_id=0, has_side_effects=True, vmem_limit_bytes=60 * 1024 * 1024
        ),
    )(
        sent_codes[0],
        start_codes,
        sent_grads[0],
        loss_grads,
        w_query[0],
        w_key[0],
        w_value[0],
        w_out[0],
        q_gain,
        k_gain,
        cosines,
        sines,
    )
    return (results[0][None], results[1][None])


def solution(mesh):
    in_specs = (
        P("section", "seq", None),
        P("seq", None),
        P("section", "seq", None),
        P("seq", None),
        P("section", None, None),
        P("section", None, None),
        P("section", None, None),
        P("section", None, None),
        P("section", None),
        P("section", None),
    )
    out_specs = (P("section", "seq", None), P("section", "seq", None))
    return jax.shard_map(local, mesh=mesh, in_specs=in_specs, out_specs=out_specs, check_vma=False)
```

```python
import functools

import jax
import jax.numpy as jnp
from jax import lax
from jax.experimental import pallas as pl
from jax.experimental.pallas import tpu as pltpu
from jax.sharding import PartitionSpec as P

D = 5120
ROPE_BASE = 1000000.0
NORM_EPS = 1e-06
MASK_FILL = -1e30
LOG2_E = 1.4426950408889634
MESH = pl.DeviceIdType.MESH
F32 = jnp.float32
BF16 = jnp.bfloat16
TOK = 128
HD = 128
PIECE = 64
CONTRACT_LAST = (((1,), (1,)), ((), ()))
CONTRACT_FIRST = (((0,), (0,)), ((), ()))

CODES, GRADS, KV_X, ATT_X, DQ_X, DKV_X, ACC_C, STATS_C, DQ_C0, DQ_C1 = range(10)
Q_X, Q_C, Q_R, DO_X, DO_C, DO_R = range(10, 16)


def dot(a, b):
    return jnp.dot(a, b, preferred_element_type=F32)


def dot_last(a, b):
    return lax.dot_general(a, b, CONTRACT_LAST, preferred_element_type=F32)


def dot_first(a, b):
    return lax.dot_general(a, b, CONTRACT_FIRST, preferred_element_type=F32)


def rows(start, count=TOK):
    return pl.ds(pl.multiple_of(start, TOK), count)


def kernel(
    ring,
    sections,
    sent_codes,
    start_codes,
    sent_grads,
    loss_grads,
    w_query_hbm,
    w_key_hbm,
    w_value_hbm,
    w_out_hbm,
    q_gain,
    k_gain,
    cosines,
    sines,
    out_codes,
    in_grads,
    w_query,
    w_key,
    w_value,
    w_out,
    codes_out,
    grads_out,
    codes_edge,
    grads_edge,
    codes_buf,
    grads_buf,
    codes_in,
    grads_in,
    q_lin,
    k_lin,
    q_own,
    q_rows,
    q_cols,
    do_own,
    do_rows,
    do_cols,
    kv,
    stats,
    stats_peer,
    acc,
    acc_peer,
    lse,
    delta,
    att_cols,
    att_rows,
    att_own,
    dq_cols,
    dq_rows,
    dq_core,
    dq_out,
    dq_own,
    kept_weights,
    kept_tops,
    part,
    ring_out,
    ring_in,
    cross_out,
    cross_in,
    kv_grad,
    kv_send,
    kv_peer,
    once_send,
    once_recv,
    gather_send,
    gather_recv,
    reduce_send,
    reduce_recv,
    relay_send,
    relay_recv,
    cross_send,
    cross_recv,
    load_sems,
):
    half = ring // 2
    sec = lax.axis_index("section")
    me = lax.axis_index("seq")
    x = lax.div(me, 2 * ring)
    z = lax.rem(lax.div(me, 2), ring)
    c = lax.rem(me, 2)

    def device(xx, zz, cc):
        return (sec, (xx * ring + zz) * 2 + cc)

    def along(way):
        return device(x, lax.rem(z + 1 + way * (ring - 2), ring), c)

    def diagonal(way):
        return device(1 - x, lax.rem(z + 1 + way * (ring - 2), ring), c)

    other_core = device(x, z, 1 - c)
    across = device(1 - x, z, c)
    next_section = (lax.rem(sec + 1, sections), me)
    last_section = (lax.rem(sec + sections - 1, sections), me)

    def copy(src, dst, send, recv, target):
        return pltpu.make_async_remote_copy(
            src_ref=src,
            dst_ref=dst,
            send_sem=send,
            recv_sem=recv,
            device_id=target,
            device_id_type=MESH,
        )

    def copy_once(number, src, dst, target):
        return copy(src, dst, once_send.at[number], once_recv.at[number], target)

    loads = [
        pltpu.make_async_copy(src, dst, load_sems.at[number])
        for number, (src, dst) in enumerate(
            (
                (sent_codes, codes_out),
                (start_codes, codes_edge),
                (w_key_hbm, w_key),
                (w_value_hbm, w_value),
                (w_query_hbm, w_query),
                (sent_grads, grads_out),
                (loss_grads, grads_edge),
                (w_out_hbm, w_out),
            )
        )
    ]
    for load in loads:
        load.start()

    barrier = pltpu.get_barrier_semaphore()
    partners = (along(0), along(1), diagonal(0), diagonal(1), other_core, across)
    for partner in (*partners, next_section, last_section):
        pl.semaphore_signal(barrier, inc=1, device_id=partner, device_id_type=MESH)
    pl.semaphore_wait(barrier, 8)

    codes_copy = copy_once(CODES, codes_out, codes_buf, next_section)
    grads_copy = copy_once(GRADS, grads_out, grads_buf, last_section)
    loads[0].wait()
    codes_copy.start()

    stats[...] = jnp.where(
        lax.broadcasted_iota(jnp.int32, stats.shape, 0) == 0, F32(MASK_FILL), F32(0.0)
    )
    acc[...] = jnp.zeros(acc.shape, F32)
    dq_cols[...] = jnp.zeros(dq_cols.shape, F32)
    for way, farthest in ((0, half), (1, half - 1)):
        ring_in[way, farthest] = jnp.zeros(ring_in.shape[2:], BF16)

    lane = lax.broadcasted_iota(jnp.int32, (TOK, HD), 1)
    first_half = lane < HD // 2

    def unpack_table(packed):
        turned = pltpu.roll(packed, HD // 2, 1)
        left = first_half[: TOK // 2]
        return jnp.concatenate(
            [jnp.where(left, packed, turned), jnp.where(left, turned, packed)], axis=0
        )

    cos = unpack_table(cosines[...])
    sin = unpack_table(sines[...])
    sin_turned = jnp.where(first_half, -sin, sin)

    def head_norm(tensor, gain):
        inv = lax.rsqrt(jnp.mean(tensor * tensor, axis=-1, keepdims=True) + NORM_EPS)
        hat = tensor * inv * gain
        return (hat * cos + pltpu.roll(hat, HD // 2, 1) * sin_turned).astype(BF16)

    def norm_back(tensor, gain, rot_grad):
        turned = pltpu.roll(rot_grad * sin, HD // 2, 1)
        hat_grad = rot_grad * cos + jnp.where(first_half, turned, -turned)
        inv = lax.rsqrt(jnp.mean(tensor * tensor, axis=-1, keepdims=True) + NORM_EPS)
        scaled = hat_grad * gain
        inner = jnp.mean(tensor * scaled, axis=-1, keepdims=True)
        return (inv * scaled - tensor * (inv * inv * inv) * inner).astype(BF16)

    def piece_of(piece, zz, xx=None):
        if xx is None:
            xx = x if piece < 2 else 1 - x
        start = (zz * 2 + xx) * TOK + piece % 2 * PIECE
        return kv.at[pl.ds(pl.multiple_of(start, PIECE), PIECE)]

    def place(way, step):
        return lax.rem(z + way * step + (1 - way) * (ring - step), ring)

    def gather_copy(way, step, piece, zz):
        ref = piece_of(piece, zz)
        sems = (gather_send.at[way, step, piece], gather_recv.at[way, step, piece])
        return copy(ref, ref, *sems, along(way))

    def relay_copy(way, step, zz, xx):
        ref = piece_of(3, zz, xx)
        return copy(ref, ref, relay_send.at[way, step], relay_recv.at[way, step], across)

    peer_heads = rows((1 - x) * 2 * TOK, 2 * TOK)
    own_heads = rows(x * 2 * TOK, 2 * TOK)
    own_rows = rows((x * 2 + c) * 2 * TOK, 2 * TOK)
    relay_rows = rows(((1 - x) * 2 + c) * 2 * TOK, 2 * TOK)

    def spread(number, src, dst):
        return (
            copy_once(number, src.at[peer_heads], dst.at[own_rows], across),
            copy_once(number + 1, src.at[own_heads], dst.at[own_rows], other_core),
            copy_once(number + 2, dst.at[relay_rows], dst.at[relay_rows], other_core),
        )

    q_copies = spread(Q_X, q_own, q_rows)
    do_copies = spread(DO_X, do_own, do_rows)

    def turn(src, dst):
        for block in range(src.shape[0] // TOK):
            span = slice(block * TOK, (block + 1) * TOK)
            dst[:, span] = src[span, :].T

    for load in loads[1:4]:
        load.wait()
    codes_copy.wait_recv()

    @pl.when(sec == 0)
    def _():
        codes_in[...] = codes_edge[...]

    @pl.when(sec != 0)
    def _():
        codes_in[...] = codes_buf[...]

    wide = codes_in[...].astype(F32)
    inv_norm = lax.rsqrt(jnp.sum(wide * wide, axis=-1, keepdims=True) / D + NORM_EPS)
    normed = (wide * inv_norm).astype(BF16)
    key_lin = dot(normed, w_key[...])
    k_lin[...] = key_lin
    own = rows((z * 2 + x) * TOK)
    kv[own, :HD] = head_norm(key_lin, k_gain[...])
    kv[own, HD:] = dot(normed, w_value[...]).astype(BF16)

    first_piece = piece_of(0, z, x)
    for piece in (1, 0):
        for way in range(2):
            gather_copy(way, 1, piece, z).start()
    for way in range(2):
        sems = (gather_send.at[way, 1, 2], gather_recv.at[way, 1, 2])
        copy(first_piece, first_piece, *sems, diagonal(way)).start()
    kv_copy = copy_once(KV_X, first_piece, first_piece, across)
    kv_copy.start()
    relay_copy(0, 0, z, x).start()

    loads[4].wait()
    q_lin[...] = dot(normed, w_query[...])
    for head in range(4):
        q_own[head * TOK : (head + 1) * TOK, :] = head_norm(
            q_lin[:, head * HD : (head + 1) * HD], q_gain[...]
        )
    q_copies[0].start()
    q_copies[1].start()
    q_rows[own_rows, :] = q_own[own_heads, :]

    loads[5].wait()
    grads_copy.start()

    scale = HD ** (-0.5)
    scale_two = scale * LOG2_E
    late = 4 * TOK

    wide_chain = 2 * TOK
    late_chains = (late, late + wide_chain)
    early_chains = (0, wide_chain)
    seen_chains = [(2 * TOK, col) for col in late_chains] + [(TOK, col) for col in early_chains]
    unseen_chains = [(TOK, col) for col in late_chains]

    def own_mask(keys, first_col):
        shape = (keys, wide_chain)
        key = lax.broadcasted_iota(jnp.int32, shape, 0)
        col = lax.broadcasted_iota(jnp.int32, shape, 1)
        query = (col & (TOK - 1)) + first_col % late // 2
        if first_col < late:
            return key + c * TOK <= query
        return (key < TOK) | (key - TOK + c * TOK <= query)

    def forward_chains(kept, step, zz, chains, masked):
        def raw_scores(keys, first_col):
            block = rows(zz * 2 * TOK, keys)
            return dot(kv[block, :HD], q_cols[:, first_col : first_col + wide_chain])

        following = raw_scores(*chains[0])
        for number, (keys, first_col) in enumerate(chains):
            scores = following * scale_two
            if number + 1 < len(chains):
                following = raw_scores(*chains[number + 1])
            span = slice(first_col, first_col + wide_chain)
            block = rows(zz * 2 * TOK, keys)
            if masked:
                scores = jnp.where(own_mask(keys, first_col), scores, 2 * MASK_FILL)
            top_old = stats[0:1, span]
            top_new = jnp.maximum(top_old, jnp.max(scores, axis=0, keepdims=True))
            weights = jnp.exp2(scores - top_new)
            kept_weights[kept, step, :keys, span] = weights
            kept_tops[kept, step, 0:1, span] = top_new
            shrink = jnp.exp2(top_old - top_new)
            stats[1:2, span] = stats[1:2, span] * shrink + jnp.sum(weights, axis=0, keepdims=True)
            acc[:, span] = acc[:, span] * shrink + dot_first(kv[block, HD:], weights.astype(BF16))
            stats[0:1, span] = top_new

    def arrive(way, step, forward):
        zz = place(way, step)
        for piece in (1, 0, 2):
            gather_copy(way, step, piece, zz).wait_recv()

            @pl.when(forward)
            def _():
                gather_copy(way, step + 1, piece, zz).start()

            if piece == 1:
                relay_copy(way, step, zz, x).start()

    def gathered(item):
        return lax.rem(item + 1, 2), lax.div(item + 1, 2)

    def forward_block(item):
        way, step = gathered(item)
        zz = place(way, step)
        relay_copy(way, step, zz, 1 - x).wait_recv()
        kept = way + lax.div(step, half)

        @pl.when(zz < z)
        def _():
            forward_chains(kept, step, zz, seen_chains, False)

        @pl.when(zz > z)
        def _():
            forward_chains(kept, step, zz, unseen_chains, False)

    def arrive_item(item):
        way, step = gathered(item)
        arrive(way, step, step < half - way)

    arrive_item(1)
    arrive_item(2)
    q_copies[0].wait_recv()
    q_copies[2].start()
    arrive_item(3)
    if ring > 4:
        arrive_item(4)
    q_copies[1].wait_recv()
    q_copies[2].wait_recv()
    turn(q_rows, q_cols)
    kv_copy.wait_recv()
    relay_copy(0, 0, z, 1 - x).wait_recv()
    forward_chains(0, 0, z, seen_chains, True)

    catches = (5 + ring // 4, 4 + ring // 2) if ring >= 16 else ()

    def caught_up(item):
        return sum(jnp.where(item >= catch, 1, 0) for catch in catches)

    def forward_step(item, carry):
        @pl.when(item < ring)
        def _():
            arrive_item(item)

        forward_block(item - 4 + caught_up(item - 1))

        if catches:

            @pl.when(caught_up(item) > caught_up(item - 1))
            def _():
                forward_block(item - 3 + caught_up(item - 1))

        @pl.when(item == 5 + ring // 4)
        def _():
            for load in loads[6:]:
                load.wait()
            grads_copy.wait_recv()

            @pl.when(sec == sections - 1)
            def _():
                grads_in[...] = grads_edge[...]

            @pl.when(sec != sections - 1)
            def _():
                grads_in[...] = grads_buf[...]

            grad_att = dot_last(grads_in[...], w_out[...]).astype(BF16)
            for head in range(4):
                do_own[head * TOK : (head + 1) * TOK, :] = grad_att[:, head * HD : (head + 1) * HD]
            do_copies[0].start()
            do_copies[1].start()
            do_rows[own_rows, :] = do_own[own_heads, :]

        @pl.when(item == 5 + ring // 2)
        def _():
            do_copies[0].wait_recv()
            do_copies[2].start()

        return carry

    lax.fori_loop(5, ring + 4 - len(catches), forward_step, 0)

    acc_copy = copy_once(ACC_C, acc, acc_peer, other_core)
    stats_copy = copy_once(STATS_C, stats, stats_peer, other_core)
    stats_copy.start()
    acc_copy.start()
    do_copies[1].wait_recv()
    do_copies[2].wait_recv()
    turn(do_rows, do_cols)
    stats_copy.wait_recv()
    top = jnp.maximum(stats[0:1, :], stats_peer[0:1, :])
    shrink = jnp.exp2(stats[0:1, :] - top)
    shrink_peer = jnp.exp2(stats_peer[0:1, :] - top)
    total = stats[1:2, :] * shrink + stats_peer[1:2, :] * shrink_peer
    lse[...] = top + jnp.log2(total)
    acc_copy.wait_recv()
    attended = (
        acc[...] * (shrink / total) + acc_peer[...] * (shrink_peer / total)
    ).astype(BF16)
    delta[...] = jnp.sum(
        do_cols[...].astype(F32) * attended.astype(F32), axis=0, keepdims=True
    )
    att_cols[...] = attended

    def backward_chains(way, step, zz, chains):
        def raw_grads(keys, first_col):
            block = rows(zz * 2 * TOK, keys)
            return dot(kv[block, HD:], do_cols[:, first_col : first_col + wide_chain])

        sums = {}

        def add(keys, name, term):
            sums[keys, name] = sums[keys, name] + term if (keys, name) in sums else term

        following = raw_grads(*chains[0])
        for number, (keys, first_col) in enumerate(chains):
            grad_prob = following
            if number + 1 < len(chains):
                following = raw_grads(*chains[number + 1])
            span = slice(first_col, first_col + wide_chain)
            block = rows(zz * 2 * TOK, keys)
            factor = jnp.exp2(kept_tops[1 - way, step, 0:1, span] - lse[:, span])
            probs = kept_weights[1 - way, step, :keys, span] * factor
            grad_score = (probs * (grad_prob - delta[:, span]) * scale).astype(BF16)
            add(keys, 0, dot(grad_score, q_rows[span, :]))
            add(keys, 1, dot(probs.astype(BF16), do_rows[span, :]))
            dq_cols[:, span] += dot_first(kv[block, :HD], grad_score)
        for name in range(2):
            cols = slice(name * HD, (name + 1) * HD)
            if (2 * TOK, name) in sums:
                both = sums[2 * TOK, name]
                part[way, step, :TOK, cols] = both[:TOK] + sums[TOK, name]
                part[way, step, TOK:, cols] = both[TOK:]
            else:
                part[way, step, :TOK, cols] = sums[TOK, name]
                part[way, step, TOK:, cols] = jnp.zeros((TOK, HD), F32)

    def leaving(item):
        return lax.rem(item, 2), half - lax.div(item + 1, 2)

    def own_part(way, step, piece):
        xx = x if piece < 2 else 1 - x
        return part[way, step, pl.ds(pl.multiple_of(xx * TOK + piece % 2 * PIECE, PIECE), PIECE), :]

    def cross_copy(way, step):
        return copy(
            cross_out.at[way, step],
            cross_in.at[way, step],
            cross_send.at[way, step],
            cross_recv.at[way, step],
            across,
        )

    def backward_block(item):
        way, step = leaving(item)
        zz = place(1 - way, step)

        @pl.when(zz <= z)
        def _():
            backward_chains(way, step, zz, seen_chains)

        @pl.when(zz > z)
        def _():
            backward_chains(way, step, zz, unseen_chains)

        cross_out[way, step] = own_part(way, step, 3).astype(BF16)
        cross_copy(way, step).start()

    def reduce_copy(way, step, piece, target=None):
        span = slice(piece * PIECE, (piece + 1) * PIECE)
        return copy(
            ring_out.at[way, step, span],
            ring_in.at[way, step - 1, span],
            reduce_send.at[way, step, piece],
            reduce_recv.at[way, step - 1, piece],
            along(way) if target is None else target,
        )

    def reduce_step(item, last=False):
        way, step = leaving(item)
        for piece in (0, 2, 1):

            @pl.when(step < half - way)
            def _():
                reduce_copy(way, step + 1, piece).wait_recv()

            span = slice(piece * PIECE, (piece + 1) * PIECE)
            summed = own_part(way, step, piece) + ring_in[way, step, span].astype(F32)
            if piece == 1:
                cross_copy(way, step).wait_recv()
                summed = summed + cross_in[way, step].astype(F32)
            ring_out[way, step, span] = summed.astype(BF16)
            target = diagonal(way) if last and piece == 2 else None
            reduce_copy(way, step, piece, target).start()

    def backward_step(count, carry):
        block = 2 + 3 * count
        backward_block(block)
        reduce_step(2 * count)
        backward_block(block + 1)
        reduce_step(2 * count + 1)
        backward_block(block + 2)
        return carry

    def reduce_only(item, carry):
        reduce_step(item)
        return carry

    rounds = (ring - 4) // 3
    reduced = 2 * rounds
    backward_block(0)
    backward_block(1)
    lax.fori_loop(0, rounds, backward_step, 0)
    backward_block(ring - 2)
    reduce_step(reduced)
    backward_block(ring - 1)

    kv_send[...] = own_part(1, 0, 2).astype(BF16)
    dkv_copy = copy_once(DKV_X, kv_send, kv_peer, across)
    dkv_copy.start()
    turn_back = [(xx, head) for xx in range(2) for head in range(2)]
    for block in range(8):
        span = slice(block * TOK, (block + 1) * TOK)
        dq_rows[span, :] = dq_cols[:, span].T
    dq_core_copies = [
        copy_once(
            number,
            dq_rows.at[rows((xx * 2 + 1 - c) * 2 * TOK, 2 * TOK)],
            dq_core.at[rows(xx * 2 * TOK, 2 * TOK)],
            other_core,
        )
        for xx, number in enumerate((DQ_C0, DQ_C1))
    ]
    for number in range(2):
        dq_core_copies[number].start()
    reduce_step(reduced + 1, reduced + 1 >= ring - 3)

    def settle_gather(item, carry):
        way, step = gathered(item)
        relay_copy(way, step, z, x).wait_send()
        for piece in range(3):
            gather_copy(way, step, piece, z).wait_send()
        return carry

    def settle_reduce(item, carry):
        way, step = leaving(item)
        cross_copy(way, step).wait_send()

        @pl.when(step > 0)
        def _():
            for piece in range(3):
                reduce_copy(way, step, piece).wait_send()

        return carry

    lax.fori_loop(1, ring, settle_gather, 0)
    for number in range(2):
        dq_core_copies[number].wait_recv()
    dq_out[...] = dq_rows[relay_rows, :] + dq_core[peer_heads, :]
    dq_copy = copy_once(DQ_X, dq_out, dq_own.at[own_heads], across)
    dq_copy.start()
    dq_own[own_heads, :] = dq_rows[own_rows, :] + dq_core[own_heads, :]

    for xx, head in turn_back:
        cols = rows(((xx * 2 + c) * 2 + head) * TOK)
        att_rows[(xx * 2 + head) * TOK : (xx * 2 + head + 1) * TOK, :] = att_cols[:, cols].T
    att_copy = copy_once(ATT_X, att_rows.at[peer_heads], att_own.at[own_heads], across)
    att_copy.start()
    att_own[own_heads, :] = att_rows[own_heads, :]

    lax.fori_loop(reduced + 2, ring - 3, reduce_only, 0)
    for item in range(max(reduced + 2, ring - 3), ring - 1):
        reduce_step(item, True)
    lax.fori_loop(0, ring - 3, settle_reduce, 0)

    att_copy.wait_recv()
    result = codes_in[...].astype(F32)
    for head in range(4):
        span = slice(head * TOK, (head + 1) * TOK)
        result = result + dot(att_own[span, :], w_out[span, :])
    out_codes[...] = result.astype(BF16)

    dq_copy.wait_recv()
    normed_grad = jnp.zeros((TOK, w_query.shape[0]), F32)
    for head in range(4):
        span = slice(head * TOK, (head + 1) * TOK)
        lin_grad = norm_back(q_lin[:, span], q_gain[...], dq_own[span, :])
        normed_grad = normed_grad + dot_last(lin_grad, w_query[:, span])

    def ringed(piece):
        for way in range(2):
            reduce_copy(way, 1, piece).wait_recv()
        span = slice(piece * PIECE, (piece + 1) * PIECE)
        return ring_in[0, 0, span].astype(F32) + ring_in[1, 0, span].astype(F32)

    cross_copy(1, 0).wait_recv()
    dkv_copy.wait_recv()
    first_part = own_part(1, 0, 0) + kv_peer[...].astype(F32)
    second_part = own_part(1, 0, 1) + cross_in[1, 0].astype(F32)
    kv_grad[:PIECE, :] = first_part + ringed(0) + ringed(2)
    kv_grad[PIECE:, :] = second_part + ringed(1)
    key_grad = norm_back(k_lin[...], k_gain[...], kv_grad[:, :HD])
    normed_grad = normed_grad + dot_last(key_grad, w_key[...])
    normed_grad = normed_grad + dot_last(kv_grad[:, HD:].astype(BF16), w_value[...])
    wide = codes_in[...].astype(F32)
    inv_norm = lax.rsqrt(jnp.sum(wide * wide, axis=-1, keepdims=True) / D + NORM_EPS)
    inner = jnp.sum(wide * normed_grad, axis=-1, keepdims=True)
    in_grads[...] = (
        grads_in[...].astype(F32)
        + inv_norm * normed_grad
        - wide * (inv_norm * inv_norm * inv_norm) * inner / D
    ).astype(BF16)

    for once in (codes_copy, grads_copy, kv_copy, acc_copy, stats_copy, att_copy, dq_copy, dkv_copy):
        once.wait_send()
    for once in (*q_copies, *do_copies, *dq_core_copies):
        once.wait_send()

    relay_copy(0, 0, z, x).wait_send()
    lax.fori_loop(ring - 3, ring, settle_reduce, 0)


def rope_tables(first_pos):
    half_dim = HD // 2
    exponent = jnp.arange(half_dim).astype(F32) * (2.0 / HD)
    frequency = jnp.power(F32(ROPE_BASE), -exponent)
    frequency = jnp.concatenate([frequency, frequency])
    shape = (TOK // 2, HD)
    lane = lax.broadcasted_iota(jnp.int32, shape, 1)
    offset = lax.broadcasted_iota(jnp.int32, shape, 0) + jnp.where(lane < half_dim, 0, TOK // 2)
    angles = (first_pos + offset).astype(F32) * frequency[None, :]
    return (jnp.cos(angles), jnp.sin(angles))


def local(
    sent_codes, start_codes, sent_grads, loss_grads, w_query, w_key, w_value, w_out, q_gain, k_gain
):
    ring = lax.axis_size("seq") // 4
    sections = lax.axis_size("section")
    steps = ring // 2 + 1
    width = start_codes.shape[1]
    cosines, sines = rope_tables(lax.axis_index("seq") * TOK)
    vmem = pltpu.VMEM
    dma = pltpu.SemaphoreType.DMA
    one_block = (TOK, width)
    heads = (4 * TOK, HD)
    all_rows = (8 * TOK, HD)
    columns = (HD, 8 * TOK)
    stat = (1, 8 * TOK)
    results = pl.pallas_call(
        functools.partial(kernel, ring, sections),
        out_shape=(jax.ShapeDtypeStruct(one_block, BF16),) * 2,
        in_specs=[pl.BlockSpec(memory_space=pltpu.HBM)] * 8 + [pl.BlockSpec(memory_space=vmem)] * 4,
        out_specs=(pl.BlockSpec(memory_space=vmem),) * 2,
        scratch_shapes=[
            vmem(w_query.shape[1:], BF16),
            vmem(w_key.shape[1:], BF16),
            vmem(w_value.shape[1:], BF16),
            vmem(w_out.shape[1:], BF16),
            vmem(one_block, BF16),
            vmem(one_block, BF16),
            vmem(one_block, BF16),
            vmem(one_block, BF16),
            vmem(one_block, BF16),
            vmem(one_block, BF16),
            vmem(one_block, BF16),
            vmem(one_block, BF16),
            vmem(one_block, F32),
            vmem((TOK, HD), F32),
            vmem(heads, BF16),
            vmem(all_rows, BF16),
            vmem(columns, BF16),
            vmem(heads, BF16),
            vmem(all_rows, BF16),
            vmem(columns, BF16),
            vmem((ring * 2 * TOK, 2 * HD), BF16),
            vmem((8, 8 * TOK), F32),
            vmem((8, 8 * TOK), F32),
            vmem(columns, F32),
            vmem(columns, F32),
            vmem(stat, F32),
            vmem(stat, F32),
            vmem(columns, BF16),
            vmem(heads, BF16),
            vmem(heads, BF16),
            vmem(columns, F32),
            vmem(all_rows, F32),
            vmem(heads, F32),
            vmem((2 * TOK, HD), F32),
            vmem(heads, F32),
            vmem((2, steps, 2 * TOK, 8 * TOK), F32),
            vmem((2, steps, 8, 8 * TOK), F32),
            vmem((2, steps, 2 * TOK, 2 * HD), F32),
            vmem((2, steps, 3 * PIECE, 2 * HD), BF16),
            vmem((2, steps, 3 * PIECE, 2 * HD), BF16),
            vmem((2, steps, PIECE, 2 * HD), BF16),
            vmem((2, steps, PIECE, 2 * HD), BF16),
            vmem((TOK, 2 * HD), F32),
            vmem((PIECE, 2 * HD), BF16),
            vmem((PIECE, 2 * HD), BF16),
            dma((16,)),
            dma((16,)),
            dma((2, steps, 3)),
            dma((2, steps, 3)),
            dma((2, steps, 3)),
            dma((2, steps, 3)),
            dma((2, steps)),
            dma((2, steps)),
            dma((2, steps)),
            dma((2, steps)),
            dma((8,)),
        ],
        compiler_params=pltpu.CompilerParams(
            collective_id=0, has_side_effects=True, vmem_limit_bytes=60 * 1024 * 1024
        ),
    )(
        sent_codes[0],
        start_codes,
        sent_grads[0],
        loss_grads,
        w_query[0],
        w_key[0],
        w_value[0],
        w_out[0],
        q_gain,
        k_gain,
        cosines,
        sines,
    )
    return (results[0][None], results[1][None])


def solution(mesh):
    in_specs = (
        P("section", "seq", None),
        P("seq", None),
        P("section", "seq", None),
        P("seq", None),
        P("section", None, None),
        P("section", None, None),
        P("section", None, None),
        P("section", None, None),
        P("section", None),
        P("section", None),
    )
    out_specs = (P("section", "seq", None), P("section", "seq", None))
    return jax.shard_map(local, mesh=mesh, in_specs=in_specs, out_specs=out_specs, check_vma=False)
```

```python
import functools

import jax
import jax.numpy as jnp
from jax import lax
from jax.experimental import pallas as pl
from jax.experimental.pallas import tpu as pltpu
from jax.sharding import PartitionSpec as P

D = 5120
ROPE_BASE = 1000000.0
NORM_EPS = 1e-06
MASK_FILL = -1e30
LOG2_E = 1.4426950408889634
MESH = pl.DeviceIdType.MESH
F32 = jnp.float32
BF16 = jnp.bfloat16
TOK = 128
HD = 128
PIECE = 64
CONTRACT_LAST = (((1,), (1,)), ((), ()))
CONTRACT_FIRST = (((0,), (0,)), ((), ()))

CODES, GRADS, KV_X, ATT_X, DQ_X, DKV_X, ACC_C, STATS_C, DQ_C0, DQ_C1 = range(10)
Q_X, Q_C, Q_R, DO_X, DO_C, DO_R = range(10, 16)


def dot(a, b):
    return jnp.dot(a, b, preferred_element_type=F32)


def dot_last(a, b):
    return lax.dot_general(a, b, CONTRACT_LAST, preferred_element_type=F32)


def dot_first(a, b):
    return lax.dot_general(a, b, CONTRACT_FIRST, preferred_element_type=F32)


def rows(start, count=TOK):
    return pl.ds(pl.multiple_of(start, TOK), count)


def kernel(
    ring,
    sections,
    sent_codes,
    start_codes,
    sent_grads,
    loss_grads,
    w_query_hbm,
    w_key_hbm,
    w_value_hbm,
    w_out_hbm,
    q_gain,
    k_gain,
    cosines,
    sines,
    out_codes,
    in_grads,
    w_query,
    w_key,
    w_value,
    w_out,
    codes_out,
    grads_out,
    codes_edge,
    grads_edge,
    codes_buf,
    grads_buf,
    codes_in,
    grads_in,
    q_lin,
    k_lin,
    q_own,
    q_rows,
    q_cols,
    do_own,
    do_rows,
    do_cols,
    kv,
    stats,
    stats_peer,
    acc,
    acc_peer,
    lse,
    delta,
    att_cols,
    att_rows,
    att_own,
    dq_cols,
    dq_rows,
    dq_core,
    dq_out,
    dq_own,
    kept_weights,
    kept_tops,
    part,
    ring_out,
    ring_in,
    cross_out,
    cross_in,
    kv_grad,
    kv_send,
    kv_peer,
    once_send,
    once_recv,
    gather_send,
    gather_recv,
    reduce_send,
    reduce_recv,
    relay_send,
    relay_recv,
    cross_send,
    cross_recv,
    load_sems,
):
    half = ring // 2
    sec = lax.axis_index("section")
    me = lax.axis_index("seq")
    x = lax.div(me, 2 * ring)
    z = lax.rem(lax.div(me, 2), ring)
    c = lax.rem(me, 2)

    def device(xx, zz, cc):
        return (sec, (xx * ring + zz) * 2 + cc)

    def along(way):
        return device(x, lax.rem(z + 1 + way * (ring - 2), ring), c)

    def diagonal(way):
        return device(1 - x, lax.rem(z + 1 + way * (ring - 2), ring), c)

    other_core = device(x, z, 1 - c)
    across = device(1 - x, z, c)
    next_section = (lax.rem(sec + 1, sections), me)
    last_section = (lax.rem(sec + sections - 1, sections), me)

    def copy(src, dst, send, recv, target):
        return pltpu.make_async_remote_copy(
            src_ref=src,
            dst_ref=dst,
            send_sem=send,
            recv_sem=recv,
            device_id=target,
            device_id_type=MESH,
        )

    def copy_once(number, src, dst, target):
        return copy(src, dst, once_send.at[number], once_recv.at[number], target)

    loads = [
        pltpu.make_async_copy(src, dst, load_sems.at[number])
        for number, (src, dst) in enumerate(
            (
                (sent_codes, codes_out),
                (start_codes, codes_edge),
                (w_key_hbm, w_key),
                (w_value_hbm, w_value),
                (w_query_hbm, w_query),
                (sent_grads, grads_out),
                (loss_grads, grads_edge),
                (w_out_hbm, w_out),
            )
        )
    ]
    for load in loads:
        load.start()

    barrier = pltpu.get_barrier_semaphore()
    partners = (along(0), along(1), diagonal(0), diagonal(1), other_core, across)
    for partner in (*partners, next_section, last_section):
        pl.semaphore_signal(barrier, inc=1, device_id=partner, device_id_type=MESH)
    pl.semaphore_wait(barrier, 8)

    codes_copy = copy_once(CODES, codes_out, codes_buf, next_section)
    grads_copy = copy_once(GRADS, grads_out, grads_buf, last_section)
    loads[0].wait()
    codes_copy.start()

    stats[...] = jnp.where(
        lax.broadcasted_iota(jnp.int32, stats.shape, 0) == 0, F32(MASK_FILL), F32(0.0)
    )
    acc[...] = jnp.zeros(acc.shape, F32)
    dq_cols[...] = jnp.zeros(dq_cols.shape, F32)
    for way, farthest in ((0, half), (1, half - 1)):
        ring_in[way, farthest] = jnp.zeros(ring_in.shape[2:], BF16)

    lane = lax.broadcasted_iota(jnp.int32, (TOK, HD), 1)
    first_half = lane < HD // 2

    def unpack_table(packed):
        turned = pltpu.roll(packed, HD // 2, 1)
        left = first_half[: TOK // 2]
        return jnp.concatenate(
            [jnp.where(left, packed, turned), jnp.where(left, turned, packed)], axis=0
        )

    cos = unpack_table(cosines[...])
    sin = unpack_table(sines[...])
    sin_turned = jnp.where(first_half, -sin, sin)

    def head_norm(tensor, gain):
        inv = lax.rsqrt(jnp.mean(tensor * tensor, axis=-1, keepdims=True) + NORM_EPS)
        hat = tensor * inv * gain
        return (hat * cos + pltpu.roll(hat, HD // 2, 1) * sin_turned).astype(BF16)

    def norm_back(tensor, gain, rot_grad):
        turned = pltpu.roll(rot_grad * sin, HD // 2, 1)
        hat_grad = rot_grad * cos + jnp.where(first_half, turned, -turned)
        inv = lax.rsqrt(jnp.mean(tensor * tensor, axis=-1, keepdims=True) + NORM_EPS)
        scaled = hat_grad * gain
        inner = jnp.mean(tensor * scaled, axis=-1, keepdims=True)
        return (inv * scaled - tensor * (inv * inv * inv) * inner).astype(BF16)

    def piece_of(piece, zz, xx=None):
        if xx is None:
            xx = x if piece == 0 else 1 - x
        start = (zz * 2 + xx) * TOK + piece % 2 * PIECE
        return kv.at[pl.ds(pl.multiple_of(start, PIECE), TOK if piece == 0 else PIECE)]

    def place(way, step):
        return lax.rem(z + way * step + (1 - way) * (ring - step), ring)

    def gather_copy(way, step, piece, zz):
        ref = piece_of(piece, zz)
        sems = (gather_send.at[way, step, piece], gather_recv.at[way, step, piece])
        return copy(ref, ref, *sems, along(way))

    def relay_copy(way, step, zz, xx):
        ref = piece_of(3, zz, xx)
        return copy(ref, ref, relay_send.at[way, step], relay_recv.at[way, step], across)

    peer_heads = rows((1 - x) * 2 * TOK, 2 * TOK)
    own_heads = rows(x * 2 * TOK, 2 * TOK)
    own_rows = rows((x * 2 + c) * 2 * TOK, 2 * TOK)
    relay_rows = rows(((1 - x) * 2 + c) * 2 * TOK, 2 * TOK)

    def spread(number, src, dst):
        return (
            copy_once(number, src.at[peer_heads], dst.at[own_rows], across),
            copy_once(number + 1, src.at[own_heads], dst.at[own_rows], other_core),
            copy_once(number + 2, dst.at[relay_rows], dst.at[relay_rows], other_core),
        )

    q_copies = spread(Q_X, q_own, q_rows)
    do_copies = spread(DO_X, do_own, do_rows)

    def turn(src, dst):
        for block in range(src.shape[0] // TOK):
            span = slice(block * TOK, (block + 1) * TOK)
            dst[:, span] = src[span, :].T

    for load in loads[1:4]:
        load.wait()
    codes_copy.wait_recv()

    @pl.when(sec == 0)
    def _():
        codes_in[...] = codes_edge[...]

    @pl.when(sec != 0)
    def _():
        codes_in[...] = codes_buf[...]

    wide = codes_in[...].astype(F32)
    inv_norm = lax.rsqrt(jnp.sum(wide * wide, axis=-1, keepdims=True) / D + NORM_EPS)
    normed = (wide * inv_norm).astype(BF16)
    key_lin = dot(normed, w_key[...])
    k_lin[...] = key_lin
    own = rows((z * 2 + x) * TOK)
    kv[own, :HD] = head_norm(key_lin, k_gain[...])
    kv[own, HD:] = dot(normed, w_value[...]).astype(BF16)

    first_piece = piece_of(2, z, x)
    for way in range(2):
        gather_copy(way, 1, 0, z).start()
    for way in range(2):
        sems = (gather_send.at[way, 1, 2], gather_recv.at[way, 1, 2])
        copy(first_piece, first_piece, *sems, diagonal(way)).start()
    kv_copy = copy_once(KV_X, first_piece, first_piece, across)
    kv_copy.start()
    relay_copy(0, 0, z, x).start()

    loads[4].wait()
    q_lin[...] = dot(normed, w_query[...])
    for head in range(4):
        q_own[head * TOK : (head + 1) * TOK, :] = head_norm(
            q_lin[:, head * HD : (head + 1) * HD], q_gain[...]
        )
    q_copies[0].start()
    q_copies[1].start()
    q_rows[own_rows, :] = q_own[own_heads, :]

    loads[5].wait()
    grads_copy.start()

    scale = HD ** (-0.5)
    scale_two = scale * LOG2_E
    late = 4 * TOK

    wide_chain = 2 * TOK
    late_chains = (late, late + wide_chain)
    early_chains = (0, wide_chain)
    seen_chains = [(2 * TOK, col) for col in late_chains] + [(TOK, col) for col in early_chains]
    unseen_chains = [(TOK, col) for col in late_chains]

    def own_mask(keys, first_col):
        shape = (keys, wide_chain)
        key = lax.broadcasted_iota(jnp.int32, shape, 0)
        col = lax.broadcasted_iota(jnp.int32, shape, 1)
        query = (col & (TOK - 1)) + first_col % late // 2
        if first_col < late:
            return key + c * TOK <= query
        return (key < TOK) | (key - TOK + c * TOK <= query)

    def forward_chains(kept, step, zz, chains, masked):
        def raw_scores(keys, first_col):
            block = rows(zz * 2 * TOK, keys)
            return dot(kv[block, :HD], q_cols[:, first_col : first_col + wide_chain])

        following = raw_scores(*chains[0])
        for number, (keys, first_col) in enumerate(chains):
            scores = following * scale_two
            if number + 1 < len(chains):
                following = raw_scores(*chains[number + 1])
            span = slice(first_col, first_col + wide_chain)
            block = rows(zz * 2 * TOK, keys)
            if masked:
                scores = jnp.where(own_mask(keys, first_col), scores, 2 * MASK_FILL)
            top_old = stats[0:1, span]
            top_new = jnp.maximum(top_old, jnp.max(scores, axis=0, keepdims=True))
            weights = jnp.exp2(scores - top_new)
            kept_weights[kept, step, :keys, span] = weights
            kept_tops[kept, step, 0:1, span] = top_new
            shrink = jnp.exp2(top_old - top_new)
            stats[1:2, span] = stats[1:2, span] * shrink + jnp.sum(weights, axis=0, keepdims=True)
            acc[:, span] = acc[:, span] * shrink + dot_first(kv[block, HD:], weights.astype(BF16))
            stats[0:1, span] = top_new

    def arrive(way, step, forward):
        zz = place(way, step)
        for piece in (0, 2):
            gather_copy(way, step, piece, zz).wait_recv()

            @pl.when(forward)
            def _():
                gather_copy(way, step + 1, piece, zz).start()

            if piece == 0:
                relay_copy(way, step, zz, x).start()

    def gathered(item):
        return lax.rem(item + 1, 2), lax.div(item + 1, 2)

    def forward_block(item):
        way, step = gathered(item)
        zz = place(way, step)
        relay_copy(way, step, zz, 1 - x).wait_recv()
        kept = way + lax.div(step, half)

        @pl.when(zz < z)
        def _():
            forward_chains(kept, step, zz, seen_chains, False)

        @pl.when(zz > z)
        def _():
            forward_chains(kept, step, zz, unseen_chains, False)

    def arrive_item(item):
        way, step = gathered(item)
        arrive(way, step, step < half - way)

    arrive_item(1)
    arrive_item(2)
    q_copies[0].wait_recv()
    q_copies[2].start()
    arrive_item(3)
    if ring > 4:
        arrive_item(4)
    q_copies[1].wait_recv()
    q_copies[2].wait_recv()
    turn(q_rows, q_cols)
    kv_copy.wait_recv()
    relay_copy(0, 0, z, 1 - x).wait_recv()
    forward_chains(0, 0, z, seen_chains, True)

    catches = (5 + ring // 4, 4 + ring // 2) if ring >= 16 else ()

    def caught_up(item):
        return sum(jnp.where(item >= catch, 1, 0) for catch in catches)

    def forward_step(item, carry):
        @pl.when(item < ring)
        def _():
            arrive_item(item)

        forward_block(item - 4 + caught_up(item - 1))

        if catches:

            @pl.when(caught_up(item) > caught_up(item - 1))
            def _():
                forward_block(item - 3 + caught_up(item - 1))

        @pl.when(item == 5 + ring // 4)
        def _():
            for load in loads[6:]:
                load.wait()
            grads_copy.wait_recv()

            @pl.when(sec == sections - 1)
            def _():
                grads_in[...] = grads_edge[...]

            @pl.when(sec != sections - 1)
            def _():
                grads_in[...] = grads_buf[...]

            grad_att = dot_last(grads_in[...], w_out[...]).astype(BF16)
            for head in range(4):
                do_own[head * TOK : (head + 1) * TOK, :] = grad_att[:, head * HD : (head + 1) * HD]
            do_copies[0].start()
            do_copies[1].start()
            do_rows[own_rows, :] = do_own[own_heads, :]

        @pl.when(item == 5 + ring // 2)
        def _():
            do_copies[0].wait_recv()
            do_copies[2].start()

        return carry

    lax.fori_loop(5, ring + 4 - len(catches), forward_step, 0)

    acc_copy = copy_once(ACC_C, acc, acc_peer, other_core)
    stats_copy = copy_once(STATS_C, stats, stats_peer, other_core)
    stats_copy.start()
    acc_copy.start()
    do_copies[1].wait_recv()
    do_copies[2].wait_recv()
    turn(do_rows, do_cols)
    stats_copy.wait_recv()
    top = jnp.maximum(stats[0:1, :], stats_peer[0:1, :])
    shrink = jnp.exp2(stats[0:1, :] - top)
    shrink_peer = jnp.exp2(stats_peer[0:1, :] - top)
    total = stats[1:2, :] * shrink + stats_peer[1:2, :] * shrink_peer
    lse[...] = top + jnp.log2(total)
    acc_copy.wait_recv()
    attended = (
        acc[...] * (shrink / total) + acc_peer[...] * (shrink_peer / total)
    ).astype(BF16)
    delta[...] = jnp.sum(
        do_cols[...].astype(F32) * attended.astype(F32), axis=0, keepdims=True
    )
    att_cols[...] = attended

    def backward_chains(way, step, zz, chains):
        def raw_grads(keys, first_col):
            block = rows(zz * 2 * TOK, keys)
            return dot(kv[block, HD:], do_cols[:, first_col : first_col + wide_chain])

        sums = {}

        def add(keys, name, term):
            sums[keys, name] = sums[keys, name] + term if (keys, name) in sums else term

        following = raw_grads(*chains[0])
        for number, (keys, first_col) in enumerate(chains):
            grad_prob = following
            if number + 1 < len(chains):
                following = raw_grads(*chains[number + 1])
            span = slice(first_col, first_col + wide_chain)
            block = rows(zz * 2 * TOK, keys)
            factor = jnp.exp2(kept_tops[1 - way, step, 0:1, span] - lse[:, span])
            probs = kept_weights[1 - way, step, :keys, span] * factor
            grad_score = (probs * (grad_prob - delta[:, span]) * scale).astype(BF16)
            add(keys, 0, dot(grad_score, q_rows[span, :]))
            add(keys, 1, dot(probs.astype(BF16), do_rows[span, :]))
            dq_cols[:, span] += dot_first(kv[block, :HD], grad_score)
        for name in range(2):
            cols = slice(name * HD, (name + 1) * HD)
            if (2 * TOK, name) in sums:
                both = sums[2 * TOK, name]
                part[way, step, :TOK, cols] = both[:TOK] + sums[TOK, name]
                part[way, step, TOK:, cols] = both[TOK:]
            else:
                part[way, step, :TOK, cols] = sums[TOK, name]
                part[way, step, TOK:, cols] = jnp.zeros((TOK, HD), F32)

    def leaving(item):
        return lax.rem(item, 2), half - lax.div(item + 1, 2)

    def own_part(way, step, piece):
        xx = x if piece < 2 else 1 - x
        return part[way, step, pl.ds(pl.multiple_of(xx * TOK + piece % 2 * PIECE, PIECE), PIECE), :]

    def cross_copy(way, step):
        return copy(
            cross_out.at[way, step],
            cross_in.at[way, step],
            cross_send.at[way, step],
            cross_recv.at[way, step],
            across,
        )

    def backward_block(item):
        way, step = leaving(item)
        zz = place(1 - way, step)

        @pl.when(zz <= z)
        def _():
            backward_chains(way, step, zz, seen_chains)

        @pl.when(zz > z)
        def _():
            backward_chains(way, step, zz, unseen_chains)

        cross_out[way, step] = own_part(way, step, 3).astype(BF16)
        cross_copy(way, step).start()

    def reduce_copy(way, step, piece, target=None):
        span = slice(0, TOK) if piece == 0 else slice(TOK, TOK + PIECE)
        return copy(
            ring_out.at[way, step, span],
            ring_in.at[way, step - 1, span],
            reduce_send.at[way, step, piece],
            reduce_recv.at[way, step - 1, piece],
            along(way) if target is None else target,
        )

    def reduce_step(item, last=False):
        way, step = leaving(item)
        for piece in (2, 0):

            @pl.when(step < half - way)
            def _():
                reduce_copy(way, step + 1, piece).wait_recv()

            for part_piece in (2,) if piece == 2 else (0, 1):
                span = slice(part_piece * PIECE, (part_piece + 1) * PIECE)
                summed = own_part(way, step, part_piece) + ring_in[way, step, span].astype(F32)
                if part_piece == 1:
                    cross_copy(way, step).wait_recv()
                    summed = summed + cross_in[way, step].astype(F32)
                ring_out[way, step, span] = summed.astype(BF16)
            target = diagonal(way) if last and piece == 2 else None
            reduce_copy(way, step, piece, target).start()

    def backward_step(count, carry):
        block = 2 + 3 * count
        backward_block(block)
        reduce_step(2 * count)
        backward_block(block + 1)
        reduce_step(2 * count + 1)
        backward_block(block + 2)
        return carry

    def reduce_only(item, carry):
        reduce_step(item)
        return carry

    rounds = (ring - 4) // 3
    reduced = 2 * rounds
    backward_block(0)
    backward_block(1)
    lax.fori_loop(0, rounds, backward_step, 0)
    backward_block(ring - 2)
    reduce_step(reduced)
    backward_block(ring - 1)

    kv_send[...] = own_part(1, 0, 2).astype(BF16)
    dkv_copy = copy_once(DKV_X, kv_send, kv_peer, across)
    dkv_copy.start()
    turn_back = [(xx, head) for xx in range(2) for head in range(2)]
    for block in range(8):
        span = slice(block * TOK, (block + 1) * TOK)
        dq_rows[span, :] = dq_cols[:, span].T
    dq_core_copies = [
        copy_once(
            number,
            dq_rows.at[rows((xx * 2 + 1 - c) * 2 * TOK, 2 * TOK)],
            dq_core.at[rows(xx * 2 * TOK, 2 * TOK)],
            other_core,
        )
        for xx, number in enumerate((DQ_C0, DQ_C1))
    ]
    for number in range(2):
        dq_core_copies[number].start()
    reduce_step(reduced + 1, reduced + 1 >= ring - 3)

    def settle_gather(item, carry):
        way, step = gathered(item)
        relay_copy(way, step, z, x).wait_send()
        for piece in (0, 2):
            gather_copy(way, step, piece, z).wait_send()
        return carry

    def settle_reduce(item, carry):
        way, step = leaving(item)
        cross_copy(way, step).wait_send()

        @pl.when(step > 0)
        def _():
            for piece in (0, 2):
                reduce_copy(way, step, piece).wait_send()

        return carry

    lax.fori_loop(1, ring, settle_gather, 0)
    for number in range(2):
        dq_core_copies[number].wait_recv()
    dq_out[...] = dq_rows[relay_rows, :] + dq_core[peer_heads, :]
    dq_copy = copy_once(DQ_X, dq_out, dq_own.at[own_heads], across)
    dq_copy.start()
    dq_own[own_heads, :] = dq_rows[own_rows, :] + dq_core[own_heads, :]

    for xx, head in turn_back:
        cols = rows(((xx * 2 + c) * 2 + head) * TOK)
        att_rows[(xx * 2 + head) * TOK : (xx * 2 + head + 1) * TOK, :] = att_cols[:, cols].T
    att_copy = copy_once(ATT_X, att_rows.at[peer_heads], att_own.at[own_heads], across)
    att_copy.start()
    att_own[own_heads, :] = att_rows[own_heads, :]

    lax.fori_loop(reduced + 2, ring - 3, reduce_only, 0)
    for item in range(max(reduced + 2, ring - 3), ring - 1):
        reduce_step(item, True)
    lax.fori_loop(0, ring - 3, settle_reduce, 0)

    att_copy.wait_recv()
    result = codes_in[...].astype(F32)
    for head in range(4):
        span = slice(head * TOK, (head + 1) * TOK)
        result = result + dot(att_own[span, :], w_out[span, :])
    out_codes[...] = result.astype(BF16)

    dq_copy.wait_recv()
    normed_grad = jnp.zeros((TOK, w_query.shape[0]), F32)
    for head in range(4):
        span = slice(head * TOK, (head + 1) * TOK)
        lin_grad = norm_back(q_lin[:, span], q_gain[...], dq_own[span, :])
        normed_grad = normed_grad + dot_last(lin_grad, w_query[:, span])

    def ringed(piece):
        span = slice(piece * PIECE, (piece + 1) * PIECE)
        return ring_in[0, 0, span].astype(F32) + ring_in[1, 0, span].astype(F32)

    for piece in (0, 2):
        for way in range(2):
            reduce_copy(way, 1, piece).wait_recv()

    cross_copy(1, 0).wait_recv()
    dkv_copy.wait_recv()
    first_part = own_part(1, 0, 0) + kv_peer[...].astype(F32)
    second_part = own_part(1, 0, 1) + cross_in[1, 0].astype(F32)
    kv_grad[:PIECE, :] = first_part + ringed(0) + ringed(2)
    kv_grad[PIECE:, :] = second_part + ringed(1)
    key_grad = norm_back(k_lin[...], k_gain[...], kv_grad[:, :HD])
    normed_grad = normed_grad + dot_last(key_grad, w_key[...])
    normed_grad = normed_grad + dot_last(kv_grad[:, HD:].astype(BF16), w_value[...])
    wide = codes_in[...].astype(F32)
    inv_norm = lax.rsqrt(jnp.sum(wide * wide, axis=-1, keepdims=True) / D + NORM_EPS)
    inner = jnp.sum(wide * normed_grad, axis=-1, keepdims=True)
    in_grads[...] = (
        grads_in[...].astype(F32)
        + inv_norm * normed_grad
        - wide * (inv_norm * inv_norm * inv_norm) * inner / D
    ).astype(BF16)

    for once in (codes_copy, grads_copy, kv_copy, acc_copy, stats_copy, att_copy, dq_copy, dkv_copy):
        once.wait_send()
    for once in (*q_copies, *do_copies, *dq_core_copies):
        once.wait_send()

    relay_copy(0, 0, z, x).wait_send()
    lax.fori_loop(ring - 3, ring, settle_reduce, 0)


def rope_tables(first_pos):
    half_dim = HD // 2
    exponent = jnp.arange(half_dim).astype(F32) * (2.0 / HD)
    frequency = jnp.power(F32(ROPE_BASE), -exponent)
    frequency = jnp.concatenate([frequency, frequency])
    shape = (TOK // 2, HD)
    lane = lax.broadcasted_iota(jnp.int32, shape, 1)
    offset = lax.broadcasted_iota(jnp.int32, shape, 0) + jnp.where(lane < half_dim, 0, TOK // 2)
    angles = (first_pos + offset).astype(F32) * frequency[None, :]
    return (jnp.cos(angles), jnp.sin(angles))


def local(
    sent_codes, start_codes, sent_grads, loss_grads, w_query, w_key, w_value, w_out, q_gain, k_gain
):
    ring = lax.axis_size("seq") // 4
    sections = lax.axis_size("section")
    steps = ring // 2 + 1
    width = start_codes.shape[1]
    cosines, sines = rope_tables(lax.axis_index("seq") * TOK)
    vmem = pltpu.VMEM
    dma = pltpu.SemaphoreType.DMA
    one_block = (TOK, width)
    heads = (4 * TOK, HD)
    all_rows = (8 * TOK, HD)
    columns = (HD, 8 * TOK)
    stat = (1, 8 * TOK)
    results = pl.pallas_call(
        functools.partial(kernel, ring, sections),
        out_shape=(jax.ShapeDtypeStruct(one_block, BF16),) * 2,
        in_specs=[pl.BlockSpec(memory_space=pltpu.HBM)] * 8 + [pl.BlockSpec(memory_space=vmem)] * 4,
        out_specs=(pl.BlockSpec(memory_space=vmem),) * 2,
        scratch_shapes=[
            vmem(w_query.shape[1:], BF16),
            vmem(w_key.shape[1:], BF16),
            vmem(w_value.shape[1:], BF16),
            vmem(w_out.shape[1:], BF16),
            vmem(one_block, BF16),
            vmem(one_block, BF16),
            vmem(one_block, BF16),
            vmem(one_block, BF16),
            vmem(one_block, BF16),
            vmem(one_block, BF16),
            vmem(one_block, BF16),
            vmem(one_block, BF16),
            vmem(one_block, F32),
            vmem((TOK, HD), F32),
            vmem(heads, BF16),
            vmem(all_rows, BF16),
            vmem(columns, BF16),
            vmem(heads, BF16),
            vmem(all_rows, BF16),
            vmem(columns, BF16),
            vmem((ring * 2 * TOK, 2 * HD), BF16),
            vmem((8, 8 * TOK), F32),
            vmem((8, 8 * TOK), F32),
            vmem(columns, F32),
            vmem(columns, F32),
            vmem(stat, F32),
            vmem(stat, F32),
            vmem(columns, BF16),
            vmem(heads, BF16),
            vmem(heads, BF16),
            vmem(columns, F32),
            vmem(all_rows, F32),
            vmem(heads, F32),
            vmem((2 * TOK, HD), F32),
            vmem(heads, F32),
            vmem((2, steps, 2 * TOK, 8 * TOK), F32),
            vmem((2, steps, 8, 8 * TOK), F32),
            vmem((2, steps, 2 * TOK, 2 * HD), F32),
            vmem((2, steps, 3 * PIECE, 2 * HD), BF16),
            vmem((2, steps, 3 * PIECE, 2 * HD), BF16),
            vmem((2, steps, PIECE, 2 * HD), BF16),
            vmem((2, steps, PIECE, 2 * HD), BF16),
            vmem((TOK, 2 * HD), F32),
            vmem((PIECE, 2 * HD), BF16),
            vmem((PIECE, 2 * HD), BF16),
            dma((16,)),
            dma((16,)),
            dma((2, steps, 3)),
            dma((2, steps, 3)),
            dma((2, steps, 3)),
            dma((2, steps, 3)),
            dma((2, steps)),
            dma((2, steps)),
            dma((2, steps)),
            dma((2, steps)),
            dma((8,)),
        ],
        compiler_params=pltpu.CompilerParams(
            collective_id=0, has_side_effects=True, vmem_limit_bytes=60 * 1024 * 1024
        ),
    )(
        sent_codes[0],
        start_codes,
        sent_grads[0],
        loss_grads,
        w_query[0],
        w_key[0],
        w_value[0],
        w_out[0],
        q_gain,
        k_gain,
        cosines,
        sines,
    )
    return (results[0][None], results[1][None])


def solution(mesh):
    in_specs = (
        P("section", "seq", None),
        P("seq", None),
        P("section", "seq", None),
        P("seq", None),
        P("section", None, None),
        P("section", None, None),
        P("section", None, None),
        P("section", None, None),
        P("section", None),
        P("section", None),
    )
    out_specs = (P("section", "seq", None), P("section", "seq", None))
    return jax.shard_map(local, mesh=mesh, in_specs=in_specs, out_specs=out_specs, check_vma=False)
```
